256 devices in a mesh: space: 64 (over x, y, z_lo, core), sample: 4 (over z_hi).
Axes of the slice: x: 4, y: 4, z: 8 (z_hi: 4, z_lo: 2; z = z_hi * 2 + z_lo), core: 2. Of those that a mesh axis runs over, the one named last changes fastest.
Arguments:
- volume: bfloat16 [4, 128, 32, 64, 128], P('sample', 'space'), may hold values from -6 to 6
- upstream: bfloat16 [4, 128, 32, 64, 128], P('sample', 'space'), may hold values from -16 to 16
- weight: bfloat16 [3456, 128], replicated, may hold values from -0.109375 to 0.109375
- first_moment: float32 [3456, 128], P('sample'), may hold values from -1792 to 1792
- second_moment: float32 [3456, 128], P('sample'), may hold values from 2097.152 to 20971.52
Outputs:
- grad_volume: bfloat16 [4, 128, 32, 64, 128], P('sample', 'space')
- direction: float32 [3456, 128], P('sample')
The draws below stay inside these ranges and needn't reach their ends.
All inputs are finite; a program needn't handle non-finite values.
Results may differ from the reference program's by a relative error of at most 0.0039.
Values may be sent and summed in bfloat16 or wider, within the bound.
No kernel may reach another device: no remote copies, remote signals or barrier semaphores. Data moves between devices by JAX's collectives and lax.ppermute only.
A program may use at most 64 MiB of HBM per device.

```python
import math
import jax
import jax.numpy as jnp
from jax import lax

C = 128
NY = 32
NX = 64
ADAM_STEP = 10
NZ = 128
SAMPLES = 4
KROWS = 3456


def spiked(entries, stream_key, source, target, blocks, factor):
    owner, partner = [(jnp.arange(entries.shape[axis_at]) // (entries.shape[axis_at] // blocks)).reshape([-1 if axis == axis_at else 1 for axis in range(entries.ndim)]) for axis_at in (source, target)]
    chosen = jax.random.permutation(stream_key, blocks)[partner]
    strong = (owner == chosen) | (owner == (partner + blocks // 2) % blocks)
    return jnp.where(strong, factor * entries, entries)


def level_of(own_key, shape, shards, least, largest):
    def one(position, parts):
        steps = jax.random.uniform(jax.random.fold_in(jax.random.fold_in(own_key, 6), position), (parts,), jnp.float32, least / len(shards), largest / len(shards))
        return jnp.repeat(jnp.exp(steps), shape[position] // parts).reshape((-1,) + (1,) * (len(shape) - position - 1))

    level = one(*shards[0])
    for cut in shards[1:]:
        level = level * one(*cut)
    return level


def noise(own_key, extent, spread, bound, split=(), kind=jnp.bfloat16):
    drawn = spread * jax.random.normal(own_key, extent, jnp.float32)
    if split:
        drawn = drawn * level_of(own_key, extent, split, -0.22, 0.18)
    return jnp.clip(drawn, -bound, bound).astype(kind)


def bell_draw_with(stream_key, shape, width, most, cuts, heavy, held_as=jnp.bfloat16):
    entries = width * jax.random.normal(stream_key, shape, jnp.float32)
    if cuts:
        entries = entries * level_of(stream_key, shape, cuts, -0.22, 0.18)
    return jnp.clip(spiked(entries, jax.random.fold_in(stream_key, 3), *heavy), -most, most).astype(held_as)


def setup_inputs(seed: int = 0) -> dict:
    keys = jax.random.split(jax.random.key(seed), 6)
    volume = noise(keys[0], (SAMPLES, NZ, NY, NX, C), 1.0, 6.0, ((0, 4), (1, 64)))
    upstream = bell_draw_with(keys[1], (SAMPLES, NZ, NY, NX, C), 1.0, 16.0, ((0, 4), (1, 64)), (1, 4, 64, 4.0))
    weight = noise(keys[2], (KROWS, C), (27 * C) ** -0.5, 0.109375)
    first_moment = noise(keys[3], (KROWS, C), (0.3 * (SAMPLES * NZ * NY * NX) ** 0.5), 1792.0, ((0, 4),), jnp.float32)
    second_moment = jnp.clip(jnp.exp(math.log(20971.52) - 2.30258502 * jax.random.uniform(keys[4], (KROWS, C), jnp.float32) ** level_of(keys[4], (KROWS, C), ((0, 4),), -0.2, 0.2)), 2097.152, 20971.52)
    return {"volume": volume, "upstream": upstream, "weight": weight, "first_moment": first_moment, "second_moment": second_moment}


beta_one = 0.9
beta_two = 0.999
eps_adam = 1e-08

def conv_same(field, kernel):
    return lax.conv_general_dilated(field, kernel, (1, 1, 1), ((1, 1), (1, 1), (1, 1)), dimension_numbers=('NDHWC', 'DHWIO', 'NDHWC'), preferred_element_type=jnp.float32)

def one_sample(kernel, flipped, pair):
    volume_one, upstream_one = pair
    channels = kernel.shape[3]
    field = volume_one[None]
    preact = conv_same(field, kernel)
    sigmoid_val = jax.nn.sigmoid(preact)
    slopes = sigmoid_val * (1.0 + preact * (1.0 - sigmoid_val))
    up_float = upstream_one[None].astype(jnp.float32)
    grad_pre = (up_float * slopes).astype(jnp.bfloat16)
    grad_volume = (up_float + conv_same(grad_pre, flipped)).astype(jnp.bfloat16)
    padded = jnp.pad(volume_one, ((1, 1), (1, 1), (1, 1), (0, 0)))
    flat_grad = grad_pre.reshape(-1, channels)

    def depth_rows(carry, depth):
        slab = lax.dynamic_slice_in_dim(padded, depth, NZ, 0)
        pieces = []
        for row_off in range(3):
            for col_off in range(3):
                shifted = slab[:, row_off:row_off + NY, col_off:col_off + NX, :].reshape(-1, channels)
                pieces.append(lax.dot_general(shifted, flat_grad, (((0,), (0,)), ((), ())), preferred_element_type=jnp.float32))
        return (carry, jnp.concatenate(pieces, axis=0))
    unused, blocks = lax.scan(depth_rows, jnp.zeros((), jnp.float32), jnp.arange(3, dtype=jnp.int32))
    return (grad_volume[0], blocks.reshape(-1, channels))

def reference(volume, upstream, weight, first_moment, second_moment):
    channels = weight.shape[1]
    kernel = weight.reshape(3, 3, 3, channels, channels)
    flipped = jnp.transpose(jnp.flip(kernel, (0, 1, 2)), (0, 1, 2, 4, 3))
    grad_volume, grads = lax.map(lambda pair: one_sample(kernel, flipped, pair), (volume, upstream))
    weight_grad = lax.optimization_barrier(jnp.sum(grads, axis=0))
    m_new = beta_one * first_moment + (1.0 - beta_one) * weight_grad
    v_new = beta_two * second_moment + (1.0 - beta_two) * weight_grad * weight_grad
    direction = m_new / (1.0 - beta_one ** ADAM_STEP) / (jnp.sqrt(v_new / (1.0 - beta_two ** ADAM_STEP)) + eps_adam)
    return (grad_volume, direction)
```

```python
import jax
import jax.numpy as jnp
from jax import lax
from jax.sharding import Mesh, PartitionSpec as P

ADAM_STEP = 10


beta_one = 0.9
beta_two = 0.999
eps_adam = 1e-08

SPACE = ("x", "y", "zl", "core")
CHUNK = 32
OWNERS = 32


def padded_2(value, dim, width):
    size, length = (lax.axis_size(SPACE), value.shape[dim])
    up = [(i, (i + 1) % size) for i in range(size - 1)]
    down = [(j, i) for i, j in up]
    last = lax.slice_in_dim(value, length - width, length, axis=dim)
    initial = lax.slice_in_dim(value, 0, width, axis=dim)
    before = lax.ppermute(last, SPACE, up)
    after = lax.ppermute(initial, SPACE, down)
    return jnp.concatenate([before, value, after], axis=dim)


def conv_open(field, kernel):
    return lax.conv_general_dilated(
        field,
        kernel,
        (1, 1, 1),
        ((0, 0), (1, 1), (1, 1)),
        dimension_numbers=("NDHWC", "DHWIO", "NDHWC"),
        preferred_element_type=jnp.float32,
    )


def adam(grad, first, second):
    m_new = beta_one * first + (1.0 - beta_one) * grad
    v_new = beta_two * second + (1.0 - beta_two) * grad * grad
    return (
        m_new
        / (1.0 - beta_one**ADAM_STEP)
        / (jnp.sqrt(v_new / (1.0 - beta_two**ADAM_STEP)) + eps_adam)
    )


def reduced_direction(grad, first_moment, second_moment):
    rows, channels = first_moment.shape
    groups = grad.shape[0] // rows
    pad = OWNERS * CHUNK - rows
    core = lax.axis_index("core")
    mine_at = core * 16 + lax.axis_index("x") * 4 + lax.axis_index("y")
    spread = jnp.pad(grad.reshape(groups, rows, channels), ((0, 0), (0, pad), (0, 0)))
    spread = spread.reshape(groups, 2, 16, CHUNK, channels)
    kept = lax.dynamic_index_in_dim(spread, core, 1, False)
    sent = lax.dynamic_index_in_dim(spread, 1 - core, 1, False).astype(jnp.bfloat16)
    other = lax.ppermute(sent, "core", [(0, 1), (1, 0)])
    half = (kept + other.astype(jnp.float32)).astype(jnp.bfloat16)
    half = jnp.transpose(half, (1, 0, 2, 3))
    got = lax.all_to_all(half, ("x", "y"), 0, 0)
    part = jnp.sum(got.astype(jnp.float32), axis=0)
    part = jnp.broadcast_to(part[None], (2,) + part.shape).reshape(2 * groups, CHUNK, channels)
    got = lax.all_to_all(part, ("zl", "sample"), 0, 0)
    summed = jnp.sum(got, axis=0)
    first = jnp.pad(first_moment, ((0, pad), (0, 0)))
    second = jnp.pad(second_moment, ((0, pad), (0, 0)), constant_values=1.0)
    first = lax.dynamic_slice_in_dim(first, mine_at * CHUNK, CHUNK, 0)
    second = lax.dynamic_slice_in_dim(second, mine_at * CHUNK, CHUNK, 0)
    step = adam(summed, first, second)
    step = jnp.broadcast_to(step[None], (OWNERS, CHUNK, channels))
    whole = lax.all_to_all(step, ("core", "x", "y"), 0, 0)
    return whole.reshape(OWNERS * CHUNK, channels)[:rows]


def body(volume, upstream, weight, first_moment, second_moment):
    channels = weight.shape[1]
    planes = volume.shape[1]
    rows_y = volume.shape[2]
    cols_x = volume.shape[3]
    kernel = weight.reshape(3, 3, 3, channels, channels)
    flipped = jnp.transpose(jnp.flip(kernel, (0, 1, 2)), (0, 1, 2, 4, 3))
    haloed = padded_2(volume, 1, 1)
    preact = conv_open(haloed, kernel)
    sigmoid_val = jax.nn.sigmoid(preact)
    slopes = sigmoid_val * (1.0 + preact * (1.0 - sigmoid_val))
    grad_pre = (upstream.astype(jnp.float32) * slopes).astype(jnp.bfloat16)
    padded = jnp.pad(haloed, ((0, 0), (0, 0), (1, 1), (1, 1), (0, 0)))
    flat_grad = grad_pre.reshape(-1, channels)
    pieces = []
    for depth in range(3):
        for row_off in range(3):
            for col_off in range(3):
                shifted = padded[
                    :,
                    depth : depth + planes,
                    row_off : row_off + rows_y,
                    col_off : col_off + cols_x,
                    :,
                ].reshape(-1, channels)
                pieces.append(
                    lax.dot_general(
                        shifted,
                        flat_grad,
                        (((0,), (0,)), ((), ())),
                        preferred_element_type=jnp.float32,
                    )
                )
    weight_grad = jnp.concatenate(pieces, axis=0)
    direction = reduced_direction(weight_grad, first_moment, second_moment)
    grad_halo = padded_2(grad_pre, 1, 1)
    returned = conv_open(grad_halo, flipped)
    grad_volume = (upstream.astype(jnp.float32) + returned).astype(jnp.bfloat16)
    return (grad_volume, direction)


def solution(mesh):
    fine = Mesh(
        mesh.devices.reshape(4, 4, 2, 2, 4), ("x", "y", "zl", "core", "sample")
    )
    field = P("sample", SPACE, None, None, None)
    return jax.shard_map(
        body,
        mesh=fine,
        in_specs=(field, field, P(), P("sample", None), P("sample", None)),
        out_specs=(field, P("sample", None)),
        check_vma=False,
    )
```

```python
import functools
import jax
import jax.numpy as jnp
from jax import lax
from jax.experimental import pallas as pl
from jax.experimental.pallas import tpu as pltpu
from jax.sharding import Mesh, PartitionSpec as P

ADAM_STEP = 10


beta_one = 0.9
beta_two = 0.999
eps_adam = 1e-08

SPACE = ("x", "y", "zl", "core")
CHUNK = 32
OWNERS = 32
C = 128
COLS = 64
ROWS = 32
CELLS = ROWS * COLS
PADDED = CELLS + 2 * COLS
STRIP = 256
TILE = 512
BF = jnp.bfloat16
F32 = jnp.float32
VMEM = pl.BlockSpec(memory_space=pltpu.VMEM)
SMEM = pl.BlockSpec(memory_space=pltpu.SMEM)
PARAMS = pltpu.CompilerParams(vmem_limit_bytes=48 * 1024 * 1024)


def cost(flops, moved, special=0):
    return pl.CostEstimate(flops=flops, bytes_accessed=moved, transcendentals=special)


def shifted_columns(planes, out, first, flip):
    width = 128 * len(planes)
    blank = jnp.zeros((COLS, width), BF)
    cols = slice(first, first + width)
    for c in range(3):
        out[c, 0:COLS, cols] = blank
        out[c, PADDED - COLS : PADDED, cols] = blank
    before, after = (2, 0) if flip else (0, 2)

    def strip(i, carry):
        at = pl.multiple_of(i * STRIP, STRIP)
        to = pl.ds(pl.multiple_of(at + COLS, COLS), STRIP)
        col = lax.broadcasted_iota(jnp.int32, (STRIP, C), 0) & (COLS - 1)
        for k, plane in enumerate(planes):
            cols = slice(first + k * C, first + (k + 1) * C)
            here = plane[pl.ds(at, STRIP), :]
            wide = here.astype(F32)
            out[1, to, cols] = here
            out[before, to, cols] = jnp.where(
                col == 0, 0.0, pltpu.roll(wide, 1, 0)
            ).astype(BF)
            out[after, to, cols] = jnp.where(
                col == COLS - 1, 0.0, pltpu.roll(wide, STRIP - 1, 0)
            ).astype(BF)
        return carry

    lax.fori_loop(0, CELLS // STRIP, strip, 0)


def tap(a, b, c):
    return (a * 3 + b) * 3 + c


def taps_of(field, at, rows):
    return jnp.concatenate(
        [
            field[c, pl.ds(pl.multiple_of(at + b * COLS, COLS), rows), :]
            for b in range(3)
            for c in range(3)
        ],
        axis=1,
    )


def inner_kernel(vol, weight, out, vol_t, field, mixed):
    shifted_columns([vol.at[0], vol.at[1]], field, 0, False)
    for b in range(3):
        for c in range(3):
            base = (b * 3 + c) * 256
            for p in range(2):
                for z in range(2):
                    t = tap(1 + p - z, b, c)
                    mixed[base + p * C : base + (p + 1) * C, z * C : (z + 1) * C] = (
                        weight[t * C : (t + 1) * C, :]
                    )

    def tile(i, carry):
        at = pl.multiple_of(i * TILE, TILE)
        out[pl.ds(at, TILE), :] = jnp.dot(
            taps_of(field, at, TILE), mixed[...], preferred_element_type=F32
        )
        return carry

    lax.fori_loop(0, CELLS // TILE, tile, 0)
    for p in range(2):
        vol_t[p * C : (p + 1) * C, :] = jnp.transpose(vol[p])


def inner_conv(vol, weight):
    return pl.pallas_call(
        inner_kernel,
        out_shape=[
            jax.ShapeDtypeStruct((CELLS, 2 * C), F32),
            jax.ShapeDtypeStruct((2 * C, CELLS), BF),
        ],
        in_specs=[VMEM, VMEM],
        out_specs=[VMEM, VMEM],
        scratch_shapes=[
            pltpu.VMEM((3, PADDED, 2 * C), BF),
            pltpu.VMEM((9 * 256, 2 * C), BF),
        ],
        compiler_params=PARAMS,
        cost_estimate=cost(2 * CELLS * 2304 * 256, 5 << 20),
        name="inner_conv",
    )(vol, weight)


def outer_kernel(before, after, weight, inner, upstream, grad, field, mixed):
    shifted_columns([before, after], field, 0, False)
    blank = jnp.zeros((C, C), BF)
    for b in range(3):
        for c in range(3):
            base = (b * 3 + c) * 256
            low, high = tap(0, b, c), tap(2, b, c)
            mixed[base : base + C, 0:C] = weight[low * C : (low + 1) * C, :]
            mixed[base : base + C, C : 2 * C] = blank
            mixed[base + C : base + 2 * C, 0:C] = blank
            mixed[base + C : base + 2 * C, C : 2 * C] = weight[
                high * C : (high + 1) * C, :
            ]

    def tile(i, carry):
        at = pl.multiple_of(i * TILE, TILE)
        rows = pl.ds(at, TILE)
        preact = inner[rows, :] + jnp.dot(
            taps_of(field, at, TILE), mixed[...], preferred_element_type=F32
        )
        s = jax.nn.sigmoid(preact)
        slopes = s * (1.0 + preact * (1.0 - s))
        for z in range(2):
            grad[z, rows, :] = (
                upstream[z, rows, :].astype(F32) * slopes[:, z * C : (z + 1) * C]
            ).astype(BF)
        return carry

    lax.fori_loop(0, CELLS // TILE, tile, 0)


def outer_conv(before, after, weight, inner, upstream):
    return pl.pallas_call(
        outer_kernel,
        out_shape=jax.ShapeDtypeStruct((2, CELLS, C), BF),
        in_specs=[VMEM] * 5,
        out_specs=VMEM,
        scratch_shapes=[
            pltpu.VMEM((3, PADDED, 2 * C), BF),
            pltpu.VMEM((9 * 256, 2 * C), BF),
        ],
        compiler_params=PARAMS,
        cost_estimate=cost(2 * CELLS * 2304 * 256, 6 << 20, CELLS * 256),
        name="outer_conv",
    )(before, after, weight, inner, upstream)


def taps_kernel(core_ref, grad, before, after, vol_t, kept, sent, field, lhs):
    core = core_ref[0]
    shifted_columns([grad.at[0], grad.at[1]], field, 0, False)
    lhs[0:C, :] = jnp.transpose(before[...])
    lhs[C : 3 * C, :] = vol_t[...]
    lhs[3 * C : 4 * C, :] = jnp.transpose(after[...])

    def store(j, block):
        group = j // 27
        owner = j - group * 27
        at = (owner % 16) * 4 + group

        @pl.when(owner // 16 == core)
        def _():
            kept[at] = block

        @pl.when(owner // 16 != core)
        def _():
            sent[at] = block.astype(BF)

    for owner in range(27, 32):
        for group in range(4):
            kept[(owner % 16) * 4 + group] = jnp.zeros((CHUNK, C), F32)
            sent[(owner % 16) * 4 + group] = jnp.zeros((CHUNK, C), BF)

    def row(b, carry):
        at = pl.multiple_of((2 - b) * COLS, COLS)
        for c in range(3):
            got = jnp.dot(
                lhs[...],
                field[2 - c, pl.ds(at, CELLS), :],
                preferred_element_type=F32,
            )
            for a in range(3):
                whole = (
                    got[a * C : (a + 1) * C, 0:C]
                    + got[(a + 1) * C : (a + 2) * C, C : 2 * C]
                )
                for i in range(4):
                    store(
                        4 * tap(a, b, c) + i, whole[i * CHUNK : (i + 1) * CHUNK, :]
                    )
        return carry

    lax.fori_loop(0, 3, row, 0)


def kernel_gradient(core, grad, before, after, vol_t):
    return pl.pallas_call(
        taps_kernel,
        out_shape=[
            jax.ShapeDtypeStruct((64, CHUNK, C), F32),
            jax.ShapeDtypeStruct((64, CHUNK, C), BF),
        ],
        in_specs=[SMEM] + [VMEM] * 4,
        out_specs=[VMEM, VMEM],
        scratch_shapes=[
            pltpu.VMEM((3, PADDED, 2 * C), BF),
            pltpu.VMEM((4 * C, CELLS), BF),
        ],
        compiler_params=PARAMS,
        cost_estimate=cost(2 * CELLS * 4608 * 256, 5 << 20),
        name="kernel_gradient",
    )(core, grad, before, after, vol_t)


def back_kernel(before, grad, after, weight, upstream, out, field, mixed):
    shifted_columns([before, grad.at[0], grad.at[1], after], field, 0, False)
    blank = jnp.zeros((C, C), BF)
    for b in range(3):
        for c in range(3):
            base = (b * 3 + c) * 512
            for p in range(4):
                for z in range(2):
                    a = 2 - (p - z)
                    t = tap(a, 2 - b, 2 - c)
                    mixed[z * C : (z + 1) * C, base + p * C : base + (p + 1) * C] = (
                        weight[t * C : (t + 1) * C, :] if 0 <= a < 3 else blank
                    )

    def tile(i, carry):
        at = pl.multiple_of(i * TILE, TILE)
        rows = pl.ds(at, TILE)
        got = lax.dot_general(
            taps_of(field, at, TILE),
            mixed[...],
            (((1,), (1,)), ((), ())),
            preferred_element_type=F32,
        )
        for z in range(2):
            out[z, rows, :] = (
                upstream[z, rows, :].astype(F32) + got[:, z * C : (z + 1) * C]
            ).astype(BF)
        return carry

    lax.fori_loop(0, CELLS // TILE, tile, 0)


def back_conv(before, grad, after, weight, upstream):
    return pl.pallas_call(
        back_kernel,
        out_shape=jax.ShapeDtypeStruct((2, CELLS, C), BF),
        in_specs=[VMEM] * 5,
        out_specs=VMEM,
        scratch_shapes=[
            pltpu.VMEM((3, PADDED, 4 * C), BF),
            pltpu.VMEM((2 * C, 9 * 512), BF),
        ],
        compiler_params=PARAMS,
        cost_estimate=cost(2 * CELLS * 4608 * 256, 5 << 20),
        name="back_conv",
    )(before, grad, after, weight, upstream)


def adam(grad, first, second):
    m_new = beta_one * first + (1.0 - beta_one) * grad
    v_new = beta_two * second + (1.0 - beta_two) * grad * grad
    return (
        m_new
        / (1.0 - beta_one**ADAM_STEP)
        / (jnp.sqrt(v_new / (1.0 - beta_two**ADAM_STEP)) + eps_adam)
    )


def from_neighbours(planes):
    size = lax.axis_size(SPACE)
    up = [(i, i + 1) for i in range(size - 1)]
    down = [(j, i) for i, j in up]
    return lax.ppermute(planes[1], SPACE, up), lax.ppermute(planes[0], SPACE, down)


def reduced_direction(kept, sent, core, first_moment, second_moment):
    rows, channels = first_moment.shape
    pad = OWNERS * CHUNK - rows
    mine_at = core * 16 + lax.axis_index("x") * 4 + lax.axis_index("y")
    other = lax.ppermute(sent, "core", [(0, 1), (1, 0)])
    half = (kept + other.astype(F32)).astype(BF).reshape(16, 4, CHUNK, channels)
    got = lax.all_to_all(half, ("x", "y"), 0, 0)
    part = jnp.sum(got.astype(F32), axis=0)
    part = jnp.broadcast_to(part[None], (2,) + part.shape).reshape(8, CHUNK, channels)
    got = lax.all_to_all(part, ("zl", "sample"), 0, 0)
    summed = jnp.sum(got, axis=0)
    first = jnp.pad(first_moment, ((0, pad), (0, 0)))
    second = jnp.pad(second_moment, ((0, pad), (0, 0)), constant_values=1.0)
    first = lax.dynamic_slice_in_dim(first, mine_at * CHUNK, CHUNK, 0)
    second = lax.dynamic_slice_in_dim(second, mine_at * CHUNK, CHUNK, 0)
    step = adam(summed, first, second)
    step = jnp.broadcast_to(step[None], (OWNERS, CHUNK, channels))
    whole = lax.all_to_all(step, ("core", "x", "y"), 0, 0)
    return whole.reshape(OWNERS * CHUNK, channels)[:rows]


def body(volume, upstream, weight, first_moment, second_moment):
    vol = volume.reshape(2, CELLS, C)
    up = upstream.reshape(2, CELLS, C)
    core = lax.axis_index("core")
    before, after = from_neighbours(vol)
    inner, vol_t = inner_conv(vol, weight)
    grad = outer_conv(before, after, weight, inner, up)
    grad_before, grad_after = from_neighbours(grad)
    kept, sent = kernel_gradient(core.reshape(1), grad, before, after, vol_t)
    direction = reduced_direction(kept, sent, core, first_moment, second_moment)
    grad_volume = back_conv(grad_before, grad, grad_after, weight, up)
    return (grad_volume.reshape(volume.shape), direction)


def solution(mesh):
    fine = Mesh(
        mesh.devices.reshape(4, 4, 2, 2, 4), ("x", "y", "zl", "core", "sample")
    )
    field = P("sample", SPACE, None, None, None)
    return jax.shard_map(
        body,
        mesh=fine,
        in_specs=(field, field, P(), P("sample", None), P("sample", None)),
        out_specs=(field, P("sample", None)),
        check_vma=False,
    )
```

```python
import functools
import jax
import jax.numpy as jnp
from jax import lax
from jax.experimental import pallas as pl
from jax.experimental.pallas import tpu as pltpu
from jax.sharding import Mesh, PartitionSpec as P

ADAM_STEP = 10


beta_one = 0.9
beta_two = 0.999
eps_adam = 1e-08

SPACE = ("x", "y", "zl", "core")
CHUNK = 32
OWNERS = 32
C = 128
COLS = 64
ROWS = 32
CELLS = ROWS * COLS
PADDED = CELLS + 2 * COLS
STRIP = 256
TILE = 512
BF = jnp.bfloat16
F32 = jnp.float32
VMEM = pl.BlockSpec(memory_space=pltpu.VMEM)
ANY = pl.BlockSpec(memory_space=pl.ANY)
SMEM = pl.BlockSpec(memory_space=pltpu.SMEM)
SMALL = pltpu.CompilerParams(vmem_limit_bytes=4 * 1024 * 1024)
PARAMS = pltpu.CompilerParams(vmem_limit_bytes=32 * 1024 * 1024)


def cost(flops, moved, special=0):
    return pl.CostEstimate(flops=flops, bytes_accessed=moved, transcendentals=special)


def shifted_columns(planes, out, first, flip):
    width = 128 * len(planes)
    blank = jnp.zeros((COLS, width), BF)
    cols = slice(first, first + width)
    for c in range(3):
        out[c, 0:COLS, cols] = blank
        out[c, PADDED - COLS : PADDED, cols] = blank
    before, after = (2, 0) if flip else (0, 2)

    def strip(i, carry):
        at = pl.multiple_of(i * STRIP, STRIP)
        to = pl.ds(pl.multiple_of(at + COLS, COLS), STRIP)
        col = lax.broadcasted_iota(jnp.int32, (STRIP, C), 0) & (COLS - 1)
        for k, plane in enumerate(planes):
            cols = slice(first + k * C, first + (k + 1) * C)
            here = plane[pl.ds(at, STRIP), :]
            wide = here.astype(F32)
            out[1, to, cols] = here
            out[before, to, cols] = jnp.where(
                col == 0, 0.0, pltpu.roll(wide, 1, 0)
            ).astype(BF)
            out[after, to, cols] = jnp.where(
                col == COLS - 1, 0.0, pltpu.roll(wide, STRIP - 1, 0)
            ).astype(BF)
        return carry

    lax.fori_loop(0, CELLS // STRIP, strip, 0)


def transposed(plane, out, first):
    for at in range(0, CELLS, TILE):
        out[first : first + C, at : at + TILE] = jnp.transpose(
            plane[at : at + TILE, :]
        )


def tap(a, b, c):
    return (a * 3 + b) * 3 + c


def taps_of(field, at, rows):
    return jnp.concatenate(
        [
            field[c, pl.ds(pl.multiple_of(at + b * COLS, COLS), rows), :]
            for b in range(3)
            for c in range(3)
        ],
        axis=1,
    )


def inner_kernel(vol, weight, low, high, vol_t, field, mixed):
    shifted_columns([vol.at[0], vol.at[1]], field, 0, False)
    for b in range(3):
        for c in range(3):
            base = (b * 3 + c) * 256
            for p in range(2):
                for z in range(2):
                    t = tap(1 + p - z, b, c)
                    mixed[base + p * C : base + (p + 1) * C, z * C : (z + 1) * C] = (
                        weight[t * C : (t + 1) * C, :]
                    )

    def tile(i, carry):
        at = pl.multiple_of(i * TILE, TILE)
        got = jnp.dot(taps_of(field, at, TILE), mixed[...], preferred_element_type=F32)
        low[pl.ds(at, TILE), :] = got[:, 0:C]
        high[pl.ds(at, TILE), :] = got[:, C : 2 * C]
        return carry

    lax.fori_loop(0, CELLS // TILE, tile, 0)
    for p in range(2):
        transposed(vol.at[p], vol_t, p * C)


def inner_conv(vol, weight):
    return pl.pallas_call(
        inner_kernel,
        out_shape=[
            jax.ShapeDtypeStruct((CELLS, C), F32),
            jax.ShapeDtypeStruct((CELLS, C), F32),
            jax.ShapeDtypeStruct((2 * C, CELLS), BF),
        ],
        in_specs=[VMEM, VMEM],
        out_specs=[VMEM] * 3,
        scratch_shapes=[
            pltpu.VMEM((3, PADDED, 2 * C), BF),
            pltpu.VMEM((9 * 256, 2 * C), BF),
        ],
        compiler_params=PARAMS,
        cost_estimate=cost(2 * CELLS * 2304 * 256, 5 << 20),
        name="inner_conv",
    )(vol, weight)


def outer_kernel(z, halo, weight, inner, upstream, grad, field):
    shifted_columns([halo], field, 0, False)
    first = tap(2 * z, 0, 0) * C

    def tile(i, carry):
        at = pl.multiple_of(i * TILE, TILE)
        rows = pl.ds(at, TILE)
        preact = inner[rows, :] + jnp.dot(
            taps_of(field, at, TILE),
            weight[first : first + 9 * C, :],
            preferred_element_type=F32,
        )
        s = jax.nn.sigmoid(preact)
        slopes = s * (1.0 + preact * (1.0 - s))
        grad[rows, :] = (upstream[z, rows, :].astype(F32) * slopes).astype(BF)
        return carry

    lax.fori_loop(0, CELLS // TILE, tile, 0)


def outer_conv(z, halo, weight, inner, upstream):
    return pl.pallas_call(
        functools.partial(outer_kernel, z),
        out_shape=jax.ShapeDtypeStruct((CELLS, C), BF),
        in_specs=[VMEM] * 4,
        out_specs=VMEM,
        scratch_shapes=[pltpu.VMEM((3, PADDED, C), BF)],
        compiler_params=PARAMS,
        cost_estimate=cost(2 * CELLS * 1152 * 256, 3 << 20, CELLS * 128),
        name=f"outer_conv_{z}",
    )(halo, weight, inner, upstream)


def taps_kernel(core_ref, low, high, before, after, vol_t, kept, sent, field, lhs, whole):
    core = core_ref[0]
    shifted_columns([low, high], field, 0, False)
    lhs[C : 3 * C, :] = vol_t[...]
    transposed(before, lhs, 0)
    transposed(after, lhs, 3 * C)

    for owner in range(27, 32):
        for group in range(4):
            whole[group * 32 + owner] = jnp.zeros((CHUNK, C), F32)

    def row(b, carry):
        at = pl.multiple_of((2 - b) * COLS, COLS)
        for c in range(3):
            got = jnp.dot(
                lhs[...],
                field[2 - c, pl.ds(at, CELLS), :],
                preferred_element_type=F32,
            )
            for a in range(3):
                summed = (
                    got[a * C : (a + 1) * C, 0:C]
                    + got[(a + 1) * C : (a + 2) * C, C : 2 * C]
                )
                for i in range(4):
                    chunk = 4 * tap(a, b, c) + i
                    whole[chunk + 5 * (chunk // 27)] = summed[
                        i * CHUNK : (i + 1) * CHUNK, :
                    ]
        return carry

    lax.fori_loop(0, 3, row, 0)

    def share(owner, carry):
        for group in range(4):
            kept[owner * 4 + group] = whole[group * 32 + core * 16 + owner]
            sent[owner * 4 + group] = whole[
                group * 32 + (1 - core) * 16 + owner
            ].astype(BF)
        return carry

    lax.fori_loop(0, 16, share, 0)


def kernel_gradient(core, low, high, before, after, vol_t):
    return pl.pallas_call(
        taps_kernel,
        out_shape=[
            jax.ShapeDtypeStruct((64, CHUNK, C), F32),
            jax.ShapeDtypeStruct((64, CHUNK, C), BF),
        ],
        in_specs=[SMEM] + [VMEM] * 5,
        out_specs=[VMEM, VMEM],
        scratch_shapes=[
            pltpu.VMEM((3, PADDED, 2 * C), BF),
            pltpu.VMEM((4 * C, CELLS), BF),
            pltpu.VMEM((4 * 32, CHUNK, C), F32),
        ],
        compiler_params=PARAMS,
        cost_estimate=cost(2 * CELLS * 4608 * 256, 5 << 20),
        name="kernel_gradient",
    )(core, low, high, before, after, vol_t)


def inner_back_kernel(low, high, weight, upstream, later, out, field, mixed):
    shifted_columns([low, high], field, 0, False)
    for b in range(3):
        for c in range(3):
            base = (b * 3 + c) * 256
            for p in range(2):
                for z in range(2):
                    t = tap(1 + z - p, 2 - b, 2 - c)
                    mixed[z * C : (z + 1) * C, base + p * C : base + (p + 1) * C] = (
                        weight[t * C : (t + 1) * C, :]
                    )

    def tile(i, carry):
        at = pl.multiple_of(i * TILE, TILE)
        rows = pl.ds(at, TILE)
        got = lax.dot_general(
            taps_of(field, at, TILE),
            mixed[...],
            (((1,), (1,)), ((), ())),
            preferred_element_type=F32,
        )
        for z in range(2):
            out[z, rows, :] = (
                upstream[z, rows, :].astype(F32) + got[:, z * C : (z + 1) * C]
            )
        return carry

    lax.fori_loop(0, CELLS // TILE, tile, 0)


def inner_back(low, high, weight, upstream, later):
    return pl.pallas_call(
        inner_back_kernel,
        out_shape=jax.ShapeDtypeStruct((2, CELLS, C), F32),
        in_specs=[VMEM] * 4 + [ANY],
        out_specs=VMEM,
        scratch_shapes=[
            pltpu.VMEM((3, PADDED, 2 * C), BF),
            pltpu.VMEM((2 * C, 9 * 256), BF),
        ],
        compiler_params=PARAMS,
        cost_estimate=cost(2 * CELLS * 2304 * 256, 5 << 20),
        name="inner_back",
    )(low, high, weight, upstream, later)


def outer_back_kernel(before, after, weight, inner, out, field, mixed):
    shifted_columns([before, after], field, 0, False)
    for b in range(3):
        for c in range(3):
            base = (b * 3 + c) * C
            for z in range(2):
                t = tap(2 - 2 * z, 2 - b, 2 - c)
                mixed[z, :, base : base + C] = weight[t * C : (t + 1) * C, :]

    def tile(i, carry):
        at = pl.multiple_of(i * TILE, TILE)
        rows = pl.ds(at, TILE)
        for z in range(2):
            lhs = jnp.concatenate(
                [
                    field[
                        c,
                        pl.ds(pl.multiple_of(at + b * COLS, COLS), TILE),
                        z * C : (z + 1) * C,
                    ]
                    for b in range(3)
                    for c in range(3)
                ],
                axis=1,
            )
            got = lax.dot_general(
                lhs, mixed[z], (((1,), (1,)), ((), ())), preferred_element_type=F32
            )
            out[z, rows, :] = (inner[z, rows, :] + got).astype(BF)
        return carry

    lax.fori_loop(0, CELLS // TILE, tile, 0)


def outer_back(before, after, weight, inner):
    return pl.pallas_call(
        outer_back_kernel,
        out_shape=jax.ShapeDtypeStruct((2, CELLS, C), BF),
        in_specs=[VMEM] * 4,
        out_specs=VMEM,
        scratch_shapes=[
            pltpu.VMEM((3, PADDED, 2 * C), BF),
            pltpu.VMEM((2, C, 9 * C), BF),
        ],
        compiler_params=PARAMS,
        cost_estimate=cost(2 * CELLS * 2304 * 256, 5 << 20),
        name="outer_back",
    )(before, after, weight, inner)


def planes_kernel(vol, low, high, sems):
    first = pltpu.make_async_copy(vol.at[0], low, sems.at[0])
    second = pltpu.make_async_copy(vol.at[1], high, sems.at[1])
    first.start()
    second.start()
    first.wait()
    second.wait()


def both_planes(vol):
    plane = jax.ShapeDtypeStruct((CELLS, C), BF)
    return pl.pallas_call(
        planes_kernel,
        out_shape=[plane, plane],
        in_specs=[ANY],
        out_specs=[ANY, ANY],
        scratch_shapes=[pltpu.SemaphoreType.DMA((2,))],
        compiler_params=SMALL,
        cost_estimate=cost(0, 2 << 20),
        name="both_planes",
    )(vol)


def first_rows_kernel(whole, out, sem):
    copy = pltpu.make_async_copy(whole.at[0 : out.shape[0]], out, sem)
    copy.start()
    copy.wait()


def first_rows(whole, rows):
    return pl.pallas_call(
        first_rows_kernel,
        out_shape=jax.ShapeDtypeStruct((rows, C), F32),
        in_specs=[VMEM],
        out_specs=ANY,
        scratch_shapes=[pltpu.SemaphoreType.DMA],
        compiler_params=SMALL,
        cost_estimate=cost(0, 1 << 20),
        name="first_rows",
    )(whole)


def mix_kernel(got, out):
    for group in range(4):
        total = got[0, group].astype(F32)
        for k in range(1, 16):
            total += got[k, group].astype(F32)
        out[group] = total
        out[4 + group] = total


def mixed_rows(got):
    return pl.pallas_call(
        mix_kernel,
        out_shape=jax.ShapeDtypeStruct((8, CHUNK, C), F32),
        in_specs=[VMEM],
        out_specs=VMEM,
        compiler_params=SMALL,
        cost_estimate=cost(1 << 18, 1 << 20),
        name="mixed_rows",
    )(got)


def step_kernel(at_ref, got, first, second, later, out):
    total = got[0]
    for k in range(1, 8):
        total += got[k]
    at = pl.multiple_of(at_ref[0], CHUNK)
    rows = pl.ds(at, CHUNK)
    step = adam(total, first[rows, :], second[rows, :])
    for k in range(OWNERS):
        out[k] = step


def spread_step(at, got, first, second, later):
    return pl.pallas_call(
        step_kernel,
        out_shape=jax.ShapeDtypeStruct((OWNERS, CHUNK, C), F32),
        in_specs=[SMEM] + [VMEM] * 3 + [ANY],
        out_specs=VMEM,
        compiler_params=SMALL,
        cost_estimate=cost(1 << 18, 1 << 20),
        name="spread_step",
    )(at, got, first, second, later)


def adam(grad, first, second):
    m_new = beta_one * first + (1.0 - beta_one) * grad
    v_new = beta_two * second + (1.0 - beta_two) * grad * grad
    return (
        m_new
        / (1.0 - beta_one**ADAM_STEP)
        / (jnp.sqrt(v_new / (1.0 - beta_two**ADAM_STEP)) + eps_adam)
    )


def from_neighbours(low, high):
    size = lax.axis_size(SPACE)
    up = [(i, i + 1) for i in range(size - 1)]
    down = [(j, i) for i, j in up]
    return lax.ppermute(high, SPACE, up), lax.ppermute(low, SPACE, down)


def body(volume, upstream, weight, first_moment, second_moment):
    vol = volume.reshape(2, CELLS, C)
    up = upstream.reshape(2, CELLS, C)
    core = lax.axis_index("core")
    before, after = from_neighbours(*both_planes(vol))
    inner_low, inner_high, vol_t = inner_conv(vol, weight)
    low = outer_conv(0, before, weight, inner_low, up)
    high = outer_conv(1, after, weight, inner_high, up)
    kept, sent = kernel_gradient(core.reshape(1), low, high, before, after, vol_t)

    rows = first_moment.shape[0]
    other = lax.ppermute(sent, "core", [(0, 1), (1, 0)])
    half = (kept + other.astype(F32)).astype(BF).reshape(16, 4, CHUNK, C)
    got = lax.all_to_all(half, ("x", "y"), 0, 0)
    grad_before, grad_after = from_neighbours(low, high)
    part = mixed_rows(got)
    got = lax.all_to_all(part, ("zl", "sample"), 0, 0)
    local = inner_back(low, high, weight, up, part)
    owner = core * 16 + lax.axis_index("x") * 4 + lax.axis_index("y")
    at = jnp.minimum(owner * CHUNK, rows - CHUNK).reshape(1)
    step = spread_step(at, got, first_moment, second_moment, local)
    whole = lax.all_to_all(step, ("core", "x", "y"), 0, 0)
    direction = first_rows(whole.reshape(OWNERS * CHUNK, C), rows)
    grad_volume = outer_back(grad_before, grad_after, weight, local)
    return (grad_volume.reshape(volume.shape), direction)


def solution(mesh):
    fine = Mesh(
        mesh.devices.reshape(4, 4, 2, 2, 4), ("x", "y", "zl", "core", "sample")
    )
    field = P("sample", SPACE, None, None, None)
    return jax.shard_map(
        body,
        mesh=fine,
        in_specs=(field, field, P(), P("sample", None), P("sample", None)),
        out_specs=(field, P("sample", None)),
        check_vma=False,
    )
```

```python
import functools
import jax
import jax.numpy as jnp
from jax import lax
from jax.experimental import pallas as pl
from jax.experimental.pallas import tpu as pltpu
from jax.sharding import Mesh, PartitionSpec as P

ADAM_STEP = 10


beta_one = 0.9
beta_two = 0.999
eps_adam = 1e-08

SPACE = ("x", "y", "zl", "core")
CHUNK = 32
OWNERS = 32
C = 128
COLS = 64
ROWS = 32
CELLS = ROWS * COLS
PADDED = CELLS + 2 * COLS
STRIP = 256
TILE = 512
BF = jnp.bfloat16
F32 = jnp.float32
VMEM = pl.BlockSpec(memory_space=pltpu.VMEM)
ANY = pl.BlockSpec(memory_space=pl.ANY)
HBM = pl.BlockSpec(memory_space=pltpu.HBM)
SMEM = pl.BlockSpec(memory_space=pltpu.SMEM)
FLAG = jax.ShapeDtypeStruct((8, C), F32)
WHOLE = pltpu.CompilerParams(vmem_limit_bytes=60 * 1024 * 1024)
SMALL = pltpu.CompilerParams(vmem_limit_bytes=4 * 1024 * 1024)
PARAMS = pltpu.CompilerParams(vmem_limit_bytes=32 * 1024 * 1024)


def cost(flops, moved, special=0):
    return pl.CostEstimate(flops=flops, bytes_accessed=moved, transcendentals=special)


def shifted_columns(planes, out, first, flip):
    width = 128 * len(planes)
    blank = jnp.zeros((COLS, width), BF)
    cols = slice(first, first + width)
    for c in range(3):
        out[c, 0:COLS, cols] = blank
        out[c, PADDED - COLS : PADDED, cols] = blank
    before, after = (2, 0) if flip else (0, 2)

    def strip(i, carry):
        at = pl.multiple_of(i * STRIP, STRIP)
        to = pl.ds(pl.multiple_of(at + COLS, COLS), STRIP)
        col = lax.broadcasted_iota(jnp.int32, (STRIP, C), 0) & (COLS - 1)
        for k, plane in enumerate(planes):
            cols = slice(first + k * C, first + (k + 1) * C)
            here = plane(pl.ds(at, STRIP))
            wide = here.astype(F32)
            out[1, to, cols] = here
            out[before, to, cols] = jnp.where(
                col == 0, 0.0, pltpu.roll(wide, 1, 0)
            ).astype(BF)
            out[after, to, cols] = jnp.where(
                col == COLS - 1, 0.0, pltpu.roll(wide, STRIP - 1, 0)
            ).astype(BF)
        return carry

    lax.fori_loop(0, CELLS // STRIP, strip, 0)


def transposed(plane, out, first):
    for at in range(0, CELLS, TILE):
        out[first : first + C, at : at + TILE] = jnp.transpose(
            plane(pl.ds(at, TILE))
        )


def rows_of(plane):
    return lambda rows: plane[rows, :]


def ordered(core, near, far):
    def pick(first, second):
        return lambda rows: jnp.where(core == 0, first[rows, :], second[rows, :])

    return pick(far, near), pick(near, far)


def fetched(source, held, sem):
    copy = pltpu.make_async_copy(source, held, sem)
    copy.start()
    return copy


def tap(a, b, c):
    return (a * 3 + b) * 3 + c


def taps_of(field, at, rows):
    return jnp.concatenate(
        [
            field[c, pl.ds(pl.multiple_of(at + b * COLS, COLS), rows), :]
            for b in range(3)
            for c in range(3)
        ],
        axis=1,
    )


def inner_kernel(vol, weight, out, vol_t, field, mixed, held, sem):
    copy = fetched(weight, held, sem)
    planes = [rows_of(vol.at[0]), rows_of(vol.at[1])]
    shifted_columns(planes, field, 0, False)
    copy.wait()
    for b in range(3):
        for c in range(3):
            base = (b * 3 + c) * 256
            for p in range(2):
                for z in range(2):
                    t = tap(1 + p - z, b, c)
                    mixed[base + p * C : base + (p + 1) * C, z * C : (z + 1) * C] = (
                        held[t * C : (t + 1) * C, :]
                    )

    def tile(i, carry):
        at = pl.multiple_of(i * TILE, TILE)
        got = jnp.dot(taps_of(field, at, TILE), mixed[...], preferred_element_type=F32)
        out[0, pl.ds(at, TILE), :] = got[:, 0:C]
        out[1, pl.ds(at, TILE), :] = got[:, C : 2 * C]
        return carry

    lax.fori_loop(0, CELLS // TILE, tile, 0)
    for p in range(2):
        transposed(planes[p], vol_t, p * C)


def inner_conv(vol, weight):
    return pl.pallas_call(
        inner_kernel,
        out_shape=[
            jax.ShapeDtypeStruct((2, CELLS, C), F32),
            jax.ShapeDtypeStruct((2 * C, CELLS), BF),
        ],
        in_specs=[VMEM, HBM],
        out_specs=[VMEM] * 2,
        scratch_shapes=[
            pltpu.VMEM((3, PADDED, 2 * C), BF),
            pltpu.VMEM((9 * 256, 2 * C), BF),
            pltpu.VMEM((27 * C, C), BF),
            pltpu.SemaphoreType.DMA,
        ],
        compiler_params=PARAMS,
        cost_estimate=cost(2 * CELLS * 2304 * 256, 5 << 20),
        name="inner_conv",
    )(vol, weight)


def outer_kernel(
    at_ref, halo, weight, inner, upstream, later, grad, ended, field, held, sem
):
    z = at_ref[0]
    ended[...] = jnp.zeros_like(ended)
    first = pl.multiple_of(z * 18 * C, 18 * C)
    copy = fetched(weight.at[pl.ds(first, 9 * C), :], held, sem)
    shifted_columns([rows_of(halo)], field, 0, False)
    copy.wait()

    def tile(i, carry):
        at = pl.multiple_of(i * TILE, TILE)
        rows = pl.ds(at, TILE)
        preact = inner[z, rows, :] + jnp.dot(
            taps_of(field, at, TILE), held[...], preferred_element_type=F32
        )
        s = jax.nn.sigmoid(preact)
        slopes = s * (1.0 + preact * (1.0 - s))
        grad[rows, :] = (upstream[z, rows, :].astype(F32) * slopes).astype(BF)
        return carry

    lax.fori_loop(0, CELLS // TILE, tile, 0)


def outer_conv(name, z, halo, weight, inner, upstream, later):
    return pl.pallas_call(
        outer_kernel,
        out_shape=[jax.ShapeDtypeStruct((CELLS, C), BF), FLAG],
        in_specs=[SMEM, VMEM, HBM, VMEM, VMEM, ANY],
        out_specs=[VMEM, VMEM],
        scratch_shapes=[
            pltpu.VMEM((3, PADDED, C), BF),
            pltpu.VMEM((9 * C, C), BF),
            pltpu.SemaphoreType.DMA,
        ],
        compiler_params=PARAMS,
        cost_estimate=cost(2 * CELLS * 1152 * 256, 3 << 20, CELLS * 128),
        name=name,
    )(z, halo, weight, inner, upstream, later)


def taps_kernel(core_ref, near, far, near_halo, far_halo, vol_t, kept, sent, field, lhs, whole):
    core = core_ref[0]
    shifted_columns(ordered(core, near, far), field, 0, False)
    before, after = ordered(core, near_halo, far_halo)
    lhs[C : 3 * C, :] = vol_t[...]
    transposed(before, lhs, 0)
    transposed(after, lhs, 3 * C)

    for owner in range(27, 32):
        for group in range(4):
            whole[group * 32 + owner] = jnp.zeros((CHUNK, C), F32)

    def row(b, carry):
        at = pl.multiple_of((2 - b) * COLS, COLS)
        for c in range(3):
            got = jnp.dot(
                lhs[...],
                field[2 - c, pl.ds(at, CELLS), :],
                preferred_element_type=F32,
            )
            for a in range(3):
                summed = (
                    got[a * C : (a + 1) * C, 0:C]
                    + got[(a + 1) * C : (a + 2) * C, C : 2 * C]
                )
                for i in range(4):
                    chunk = 4 * tap(a, b, c) + i
                    whole[chunk + 5 * (chunk // 27)] = summed[
                        i * CHUNK : (i + 1) * CHUNK, :
                    ]
        return carry

    lax.fori_loop(0, 3, row, 0)

    def share(owner, carry):
        for group in range(4):
            kept[owner * 4 + group] = whole[group * 32 + core * 16 + owner]
            sent[owner * 4 + group] = whole[
                group * 32 + (1 - core) * 16 + owner
            ].astype(BF)
        return carry

    lax.fori_loop(0, 16, share, 0)


def kernel_gradient(core, near, far, near_halo, far_halo, vol_t):
    return pl.pallas_call(
        taps_kernel,
        out_shape=[
            jax.ShapeDtypeStruct((64, CHUNK, C), F32),
            jax.ShapeDtypeStruct((64, CHUNK, C), BF),
        ],
        in_specs=[SMEM] + [VMEM] * 5,
        out_specs=[VMEM, VMEM],
        scratch_shapes=[
            pltpu.VMEM((3, PADDED, 2 * C), BF),
            pltpu.VMEM((4 * C, CELLS), BF),
            pltpu.VMEM((4 * 32, CHUNK, C), F32),
        ],
        compiler_params=PARAMS,
        cost_estimate=cost(2 * CELLS * 4608 * 256, 5 << 20),
        name="kernel_gradient",
    )(core, near, far, near_halo, far_halo, vol_t)


def inner_back_kernel(
    core_ref, near, far, weight, upstream, later, out, ended, field, mixed, held, sem
):
    copy = fetched(weight, held, sem)
    ended[...] = jnp.zeros_like(ended)
    shifted_columns(ordered(core_ref[0], near, far), field, 0, False)
    copy.wait()
    for b in range(3):
        for c in range(3):
            base = (b * 3 + c) * 256
            for p in range(2):
                for z in range(2):
                    t = tap(1 + z - p, 2 - b, 2 - c)
                    mixed[z * C : (z + 1) * C, base + p * C : base + (p + 1) * C] = (
                        held[t * C : (t + 1) * C, :]
                    )

    def tile(i, carry):
        at = pl.multiple_of(i * TILE, TILE)
        rows = pl.ds(at, TILE)
        got = lax.dot_general(
            taps_of(field, at, TILE),
            mixed[...],
            (((1,), (1,)), ((), ())),
            preferred_element_type=F32,
        )
        for z in range(2):
            out[z, rows, :] = (
                upstream[z, rows, :].astype(F32) + got[:, z * C : (z + 1) * C]
            )
        return carry

    lax.fori_loop(0, CELLS // TILE, tile, 0)


def inner_back(core, near, far, weight, upstream, later):
    return pl.pallas_call(
        inner_back_kernel,
        out_shape=[
            jax.ShapeDtypeStruct((2, CELLS, C), F32),
            FLAG,
        ],
        in_specs=[SMEM, VMEM, VMEM, HBM, VMEM, ANY],
        out_specs=[VMEM, VMEM],
        scratch_shapes=[
            pltpu.VMEM((3, PADDED, 2 * C), BF),
            pltpu.VMEM((2 * C, 9 * 256), BF),
            pltpu.VMEM((27 * C, C), BF),
            pltpu.SemaphoreType.DMA,
        ],
        compiler_params=WHOLE,
        cost_estimate=cost(2 * CELLS * 2304 * 256, 5 << 20),
        name="inner_back",
    )(core, near, far, weight, upstream, later)


def outer_back_kernel(
    core_ref, near, far, weight, kept, out, field, mixed, held, inner, sem, kept_sem
):
    copy = fetched(weight, held, sem)
    kept_copy = fetched(kept, inner, kept_sem)
    core = core_ref[0]
    shifted_columns([rows_of(near), rows_of(far)], field, 0, False)
    copy.wait()
    for k in range(2):
        z = 1 - core if k == 0 else core
        first = pl.multiple_of((2 - 2 * z) * 9 * C, C)
        for b in range(3):
            for c in range(3):
                base = (b * 3 + c) * C
                mixed[k, :, base : base + C] = held[
                    pl.ds(first + tap(0, 2 - b, 2 - c) * C, C), :
                ]

    kept_copy.wait()

    def tile(i, carry):
        at = pl.multiple_of(i * TILE, TILE)
        rows = pl.ds(at, TILE)
        for k in range(2):
            z = 1 - core if k == 0 else core
            lhs = jnp.concatenate(
                [
                    field[
                        c,
                        pl.ds(pl.multiple_of(at + b * COLS, COLS), TILE),
                        k * C : (k + 1) * C,
                    ]
                    for b in range(3)
                    for c in range(3)
                ],
                axis=1,
            )
            got = lax.dot_general(
                lhs, mixed[k], (((1,), (1,)), ((), ())), preferred_element_type=F32
            )
            out[z, rows, :] = (inner[z, rows, :] + got).astype(BF)
        return carry

    lax.fori_loop(0, CELLS // TILE, tile, 0)


def outer_back(core, near, far, weight, inner):
    return pl.pallas_call(
        outer_back_kernel,
        out_shape=jax.ShapeDtypeStruct((2, CELLS, C), BF),
        in_specs=[SMEM, VMEM, VMEM, HBM, HBM],
        out_specs=VMEM,
        scratch_shapes=[
            pltpu.VMEM((3, PADDED, 2 * C), BF),
            pltpu.VMEM((2, C, 9 * C), BF),
            pltpu.VMEM((27 * C, C), BF),
            pltpu.VMEM((2, CELLS, C), F32),
            pltpu.SemaphoreType.DMA,
            pltpu.SemaphoreType.DMA,
        ],
        compiler_params=WHOLE,
        cost_estimate=cost(2 * CELLS * 2304 * 256, 5 << 20),
        name="outer_back",
    )(core, near, far, weight, inner)


def plane_kernel(at_ref, vol, later, plane, ended, sem):
    copy = fetched(vol.at[at_ref[0]], plane, sem)
    ended[...] = jnp.zeros_like(ended)
    copy.wait()


def one_plane(name, at, vol, later):
    return pl.pallas_call(
        plane_kernel,
        out_shape=[jax.ShapeDtypeStruct((CELLS, C), BF), FLAG],
        in_specs=[SMEM, HBM, ANY],
        out_specs=[HBM, VMEM],
        scratch_shapes=[pltpu.SemaphoreType.DMA],
        compiler_params=WHOLE,
        cost_estimate=cost(0, 1 << 20),
        name=name,
    )(at, vol, later)


def first_rows_kernel(whole, out):
    out[...] = whole[0 : out.shape[0], :].astype(F32)


def first_rows(whole, rows):
    return pl.pallas_call(
        first_rows_kernel,
        out_shape=jax.ShapeDtypeStruct((rows, C), F32),
        in_specs=[VMEM],
        out_specs=VMEM,
        compiler_params=SMALL,
        cost_estimate=cost(0, 1 << 20),
        name="first_rows",
    )(whole)


def mix_kernel(got, later, out):
    for group in range(4):
        total = got[0, group].astype(F32)
        for k in range(1, 16):
            total += got[k, group].astype(F32)
        out[group] = total
        out[4 + group] = total


def mixed_rows(got, later):
    return pl.pallas_call(
        mix_kernel,
        out_shape=jax.ShapeDtypeStruct((8, CHUNK, C), F32),
        in_specs=[VMEM, ANY],
        out_specs=VMEM,
        compiler_params=SMALL,
        cost_estimate=cost(1 << 18, 1 << 20),
        name="mixed_rows",
    )(got, later)


def step_kernel(at_ref, got, first, second, out):
    total = got[0]
    for k in range(1, 8):
        total += got[k]
    at = pl.multiple_of(at_ref[0], CHUNK)
    rows = pl.ds(at, CHUNK)
    step = adam(total, first[rows, :], second[rows, :])
    step = step.astype(BF)
    for k in range(OWNERS):
        out[k] = step


def spread_step(at, got, first, second):
    return pl.pallas_call(
        step_kernel,
        out_shape=jax.ShapeDtypeStruct((OWNERS, CHUNK, C), BF),
        in_specs=[SMEM] + [VMEM] * 3,
        out_specs=VMEM,
        compiler_params=SMALL,
        cost_estimate=cost(1 << 18, 1 << 20),
        name="spread_step",
    )(at, got, first, second)


def adam(grad, first, second):
    m_new = beta_one * first + (1.0 - beta_one) * grad
    v_new = beta_two * second + (1.0 - beta_two) * grad * grad
    return (
        m_new
        / (1.0 - beta_one**ADAM_STEP)
        / (jnp.sqrt(v_new / (1.0 - beta_two**ADAM_STEP)) + eps_adam)
    )


def from_neighbours(near, far):
    size = lax.axis_size(SPACE)
    pairs = [(i, i + 1) for i in range(1, size - 1, 2)]
    far_halo = lax.ppermute(far, SPACE, pairs + [(j, i) for i, j in pairs])
    near_halo = lax.ppermute(near, "core", [(0, 1), (1, 0)])
    return near_halo, far_halo


def body(volume, upstream, weight, first_moment, second_moment):
    vol = volume.reshape(2, CELLS, C)
    up = upstream.reshape(2, CELLS, C)
    core = lax.axis_index("core")
    at_core, at_near = core.reshape(1), (1 - core).reshape(1)
    far_plane, ended = one_plane("far_plane", at_core, vol, at_core)
    near_plane, ended = one_plane("near_plane", at_near, vol, ended)
    near_halo, far_halo = from_neighbours(near_plane, far_plane)
    inner, vol_t = inner_conv(vol, weight)
    near, ended = outer_conv(
        "near_conv", at_near, near_halo, weight, inner, up, at_core
    )
    far, ended = outer_conv(
        "far_conv", at_core, far_halo, weight, inner, up, ended
    )
    kept, sent = kernel_gradient(at_core, near, far, near_halo, far_halo, vol_t)

    rows = first_moment.shape[0]
    other = lax.ppermute(sent, "core", [(0, 1), (1, 0)])
    half = (kept + other.astype(F32)).astype(BF).reshape(16, 4, CHUNK, C)
    got = lax.all_to_all(half, ("x", "y"), 0, 0)
    grad_near, grad_far = from_neighbours(near, far)
    local, ended = inner_back(at_core, near, far, weight, up, half)
    part = mixed_rows(got, ended)
    got = lax.all_to_all(part, ("zl", "sample"), 0, 0)
    owner = core * 16 + lax.axis_index("x") * 4 + lax.axis_index("y")
    at = jnp.minimum(owner * CHUNK, rows - CHUNK).reshape(1)
    step = spread_step(at, got, first_moment, second_moment)
    whole = lax.all_to_all(step, ("core", "x", "y"), 0, 0)
    grad_volume = outer_back(at_core, grad_near, grad_far, weight, local)
    direction = first_rows(whole.reshape(OWNERS * CHUNK, C), rows)
    return (grad_volume.reshape(volume.shape), direction)


def solution(mesh):
    fine = Mesh(
        mesh.devices.reshape(4, 4, 2, 2, 4), ("x", "y", "zl", "core", "sample")
    )
    field = P("sample", SPACE, None, None, None)
    return jax.shard_map(
        body,
        mesh=fine,
        in_specs=(field, field, P(), P("sample", None), P("sample", None)),
        out_specs=(field, P("sample", None)),
        check_vma=False,
    )
```

```python
import functools
import jax
import jax.numpy as jnp
from jax import lax
from jax.experimental import pallas as pl
from jax.experimental.pallas import tpu as pltpu
from jax.sharding import Mesh, PartitionSpec as P

ADAM_STEP = 10


beta_one = 0.9
beta_two = 0.999
eps_adam = 1e-08

SPACE = ("x", "y", "zl", "core")
CHUNK = 32
OWNERS = 32
C = 128
COLS = 64
ROWS = 32
CELLS = ROWS * COLS
PADDED = CELLS + 2 * COLS
STRIP = 256
TILE = 512
BF = jnp.bfloat16
F32 = jnp.float32
VMEM = pl.BlockSpec(memory_space=pltpu.VMEM)
ANY = pl.BlockSpec(memory_space=pl.ANY)
HBM = pl.BlockSpec(memory_space=pltpu.HBM)
SMEM = pl.BlockSpec(memory_space=pltpu.SMEM)
FLAG = jax.ShapeDtypeStruct((8, C), F32)
WHOLE = pltpu.CompilerParams(vmem_limit_bytes=60 * 1024 * 1024)
SMALL = pltpu.CompilerParams(vmem_limit_bytes=4 * 1024 * 1024)
PARAMS = pltpu.CompilerParams(vmem_limit_bytes=32 * 1024 * 1024)


def cost(flops, moved, special=0):
    return pl.CostEstimate(flops=flops, bytes_accessed=moved, transcendentals=special)


def shifted_columns(planes, out, first, flip):
    width = 128 * len(planes)
    blank = jnp.zeros((COLS, width), BF)
    cols = slice(first, first + width)
    for c in range(3):
        out[c, 0:COLS, cols] = blank
        out[c, PADDED - COLS : PADDED, cols] = blank
    before, after = (2, 0) if flip else (0, 2)

    def strip(i, carry):
        at = pl.multiple_of(i * STRIP, STRIP)
        to = pl.ds(pl.multiple_of(at + COLS, COLS), STRIP)
        col = lax.broadcasted_iota(jnp.int32, (STRIP, C), 0) & (COLS - 1)
        for k, plane in enumerate(planes):
            cols = slice(first + k * C, first + (k + 1) * C)
            here = plane(pl.ds(at, STRIP))
            wide = here.astype(F32)
            out[1, to, cols] = here
            out[before, to, cols] = jnp.where(
                col == 0, 0.0, pltpu.roll(wide, 1, 0)
            ).astype(BF)
            out[after, to, cols] = jnp.where(
                col == COLS - 1, 0.0, pltpu.roll(wide, STRIP - 1, 0)
            ).astype(BF)
        return carry

    lax.fori_loop(0, CELLS // STRIP, strip, 0)


def transposed(plane, out, first):
    for at in range(0, CELLS, TILE):
        out[first : first + C, at : at + TILE] = jnp.transpose(
            plane(pl.ds(at, TILE))
        )


def rows_of(plane):
    return lambda rows: plane[rows, :]


def ordered(core, near, far):
    def pick(first, second):
        return lambda rows: jnp.where(core == 0, first[rows, :], second[rows, :])

    return pick(far, near), pick(near, far)


def fetched(source, held, sem):
    copy = pltpu.make_async_copy(source, held, sem)
    copy.start()
    return copy


def tap(a, b, c):
    return (a * 3 + b) * 3 + c


def taps_of(field, at, rows):
    return jnp.concatenate(
        [
            field[c, pl.ds(pl.multiple_of(at + b * COLS, COLS), rows), :]
            for b in range(3)
            for c in range(3)
        ],
        axis=1,
    )


def inner_kernel(vol, weight, out, vol_t, field, mixed, held, sem):
    copy = fetched(weight, held, sem)
    planes = [rows_of(vol.at[0]), rows_of(vol.at[1])]
    shifted_columns(planes, field, 0, False)
    copy.wait()
    for b in range(3):
        for c in range(3):
            base = (b * 3 + c) * 256
            for p in range(2):
                for z in range(2):
                    t = tap(1 + p - z, b, c)
                    mixed[base + p * C : base + (p + 1) * C, z * C : (z + 1) * C] = (
                        held[t * C : (t + 1) * C, :]
                    )

    def tile(i, carry):
        at = pl.multiple_of(i * TILE, TILE)
        got = jnp.dot(taps_of(field, at, TILE), mixed[...], preferred_element_type=F32)
        out[0, pl.ds(at, TILE), :] = got[:, 0:C]
        out[1, pl.ds(at, TILE), :] = got[:, C : 2 * C]
        return carry

    lax.fori_loop(0, CELLS // TILE, tile, 0)
    for p in range(2):
        transposed(planes[p], vol_t, p * C)


def inner_conv(vol, weight):
    return pl.pallas_call(
        inner_kernel,
        out_shape=[
            jax.ShapeDtypeStruct((2, CELLS, C), F32),
            jax.ShapeDtypeStruct((2 * C, CELLS), BF),
        ],
        in_specs=[VMEM, HBM],
        out_specs=[VMEM] * 2,
        scratch_shapes=[
            pltpu.VMEM((3, PADDED, 2 * C), BF),
            pltpu.VMEM((9 * 256, 2 * C), BF),
            pltpu.VMEM((27 * C, C), BF),
            pltpu.SemaphoreType.DMA,
        ],
        compiler_params=PARAMS,
        cost_estimate=cost(2 * CELLS * 2304 * 256, 5 << 20),
        name="inner_conv",
    )(vol, weight)


def outer_kernel(
    at_ref, halo, weight, inner, upstream, later, grad, ended, field, held, sem
):
    z = at_ref[0]
    ended[...] = jnp.zeros_like(ended)
    first = pl.multiple_of(z * 18 * C, 18 * C)
    copy = fetched(weight.at[pl.ds(first, 9 * C), :], held, sem)
    shifted_columns([rows_of(halo)], field, 0, False)
    copy.wait()

    def tile(i, carry):
        at = pl.multiple_of(i * TILE, TILE)
        rows = pl.ds(at, TILE)
        preact = inner[z, rows, :] + jnp.dot(
            taps_of(field, at, TILE), held[...], preferred_element_type=F32
        )
        s = jax.nn.sigmoid(preact)
        slopes = s * (1.0 + preact * (1.0 - s))
        grad[rows, :] = (upstream[z, rows, :].astype(F32) * slopes).astype(BF)
        return carry

    lax.fori_loop(0, CELLS // TILE, tile, 0)


def outer_conv(name, z, halo, weight, inner, upstream, later):
    return pl.pallas_call(
        outer_kernel,
        out_shape=[jax.ShapeDtypeStruct((CELLS, C), BF), FLAG],
        in_specs=[SMEM, VMEM, HBM, VMEM, VMEM, ANY],
        out_specs=[VMEM, VMEM],
        scratch_shapes=[
            pltpu.VMEM((3, PADDED, C), BF),
            pltpu.VMEM((9 * C, C), BF),
            pltpu.SemaphoreType.DMA,
        ],
        compiler_params=PARAMS,
        cost_estimate=cost(2 * CELLS * 1152 * 256, 3 << 20, CELLS * 128),
        name=name,
    )(z, halo, weight, inner, upstream, later)


def taps_kernel(core_ref, near, far, near_halo, far_halo, vol_t, kept, sent, field, lhs, whole):
    core = core_ref[0]
    shifted_columns(ordered(core, near, far), field, 0, False)
    before, after = ordered(core, near_halo, far_halo)
    lhs[C : 3 * C, :] = vol_t[...]
    transposed(before, lhs, 0)
    transposed(after, lhs, 3 * C)

    for owner in range(27, 32):
        for group in range(4):
            whole[group * 32 + owner] = jnp.zeros((CHUNK, C), F32)

    def row(b, carry):
        at = pl.multiple_of((2 - b) * COLS, COLS)
        for c in range(3):
            got = jnp.dot(
                lhs[...],
                field[2 - c, pl.ds(at, CELLS), :],
                preferred_element_type=F32,
            )
            for a in range(3):
                summed = (
                    got[a * C : (a + 1) * C, 0:C]
                    + got[(a + 1) * C : (a + 2) * C, C : 2 * C]
                )
                for i in range(4):
                    chunk = 4 * tap(a, b, c) + i
                    whole[chunk + 5 * (chunk // 27)] = summed[
                        i * CHUNK : (i + 1) * CHUNK, :
                    ]
        return carry

    lax.fori_loop(0, 3, row, 0)

    def share(owner, carry):
        for group in range(4):
            kept[owner * 4 + group] = whole[group * 32 + core * 16 + owner]
            sent[owner * 4 + group] = whole[
                group * 32 + (1 - core) * 16 + owner
            ].astype(BF)
        return carry

    lax.fori_loop(0, 16, share, 0)


def kernel_gradient(core, near, far, near_halo, far_halo, vol_t):
    return pl.pallas_call(
        taps_kernel,
        out_shape=[
            jax.ShapeDtypeStruct((64, CHUNK, C), F32),
            jax.ShapeDtypeStruct((64, CHUNK, C), BF),
        ],
        in_specs=[SMEM] + [VMEM] * 5,
        out_specs=[VMEM, VMEM],
        scratch_shapes=[
            pltpu.VMEM((3, PADDED, 2 * C), BF),
            pltpu.VMEM((4 * C, CELLS), BF),
            pltpu.VMEM((4 * 32, CHUNK, C), F32),
        ],
        compiler_params=PARAMS,
        cost_estimate=cost(2 * CELLS * 4608 * 256, 5 << 20),
        name="kernel_gradient",
    )(core, near, far, near_halo, far_halo, vol_t)


def back_kernel(
    core_ref,
    near,
    far,
    near_halo,
    far_halo,
    weight,
    given,
    later,
    out,
    field,
    mixed,
    held,
    upstream,
    sem,
    given_sem,
):
    copy = fetched(weight, held, sem)
    given_copy = fetched(given, upstream, given_sem)
    core = core_ref[0]
    low, high = ordered(core, near, far)
    before, after = ordered(core, near_halo, far_halo)
    shifted_columns([before, low, high, after], field, 0, False)
    blank = jnp.zeros((C, C), BF)
    copy.wait()
    for b in range(3):
        for c in range(3):
            base = (b * 3 + c) * 512
            for p in range(4):
                for z in range(2):
                    a = 2 - (p - z)
                    t = tap(a, 2 - b, 2 - c)
                    mixed[z * C : (z + 1) * C, base + p * C : base + (p + 1) * C] = (
                        held[t * C : (t + 1) * C, :] if 0 <= a < 3 else blank
                    )

    given_copy.wait()

    def tile(i, carry):
        at = pl.multiple_of(i * TILE, TILE)
        rows = pl.ds(at, TILE)
        got = lax.dot_general(
            taps_of(field, at, TILE),
            mixed[...],
            (((1,), (1,)), ((), ())),
            preferred_element_type=F32,
        )
        for z in range(2):
            out[z, rows, :] = (
                upstream[z, rows, :].astype(F32) + got[:, z * C : (z + 1) * C]
            ).astype(BF)
        return carry

    lax.fori_loop(0, CELLS // TILE, tile, 0)


def back_conv(core, near, far, near_halo, far_halo, weight, upstream, later):
    return pl.pallas_call(
        back_kernel,
        out_shape=jax.ShapeDtypeStruct((2, CELLS, C), BF),
        in_specs=[SMEM, VMEM, VMEM, VMEM, VMEM, HBM, HBM, ANY],
        out_specs=VMEM,
        scratch_shapes=[
            pltpu.VMEM((3, PADDED, 4 * C), BF),
            pltpu.VMEM((2 * C, 9 * 512), BF),
            pltpu.VMEM((27 * C, C), BF),
            pltpu.VMEM((2, CELLS, C), BF),
            pltpu.SemaphoreType.DMA,
            pltpu.SemaphoreType.DMA,
        ],
        compiler_params=WHOLE,
        cost_estimate=cost(2 * CELLS * 4608 * 256, 5 << 20),
        name="back_conv",
    )(core, near, far, near_halo, far_halo, weight, upstream, later)


def planes_kernel(core_ref, vol, near, far, sems):
    core = core_ref[0]
    first = fetched(vol.at[core], far, sems.at[0])
    second = fetched(vol.at[1 - core], near, sems.at[1])
    first.wait()
    second.wait()


def both_planes(core, vol):
    plane = jax.ShapeDtypeStruct((CELLS, C), BF)
    return pl.pallas_call(
        planes_kernel,
        out_shape=[plane, plane],
        in_specs=[SMEM, HBM],
        out_specs=[VMEM, VMEM],
        scratch_shapes=[pltpu.SemaphoreType.DMA((2,))],
        compiler_params=WHOLE,
        cost_estimate=cost(0, 2 << 20),
        name="both_planes",
    )(core, vol)


def first_rows_kernel(whole, out):
    out[...] = whole[0 : out.shape[0], :].astype(F32)


def first_rows(whole, rows):
    return pl.pallas_call(
        first_rows_kernel,
        out_shape=jax.ShapeDtypeStruct((rows, C), F32),
        in_specs=[VMEM],
        out_specs=VMEM,
        compiler_params=SMALL,
        cost_estimate=cost(0, 1 << 20),
        name="first_rows",
    )(whole)


def mix_kernel(got, out):
    for group in range(4):
        total = got[0, group].astype(F32)
        for k in range(1, 16):
            total += got[k, group].astype(F32)
        out[group] = total.astype(BF)
        out[4 + group] = total.astype(BF)


def mixed_rows(got):
    return pl.pallas_call(
        mix_kernel,
        out_shape=jax.ShapeDtypeStruct((8, CHUNK, C), BF),
        in_specs=[VMEM],
        out_specs=VMEM,
        compiler_params=SMALL,
        cost_estimate=cost(1 << 18, 1 << 20),
        name="mixed_rows",
    )(got)


def step_kernel(at_ref, got, first, second, out, ended):
    total = got[0].astype(F32)
    for k in range(1, 8):
        total += got[k].astype(F32)
    at = pl.multiple_of(at_ref[0], CHUNK)
    rows = pl.ds(at, CHUNK)
    step = adam(total, first[rows, :], second[rows, :])
    ended[...] = jnp.zeros_like(ended)
    step = step.astype(BF)
    for k in range(OWNERS):
        out[k] = step


def spread_step(at, got, first, second):
    return pl.pallas_call(
        step_kernel,
        out_shape=[jax.ShapeDtypeStruct((OWNERS, CHUNK, C), BF), FLAG],
        in_specs=[SMEM] + [VMEM] * 3,
        out_specs=[VMEM, VMEM],
        compiler_params=SMALL,
        cost_estimate=cost(1 << 18, 1 << 20),
        name="spread_step",
    )(at, got, first, second)


def adam(grad, first, second):
    m_new = beta_one * first + (1.0 - beta_one) * grad
    v_new = beta_two * second + (1.0 - beta_two) * grad * grad
    return (
        m_new
        / (1.0 - beta_one**ADAM_STEP)
        / (jnp.sqrt(v_new / (1.0 - beta_two**ADAM_STEP)) + eps_adam)
    )


def from_neighbours(near, far):
    size = lax.axis_size(SPACE)
    pairs = [(i, i + 1) for i in range(1, size - 1, 2)]
    far_halo = lax.ppermute(far, SPACE, pairs + [(j, i) for i, j in pairs])
    near_halo = lax.ppermute(near, "core", [(0, 1), (1, 0)])
    return near_halo, far_halo


def body(volume, upstream, weight, first_moment, second_moment):
    vol = volume.reshape(2, CELLS, C)
    up = upstream.reshape(2, CELLS, C)
    core = lax.axis_index("core")
    at_core, at_near = core.reshape(1), (1 - core).reshape(1)
    near_halo, far_halo = from_neighbours(*both_planes(at_core, vol))
    inner, vol_t = inner_conv(vol, weight)
    near, ended = outer_conv(
        "near_conv", at_near, near_halo, weight, inner, up, at_core
    )
    far, ended = outer_conv(
        "far_conv", at_core, far_halo, weight, inner, up, ended
    )
    kept, sent = kernel_gradient(at_core, near, far, near_halo, far_halo, vol_t)

    rows = first_moment.shape[0]
    other = lax.ppermute(sent, "core", [(0, 1), (1, 0)])
    half = (kept + other.astype(F32)).astype(BF).reshape(16, 4, CHUNK, C)
    got = lax.all_to_all(half, ("x", "y"), 0, 0)
    grad_near, grad_far = from_neighbours(near, far)
    part = mixed_rows(got)
    got = lax.all_to_all(part, ("zl", "sample"), 0, 0)
    owner = core * 16 + lax.axis_index("x") * 4 + lax.axis_index("y")
    at = jnp.minimum(owner * CHUNK, rows - CHUNK).reshape(1)
    step, ended = spread_step(at, got, first_moment, second_moment)
    whole = lax.all_to_all(step, ("core", "x", "y"), 0, 0)
    grad_volume = back_conv(
        at_core, near, far, grad_near, grad_far, weight, up, ended
    )
    direction = first_rows(whole.reshape(OWNERS * CHUNK, C), rows)
    return (grad_volume.reshape(volume.shape), direction)


def solution(mesh):
    fine = Mesh(
        mesh.devices.reshape(4, 4, 2, 2, 4), ("x", "y", "zl", "core", "sample")
    )
    field = P("sample", SPACE, None, None, None)
    return jax.shard_map(
        body,
        mesh=fine,
        in_specs=(field, field, P(), P("sample", None), P("sample", None)),
        out_specs=(field, P("sample", None)),
        check_vma=False,
    )
```

```python
import functools
import jax
import jax.numpy as jnp
from jax import lax
from jax.experimental import pallas as pl
from jax.experimental.pallas import tpu as pltpu
from jax.sharding import Mesh, PartitionSpec as P

ADAM_STEP = 10


beta_one = 0.9
beta_two = 0.999
eps_adam = 1e-08

SPACE = ("x", "y", "zl", "core")
CHUNK = 32
OWNERS = 32
C = 128
COLS = 64
ROWS = 32
CELLS = ROWS * COLS
PADDED = CELLS + 2 * COLS
STRIP = 256
TILE = 512
BF = jnp.bfloat16
F32 = jnp.float32
VMEM = pl.BlockSpec(memory_space=pltpu.VMEM)
ANY = pl.BlockSpec(memory_space=pl.ANY)
HBM = pl.BlockSpec(memory_space=pltpu.HBM)
SMEM = pl.BlockSpec(memory_space=pltpu.SMEM)
FLAG = jax.ShapeDtypeStruct((8, C), F32)
WHOLE = pltpu.CompilerParams(vmem_limit_bytes=60 * 1024 * 1024)
LARGE = pltpu.CompilerParams(vmem_limit_bytes=62 * 1024 * 1024)
SMALL = pltpu.CompilerParams(vmem_limit_bytes=4 * 1024 * 1024)
PARAMS = pltpu.CompilerParams(vmem_limit_bytes=32 * 1024 * 1024)


def cost(flops, moved, special=0):
    return pl.CostEstimate(flops=flops, bytes_accessed=moved, transcendentals=special)


def shifted_columns(planes, out, first, flip):
    width = 128 * len(planes)
    blank = jnp.zeros((COLS, width), BF)
    cols = slice(first, first + width)
    for c in range(3):
        out[c, 0:COLS, cols] = blank
        out[c, PADDED - COLS : PADDED, cols] = blank
    before, after = (2, 0) if flip else (0, 2)

    def strip(i, carry):
        at = pl.multiple_of(i * STRIP, STRIP)
        to = pl.ds(pl.multiple_of(at + COLS, COLS), STRIP)
        col = lax.broadcasted_iota(jnp.int32, (STRIP, C), 0) & (COLS - 1)
        for k, plane in enumerate(planes):
            cols = slice(first + k * C, first + (k + 1) * C)
            here = plane(pl.ds(at, STRIP))
            wide = here.astype(F32)
            out[1, to, cols] = here
            out[before, to, cols] = jnp.where(
                col == 0, 0.0, pltpu.roll(wide, 1, 0)
            ).astype(BF)
            out[after, to, cols] = jnp.where(
                col == COLS - 1, 0.0, pltpu.roll(wide, STRIP - 1, 0)
            ).astype(BF)
        return carry

    lax.fori_loop(0, CELLS // STRIP, strip, 0)


def transposed(plane, out, first):
    for at in range(0, CELLS, TILE):
        out[first : first + C, at : at + TILE] = jnp.transpose(
            plane(pl.ds(at, TILE))
        )


def rows_of(plane):
    return lambda rows: plane[rows, :]


def ordered(core, near, far):
    def pick(first, second):
        return lambda rows: jnp.where(core == 0, first[rows, :], second[rows, :])

    return pick(far, near), pick(near, far)


def fetched(source, held, sem):
    copy = pltpu.make_async_copy(source, held, sem)
    copy.start()
    return copy


def tap(a, b, c):
    return (a * 3 + b) * 3 + c


def taps_of(field, at, rows):
    return jnp.concatenate(
        [
            field[c, pl.ds(pl.multiple_of(at + b * COLS, COLS), rows), :]
            for b in range(3)
            for c in range(3)
        ],
        axis=1,
    )


def inner_kernel(vol, weight, out, vol_t, field, mixed, held, sem):
    copy = fetched(weight, held, sem)
    planes = [rows_of(vol.at[0]), rows_of(vol.at[1])]
    shifted_columns(planes, field, 0, False)
    copy.wait()
    for b in range(3):
        for c in range(3):
            base = (b * 3 + c) * 256
            for p in range(2):
                for z in range(2):
                    t = tap(1 + p - z, b, c)
                    mixed[base + p * C : base + (p + 1) * C, z * C : (z + 1) * C] = (
                        held[t * C : (t + 1) * C, :]
                    )

    def tile(i, carry):
        at = pl.multiple_of(i * TILE, TILE)
        got = jnp.dot(taps_of(field, at, TILE), mixed[...], preferred_element_type=F32)
        out[0, pl.ds(at, TILE), :] = got[:, 0:C]
        out[1, pl.ds(at, TILE), :] = got[:, C : 2 * C]
        return carry

    lax.fori_loop(0, CELLS // TILE, tile, 0)
    for p in range(2):
        transposed(planes[p], vol_t, p * C)


def inner_conv(vol, weight):
    return pl.pallas_call(
        inner_kernel,
        out_shape=[
            jax.ShapeDtypeStruct((2, CELLS, C), F32),
            jax.ShapeDtypeStruct((2 * C, CELLS), BF),
        ],
        in_specs=[VMEM, HBM],
        out_specs=[VMEM] * 2,
        scratch_shapes=[
            pltpu.VMEM((3, PADDED, 2 * C), BF),
            pltpu.VMEM((9 * 256, 2 * C), BF),
            pltpu.VMEM((27 * C, C), BF),
            pltpu.SemaphoreType.DMA,
        ],
        compiler_params=PARAMS,
        cost_estimate=cost(2 * CELLS * 2304 * 256, 5 << 20),
        name="inner_conv",
    )(vol, weight)


def outer_kernel(
    at_ref, halo, weight, inner, upstream, later, grad, ended, field, held, sem
):
    z = at_ref[0]
    ended[...] = jnp.zeros_like(ended)
    first = pl.multiple_of(z * 18 * C, 18 * C)
    copy = fetched(weight.at[pl.ds(first, 9 * C), :], held, sem)
    shifted_columns([rows_of(halo)], field, 0, False)
    copy.wait()

    def tile(i, carry):
        at = pl.multiple_of(i * TILE, TILE)
        rows = pl.ds(at, TILE)
        preact = inner[z, rows, :] + jnp.dot(
            taps_of(field, at, TILE), held[...], preferred_element_type=F32
        )
        s = jax.nn.sigmoid(preact)
        slopes = s * (1.0 + preact * (1.0 - s))
        grad[rows, :] = (upstream[z, rows, :].astype(F32) * slopes).astype(BF)
        return carry

    lax.fori_loop(0, CELLS // TILE, tile, 0)


def outer_conv(name, z, halo, weight, inner, upstream, later):
    return pl.pallas_call(
        outer_kernel,
        out_shape=[jax.ShapeDtypeStruct((CELLS, C), BF), FLAG],
        in_specs=[SMEM, VMEM, HBM, VMEM, VMEM, ANY],
        out_specs=[VMEM, VMEM],
        scratch_shapes=[
            pltpu.VMEM((3, PADDED, C), BF),
            pltpu.VMEM((9 * C, C), BF),
            pltpu.SemaphoreType.DMA,
        ],
        compiler_params=PARAMS,
        cost_estimate=cost(2 * CELLS * 1152 * 256, 3 << 20, CELLS * 128),
        name=name,
    )(z, halo, weight, inner, upstream, later)


def taps_kernel(core_ref, near, far, near_halo, far_halo, vol_t, kept, sent, field, lhs, whole):
    core = core_ref[0]
    shifted_columns(ordered(core, near, far), field, 0, False)
    before, after = ordered(core, near_halo, far_halo)
    lhs[C : 3 * C, :] = vol_t[...]
    transposed(before, lhs, 0)
    transposed(after, lhs, 3 * C)

    for owner in range(27, 32):
        for group in range(4):
            whole[group * 32 + owner] = jnp.zeros((CHUNK, C), F32)

    def row(b, carry):
        at = pl.multiple_of((2 - b) * COLS, COLS)
        for c in range(3):
            got = jnp.dot(
                lhs[...],
                field[2 - c, pl.ds(at, CELLS), :],
                preferred_element_type=F32,
            )
            for a in range(3):
                summed = (
                    got[a * C : (a + 1) * C, 0:C]
                    + got[(a + 1) * C : (a + 2) * C, C : 2 * C]
                )
                for i in range(4):
                    chunk = 4 * tap(a, b, c) + i
                    whole[chunk + 5 * (chunk // 27)] = summed[
                        i * CHUNK : (i + 1) * CHUNK, :
                    ]
        return carry

    lax.fori_loop(0, 3, row, 0)

    def share(owner, carry):
        for group in range(4):
            kept[owner * 4 + group] = whole[group * 32 + core * 16 + owner]
            sent[owner * 4 + group] = whole[
                group * 32 + (1 - core) * 16 + owner
            ].astype(BF)
        return carry

    lax.fori_loop(0, 16, share, 0)


def kernel_gradient(core, near, far, near_halo, far_halo, vol_t):
    return pl.pallas_call(
        taps_kernel,
        out_shape=[
            jax.ShapeDtypeStruct((64, CHUNK, C), F32),
            jax.ShapeDtypeStruct((64, CHUNK, C), BF),
        ],
        in_specs=[SMEM] + [VMEM] * 5,
        out_specs=[VMEM, VMEM],
        scratch_shapes=[
            pltpu.VMEM((3, PADDED, 2 * C), BF),
            pltpu.VMEM((4 * C, CELLS), BF),
            pltpu.VMEM((4 * 32, CHUNK, C), F32),
        ],
        compiler_params=PARAMS,
        cost_estimate=cost(2 * CELLS * 4608 * 256, 5 << 20),
        name="kernel_gradient",
    )(core, near, far, near_halo, far_halo, vol_t)


def inner_back_kernel(
    core_ref, near, far, weight, later, out, ended, field, mixed, held, made, sem, sems
):
    copy = fetched(weight, held, sem)
    ended[0] = 0
    shifted_columns(ordered(core_ref[0], near, far), field, 0, False)
    copy.wait()
    for b in range(3):
        for c in range(3):
            base = (b * 3 + c) * 256
            for p in range(2):
                for z in range(2):
                    t = tap(1 + z - p, 2 - b, 2 - c)
                    mixed[z * C : (z + 1) * C, base + p * C : base + (p + 1) * C] = (
                        held[t * C : (t + 1) * C, :]
                    )
    tiles = CELLS // TILE

    def leave(i, z):
        rows = pl.ds(pl.multiple_of(i * TILE, TILE), TILE)
        return pltpu.make_async_copy(
            made.at[z, rows, :], out.at[z, rows, :], sems.at[i, z]
        )

    def tile(i, carry):
        at = pl.multiple_of(i * TILE, TILE)
        got = lax.dot_general(
            taps_of(field, at, TILE),
            mixed[...],
            (((1,), (1,)), ((), ())),
            preferred_element_type=F32,
        )
        for z in range(2):
            made[z, pl.ds(at, TILE), :] = got[:, z * C : (z + 1) * C]
            leave(i, z).start()
        return carry

    lax.fori_loop(0, tiles, tile, 0)
    for i in range(tiles):
        for z in range(2):
            leave(i, z).wait()


def inner_back(core, near, far, weight, later):
    return pl.pallas_call(
        inner_back_kernel,
        out_shape=[
            jax.ShapeDtypeStruct((2, CELLS, C), F32),
            jax.ShapeDtypeStruct((1,), jnp.int32),
        ],
        in_specs=[SMEM, VMEM, VMEM, HBM, ANY],
        out_specs=[HBM, SMEM],
        scratch_shapes=[
            pltpu.VMEM((3, PADDED, 2 * C), BF),
            pltpu.VMEM((2 * C, 9 * 256), BF),
            pltpu.VMEM((27 * C, C), BF),
            pltpu.VMEM((2, CELLS, C), F32),
            pltpu.SemaphoreType.DMA,
            pltpu.SemaphoreType.DMA((CELLS // TILE, 2)),
        ],
        compiler_params=WHOLE,
        cost_estimate=cost(2 * CELLS * 2304 * 256, 5 << 20),
        name="inner_back",
    )(core, near, far, weight, later)


def outer_back_kernel(
    core_ref, near, far, weight, given, kept, out, field, mixed, held, upstream, inner, sems
):
    copy = fetched(weight, held, sems.at[0])
    kept_copy = fetched(kept, inner, sems.at[1])
    given_copy = fetched(given, upstream, sems.at[2])
    core = core_ref[0]
    shifted_columns([rows_of(near), rows_of(far)], field, 0, False)
    copy.wait()
    for k in range(2):
        z = 1 - core if k == 0 else core
        first = pl.multiple_of((2 - 2 * z) * 9 * C, C)
        for b in range(3):
            for c in range(3):
                base = (b * 3 + c) * C
                mixed[k, :, base : base + C] = held[
                    pl.ds(first + tap(0, 2 - b, 2 - c) * C, C), :
                ]
    kept_copy.wait()
    given_copy.wait()

    def tile(i, carry):
        at = pl.multiple_of(i * TILE, TILE)
        rows = pl.ds(at, TILE)
        for k in range(2):
            z = 1 - core if k == 0 else core
            lhs = jnp.concatenate(
                [
                    field[
                        c,
                        pl.ds(pl.multiple_of(at + b * COLS, COLS), TILE),
                        k * C : (k + 1) * C,
                    ]
                    for b in range(3)
                    for c in range(3)
                ],
                axis=1,
            )
            got = lax.dot_general(
                lhs, mixed[k], (((1,), (1,)), ((), ())), preferred_element_type=F32
            )
            out[z, rows, :] = (
                upstream[z, rows, :].astype(F32) + (inner[z, rows, :] + got)
            ).astype(BF)
        return carry

    lax.fori_loop(0, CELLS // TILE, tile, 0)


def outer_back(core, near, far, weight, given, inner):
    return pl.pallas_call(
        outer_back_kernel,
        out_shape=jax.ShapeDtypeStruct((2, CELLS, C), BF),
        in_specs=[SMEM, VMEM, VMEM, HBM, HBM, HBM],
        out_specs=VMEM,
        scratch_shapes=[
            pltpu.VMEM((3, PADDED, 2 * C), BF),
            pltpu.VMEM((2, C, 9 * C), BF),
            pltpu.VMEM((27 * C, C), BF),
            pltpu.VMEM((2, CELLS, C), BF),
            pltpu.VMEM((2, CELLS, C), F32),
            pltpu.SemaphoreType.DMA((3,)),
        ],
        compiler_params=LARGE,
        cost_estimate=cost(2 * CELLS * 2304 * 256, 5 << 20),
        name="outer_back",
    )(core, near, far, weight, given, inner)


def planes_kernel(core_ref, vol, near, far, sems):
    core = core_ref[0]
    first = fetched(vol.at[core], far, sems.at[0])
    second = fetched(vol.at[1 - core], near, sems.at[1])
    first.wait()
    second.wait()


def both_planes(core, vol):
    plane = jax.ShapeDtypeStruct((CELLS, C), BF)
    return pl.pallas_call(
        planes_kernel,
        out_shape=[plane, plane],
        in_specs=[SMEM, HBM],
        out_specs=[HBM, HBM],
        scratch_shapes=[pltpu.SemaphoreType.DMA((2,))],
        compiler_params=SMALL,
        cost_estimate=cost(0, 2 << 20),
        name="both_planes",
    )(core, vol)


def first_rows_kernel(whole, out):
    out[...] = whole[0 : out.shape[0], :].astype(F32)


def first_rows(whole, rows):
    return pl.pallas_call(
        first_rows_kernel,
        out_shape=jax.ShapeDtypeStruct((rows, C), F32),
        in_specs=[VMEM],
        out_specs=VMEM,
        compiler_params=SMALL,
        cost_estimate=cost(0, 1 << 20),
        name="first_rows",
    )(whole)


def mix_kernel(got, later, out):
    for group in range(4):
        total = got[0, group].astype(F32)
        for k in range(1, 16):
            total += got[k, group].astype(F32)
        out[group] = total.astype(BF)
        out[4 + group] = total.astype(BF)


def mixed_rows(got, later):
    return pl.pallas_call(
        mix_kernel,
        out_shape=jax.ShapeDtypeStruct((8, CHUNK, C), BF),
        in_specs=[VMEM, SMEM],
        out_specs=VMEM,
        compiler_params=SMALL,
        cost_estimate=cost(1 << 18, 1 << 20),
        name="mixed_rows",
    )(got, later)


def step_kernel(at_ref, got, first, second, out):
    total = got[0].astype(F32)
    for k in range(1, 8):
        total += got[k].astype(F32)
    at = pl.multiple_of(at_ref[0], CHUNK)
    rows = pl.ds(at, CHUNK)
    step = adam(total, first[rows, :], second[rows, :])
    step = step.astype(BF)
    for k in range(OWNERS):
        out[k] = step


def spread_step(at, got, first, second):
    return pl.pallas_call(
        step_kernel,
        out_shape=jax.ShapeDtypeStruct((OWNERS, CHUNK, C), BF),
        in_specs=[SMEM] + [VMEM] * 3,
        out_specs=VMEM,
        compiler_params=SMALL,
        cost_estimate=cost(1 << 18, 1 << 20),
        name="spread_step",
    )(at, got, first, second)


def adam(grad, first, second):
    m_new = beta_one * first + (1.0 - beta_one) * grad
    v_new = beta_two * second + (1.0 - beta_two) * grad * grad
    return (
        m_new
        / (1.0 - beta_one**ADAM_STEP)
        / (jnp.sqrt(v_new / (1.0 - beta_two**ADAM_STEP)) + eps_adam)
    )


def from_neighbours(near, far):
    size = lax.axis_size(SPACE)
    pairs = [(i, i + 1) for i in range(1, size - 1, 2)]
    far_halo = lax.ppermute(far, SPACE, pairs + [(j, i) for i, j in pairs])
    near_halo = lax.ppermute(near, "core", [(0, 1), (1, 0)])
    return near_halo, far_halo


def body(volume, upstream, weight, first_moment, second_moment):
    vol = volume.reshape(2, CELLS, C)
    up = upstream.reshape(2, CELLS, C)
    core = lax.axis_index("core")
    at_core, at_near = core.reshape(1), (1 - core).reshape(1)
    near_halo, far_halo = from_neighbours(*both_planes(at_core, vol))
    inner, vol_t = inner_conv(vol, weight)
    near, ended = outer_conv(
        "near_conv", at_near, near_halo, weight, inner, up, at_core
    )
    far, ended = outer_conv(
        "far_conv", at_core, far_halo, weight, inner, up, ended
    )
    kept, sent = kernel_gradient(at_core, near, far, near_halo, far_halo, vol_t)

    rows = first_moment.shape[0]
    other = lax.ppermute(sent, "core", [(0, 1), (1, 0)])
    half = (kept + other.astype(F32)).astype(BF).reshape(16, 4, CHUNK, C)
    got = lax.all_to_all(half, ("x", "y"), 0, 0)
    grad_near, grad_far = from_neighbours(near, far)
    local, ended = inner_back(at_core, near, far, weight, half)
    part = mixed_rows(got, ended)
    got = lax.all_to_all(part, ("zl", "sample"), 0, 0)
    owner = core * 16 + lax.axis_index("x") * 4 + lax.axis_index("y")
    at = jnp.minimum(owner * CHUNK, rows - CHUNK).reshape(1)
    step = spread_step(at, got, first_moment, second_moment)
    whole = lax.all_to_all(step, ("core", "x", "y"), 0, 0)
    grad_volume = outer_back(at_core, grad_near, grad_far, weight, up, local)
    direction = first_rows(whole.reshape(OWNERS * CHUNK, C), rows)
    return (grad_volume.reshape(volume.shape), direction)


def solution(mesh):
    fine = Mesh(
        mesh.devices.reshape(4, 4, 2, 2, 4), ("x", "y", "zl", "core", "sample")
    )
    field = P("sample", SPACE, None, None, None)
    return jax.shard_map(
        body,
        mesh=fine,
        in_specs=(field, field, P(), P("sample", None), P("sample", None)),
        out_specs=(field, P("sample", None)),
        check_vma=False,
    )
```

```python
import functools
import jax
import jax.numpy as jnp
from jax import lax
from jax.experimental import pallas as pl
from jax.experimental.pallas import tpu as pltpu
from jax.sharding import Mesh, PartitionSpec as P

ADAM_STEP = 10


beta_one = 0.9
beta_two = 0.999
eps_adam = 1e-08

SPACE = ("x", "y", "zl", "core")
CHUNK = 32
OWNERS = 32
C = 128
COLS = 64
ROWS = 32
CELLS = ROWS * COLS
PADDED = CELLS + 2 * COLS
STRIP = 256
TILE = 512
BF = jnp.bfloat16
F32 = jnp.float32
VMEM = pl.BlockSpec(memory_space=pltpu.VMEM)
ANY = pl.BlockSpec(memory_space=pl.ANY)
HBM = pl.BlockSpec(memory_space=pltpu.HBM)
SMEM = pl.BlockSpec(memory_space=pltpu.SMEM)
WHOLE = pltpu.CompilerParams(vmem_limit_bytes=60 * 1024 * 1024)
LARGE = pltpu.CompilerParams(vmem_limit_bytes=62 * 1024 * 1024 + 512 * 1024)
SMALL = pltpu.CompilerParams(vmem_limit_bytes=4 * 1024 * 1024)
PARAMS = pltpu.CompilerParams(vmem_limit_bytes=32 * 1024 * 1024)


def cost(flops, moved, special=0):
    return pl.CostEstimate(flops=flops, bytes_accessed=moved, transcendentals=special)


def shifted_columns(planes, out, first, flip):
    width = 128 * len(planes)
    blank = jnp.zeros((COLS, width), BF)
    cols = slice(first, first + width)
    for c in range(3):
        out[c, 0:COLS, cols] = blank
        out[c, PADDED - COLS : PADDED, cols] = blank
    before, after = (2, 0) if flip else (0, 2)

    def strip(i, carry):
        at = pl.multiple_of(i * STRIP, STRIP)
        to = pl.ds(pl.multiple_of(at + COLS, COLS), STRIP)
        col = lax.broadcasted_iota(jnp.int32, (STRIP, C), 0) & (COLS - 1)
        for k, plane in enumerate(planes):
            cols = slice(first + k * C, first + (k + 1) * C)
            here = plane(pl.ds(at, STRIP))
            wide = here.astype(F32)
            out[1, to, cols] = here
            out[before, to, cols] = jnp.where(
                col == 0, 0.0, pltpu.roll(wide, 1, 0)
            ).astype(BF)
            out[after, to, cols] = jnp.where(
                col == COLS - 1, 0.0, pltpu.roll(wide, STRIP - 1, 0)
            ).astype(BF)
        return carry

    lax.fori_loop(0, CELLS // STRIP, strip, 0)


def transposed(plane, out, first):
    for at in range(0, CELLS, TILE):
        out[first : first + C, at : at + TILE] = jnp.transpose(
            plane(pl.ds(at, TILE))
        )


def rows_of(plane):
    return lambda rows: plane[rows, :]


def ordered(core, near, far):
    def pick(first, second):
        return lambda rows: jnp.where(core == 0, first[rows, :], second[rows, :])

    return pick(far, near), pick(near, far)


def fetched(source, held, sem):
    copy = pltpu.make_async_copy(source, held, sem)
    copy.start()
    return copy


def tap(a, b, c):
    return (a * 3 + b) * 3 + c


def taps_of(field, at, rows):
    return jnp.concatenate(
        [
            field[c, pl.ds(pl.multiple_of(at + b * COLS, COLS), rows), :]
            for b in range(3)
            for c in range(3)
        ],
        axis=1,
    )


def inner_kernel(vol, weight, out, vol_t, field, mixed, held, sem):
    copy = fetched(weight, held, sem)
    planes = [rows_of(vol.at[0]), rows_of(vol.at[1])]
    shifted_columns(planes, field, 0, False)
    copy.wait()
    for b in range(3):
        for c in range(3):
            base = (b * 3 + c) * 256
            for p in range(2):
                for z in range(2):
                    t = tap(1 + p - z, b, c)
                    mixed[base + p * C : base + (p + 1) * C, z * C : (z + 1) * C] = (
                        held[t * C : (t + 1) * C, :]
                    )

    def tile(i, carry):
        at = pl.multiple_of(i * TILE, TILE)
        got = jnp.dot(taps_of(field, at, TILE), mixed[...], preferred_element_type=F32)
        out[0, pl.ds(at, TILE), :] = got[:, 0:C]
        out[1, pl.ds(at, TILE), :] = got[:, C : 2 * C]
        return carry

    lax.fori_loop(0, CELLS // TILE, tile, 0)
    for p in range(2):
        transposed(planes[p], vol_t, p * C)


def inner_conv(vol, weight):
    return pl.pallas_call(
        inner_kernel,
        out_shape=[
            jax.ShapeDtypeStruct((2, CELLS, C), F32),
            jax.ShapeDtypeStruct((2 * C, CELLS), BF),
        ],
        in_specs=[VMEM, HBM],
        out_specs=[VMEM] * 2,
        scratch_shapes=[
            pltpu.VMEM((3, PADDED, 2 * C), BF),
            pltpu.VMEM((9 * 256, 2 * C), BF),
            pltpu.VMEM((27 * C, C), BF),
            pltpu.SemaphoreType.DMA,
        ],
        compiler_params=PARAMS,
        cost_estimate=cost(2 * CELLS * 2304 * 256, 5 << 20),
        name="inner_conv",
    )(vol, weight)


def side(z, halo, weight, inner, upstream, vol_t, grad, part, field, held, shifts, turned, sem):
    first = pl.multiple_of(z * 18 * C, 18 * C)
    copy = fetched(weight.at[pl.ds(first, 9 * C), :], held, sem)
    shifted_columns([rows_of(halo)], field, 0, False)
    transposed(rows_of(halo), turned, 0)
    blank = jnp.zeros((COLS, C), BF)
    for c in range(3):
        shifts[c, 0:COLS, :] = blank
        shifts[c, PADDED - COLS : PADDED, :] = blank
    copy.wait()

    def tile(i, carry):
        at = pl.multiple_of(i * TILE, TILE)
        rows = pl.ds(at, TILE)
        to = pl.ds(pl.multiple_of(at + COLS, COLS), TILE)
        preact = inner[z, rows, :] + jnp.dot(
            taps_of(field, at, TILE), held[...], preferred_element_type=F32
        )
        s = jax.nn.sigmoid(preact)
        slopes = s * (1.0 + preact * (1.0 - s))
        here = (upstream[z, rows, :].astype(F32) * slopes).astype(BF)
        grad[rows, :] = here
        wide = here.astype(F32)
        col = lax.broadcasted_iota(jnp.int32, (TILE, C), 0) & (COLS - 1)
        shifts[1, to, :] = here
        shifts[0, to, :] = jnp.where(col == 0, 0.0, pltpu.roll(wide, 1, 0)).astype(BF)
        shifts[2, to, :] = jnp.where(
            col == COLS - 1, 0.0, pltpu.roll(wide, TILE - 1, 0)
        ).astype(BF)
        return carry

    lax.fori_loop(0, CELLS // TILE, tile, 0)

    lhs = jnp.concatenate([vol_t[...], turned[...]], axis=0)
    offset_of = (1 - z, 2 - z, 2 * z)
    couples = [((b, 0), (b, 1)) for b in range(3)] + [((0, 2), (1, 2)), ((2, 2),)]
    for couple in couples:
        rhs = jnp.concatenate(
            [
                shifts[2 - c, (2 - b) * COLS : (2 - b) * COLS + CELLS, :]
                for b, c in couple
            ],
            axis=1,
        )
        got = jnp.dot(lhs, rhs, preferred_element_type=F32)
        for k, (b, c) in enumerate(couple):
            for p in range(3):
                for i in range(4):
                    chunk = 4 * tap(offset_of[p], b, c) + i
                    at = p * C + i * CHUNK
                    part[chunk + 5 * (chunk // 27)] = got[
                        at : at + CHUNK, k * C : (k + 1) * C
                    ]


def near_kernel(
    core_ref, halo, weight, inner, upstream, vol_t, grad, part, *scratch
):
    side(
        1 - core_ref[0], halo, weight, inner, upstream, vol_t, grad, part, *scratch
    )
    for owner in range(27, 32):
        for group in range(4):
            part[group * 32 + owner] = jnp.zeros((CHUNK, C), F32)


def far_kernel(
    core_ref, halo, weight, inner, upstream, vol_t, near, grad, kept, sent, part, *scratch
):
    core = core_ref[0]
    side(core, halo, weight, inner, upstream, vol_t, grad, part, *scratch)
    for owner in range(27, 32):
        for group in range(4):
            part[group * 32 + owner] = jnp.zeros((CHUNK, C), F32)

    def share(owner, carry):
        for group in range(4):
            mine = group * 32 + core * 16 + owner
            other = group * 32 + (1 - core) * 16 + owner
            kept[owner * 4 + group] = part[mine] + near[mine]
            sent[owner * 4 + group] = (part[other] + near[other]).astype(BF)
        return carry

    lax.fori_loop(0, 16, share, 0)


PLANE = jax.ShapeDtypeStruct((CELLS, C), BF)
PART = (4 * 32, CHUNK, C)
SIDE = [
    pltpu.VMEM((3, PADDED, C), BF),
    pltpu.VMEM((9 * C, C), BF),
    pltpu.VMEM((3, PADDED, C), BF),
    pltpu.VMEM((C, CELLS), BF),
    pltpu.SemaphoreType.DMA,
]


def near_side(core, halo, weight, inner, upstream, vol_t):
    return pl.pallas_call(
        near_kernel,
        out_shape=[PLANE, jax.ShapeDtypeStruct(PART, F32)],
        in_specs=[SMEM, VMEM, HBM, VMEM, VMEM, VMEM],
        out_specs=[VMEM, VMEM],
        scratch_shapes=SIDE,
        compiler_params=PARAMS,
        cost_estimate=cost(2 * CELLS * 3456 * 256, 5 << 20, CELLS * 128),
        name="near_side",
    )(core, halo, weight, inner, upstream, vol_t)


def far_side(core, halo, weight, inner, upstream, vol_t, near):
    return pl.pallas_call(
        far_kernel,
        out_shape=[
            PLANE,
            jax.ShapeDtypeStruct((64, CHUNK, C), F32),
            jax.ShapeDtypeStruct((64, CHUNK, C), BF),
        ],
        in_specs=[SMEM, VMEM, HBM, VMEM, VMEM, VMEM, VMEM],
        out_specs=[VMEM] * 3,
        scratch_shapes=[pltpu.VMEM(PART, F32)] + SIDE,
        compiler_params=PARAMS,
        cost_estimate=cost(2 * CELLS * 3456 * 256, 5 << 20, CELLS * 128),
        name="far_side",
    )(core, halo, weight, inner, upstream, vol_t, near)


def inner_back_kernel(
    core_ref, near, far, weight, later, out, field, mixed, held, made, sem, sems
):
    copy = fetched(weight, held, sem)
    shifted_columns(ordered(core_ref[0], near, far), field, 0, False)
    copy.wait()
    for b in range(3):
        for c in range(3):
            base = (b * 3 + c) * 256
            for p in range(2):
                for z in range(2):
                    t = tap(1 + z - p, 2 - b, 2 - c)
                    mixed[z * C : (z + 1) * C, base + p * C : base + (p + 1) * C] = (
                        held[t * C : (t + 1) * C, :]
                    )
    tiles = CELLS // TILE

    def leave(i, z):
        rows = pl.ds(pl.multiple_of(i * TILE, TILE), TILE)
        return pltpu.make_async_copy(
            made.at[z, rows, :], out.at[z, rows, :], sems.at[i, z]
        )

    def tile(i, carry):
        at = pl.multiple_of(i * TILE, TILE)
        got = lax.dot_general(
            taps_of(field, at, TILE),
            mixed[...],
            (((1,), (1,)), ((), ())),
            preferred_element_type=F32,
        )
        for z in range(2):
            made[z, pl.ds(at, TILE), :] = got[:, z * C : (z + 1) * C]
            leave(i, z).start()
        return carry

    lax.fori_loop(0, tiles, tile, 0)
    for i in range(tiles):
        for z in range(2):
            leave(i, z).wait()


def inner_back(core, near, far, weight, later):
    return pl.pallas_call(
        inner_back_kernel,
        out_shape=jax.ShapeDtypeStruct((2, CELLS, C), F32),
        in_specs=[SMEM, VMEM, VMEM, HBM, ANY],
        out_specs=HBM,
        scratch_shapes=[
            pltpu.VMEM((3, PADDED, 2 * C), BF),
            pltpu.VMEM((2 * C, 9 * 256), BF),
            pltpu.VMEM((27 * C, C), BF),
            pltpu.VMEM((2, CELLS, C), F32),
            pltpu.SemaphoreType.DMA,
            pltpu.SemaphoreType.DMA((CELLS // TILE, 2)),
        ],
        compiler_params=WHOLE,
        cost_estimate=cost(2 * CELLS * 2304 * 256, 5 << 20),
        name="inner_back",
    )(core, near, far, weight, later)


def outer_back_kernel(
    core_ref, near, far, weight, given, kept, out, field, mixed, held, upstream, inner, sems
):
    copy = fetched(weight, held, sems.at[0])
    kept_copy = fetched(kept, inner, sems.at[1])
    given_copy = fetched(given, upstream, sems.at[2])
    core = core_ref[0]
    shifted_columns([rows_of(near), rows_of(far)], field, 0, False)
    copy.wait()
    for k in range(2):
        z = 1 - core if k == 0 else core
        first = pl.multiple_of((2 - 2 * z) * 9 * C, C)
        for b in range(3):
            for c in range(3):
                base = (b * 3 + c) * C
                mixed[k, :, base : base + C] = held[
                    pl.ds(first + tap(0, 2 - b, 2 - c) * C, C), :
                ]
    kept_copy.wait()
    given_copy.wait()

    def tile(i, carry):
        at = pl.multiple_of(i * TILE, TILE)
        rows = pl.ds(at, TILE)
        for k in range(2):
            z = 1 - core if k == 0 else core
            lhs = jnp.concatenate(
                [
                    field[
                        c,
                        pl.ds(pl.multiple_of(at + b * COLS, COLS), TILE),
                        k * C : (k + 1) * C,
                    ]
                    for b in range(3)
                    for c in range(3)
                ],
                axis=1,
            )
            got = lax.dot_general(
                lhs, mixed[k], (((1,), (1,)), ((), ())), preferred_element_type=F32
            )
            out[z, rows, :] = (
                upstream[z, rows, :].astype(F32) + (inner[z, rows, :] + got)
            ).astype(BF)
        return carry

    lax.fori_loop(0, CELLS // TILE, tile, 0)


def outer_back(core, near, far, weight, given, inner):
    return pl.pallas_call(
        outer_back_kernel,
        out_shape=jax.ShapeDtypeStruct((2, CELLS, C), BF),
        in_specs=[SMEM, VMEM, VMEM, HBM, HBM, HBM],
        out_specs=VMEM,
        scratch_shapes=[
            pltpu.VMEM((3, PADDED, 2 * C), BF),
            pltpu.VMEM((2, C, 9 * C), BF),
            pltpu.VMEM((27 * C, C), BF),
            pltpu.VMEM((2, CELLS, C), BF),
            pltpu.VMEM((2, CELLS, C), F32),
            pltpu.SemaphoreType.DMA((3,)),
        ],
        compiler_params=LARGE,
        cost_estimate=cost(2 * CELLS * 2304 * 256, 5 << 20),
        name="outer_back",
    )(core, near, far, weight, given, inner)


def planes_kernel(core_ref, vol, near, far):
    core = core_ref[0]
    far[...] = vol[core]
    near[...] = vol[1 - core]


def both_planes(core, vol):
    plane = jax.ShapeDtypeStruct((CELLS, C), BF)
    return pl.pallas_call(
        planes_kernel,
        out_shape=[plane, plane],
        in_specs=[SMEM, VMEM],
        out_specs=[VMEM, VMEM],
        compiler_params=SMALL,
        cost_estimate=cost(0, 2 << 20),
        name="both_planes",
    )(core, vol)


def first_rows_kernel(whole, out):
    out[...] = whole[0 : out.shape[0], :].astype(F32)


def first_rows(whole, rows):
    return pl.pallas_call(
        first_rows_kernel,
        out_shape=jax.ShapeDtypeStruct((rows, C), F32),
        in_specs=[VMEM],
        out_specs=VMEM,
        compiler_params=SMALL,
        cost_estimate=cost(0, 1 << 20),
        name="first_rows",
    )(whole)


def mix_kernel(got, later, out):
    for group in range(4):
        total = got[0, group].astype(F32)
        for k in range(1, 16):
            total += got[k, group].astype(F32)
        out[group] = total.astype(BF)
        out[4 + group] = total.astype(BF)


def mixed_rows(got, later):
    return pl.pallas_call(
        mix_kernel,
        out_shape=jax.ShapeDtypeStruct((8, CHUNK, C), BF),
        in_specs=[VMEM, ANY],
        out_specs=VMEM,
        compiler_params=LARGE,
        cost_estimate=cost(1 << 18, 1 << 20),
        name="mixed_rows",
    )(got, later)


def step_kernel(at_ref, got, first, second, out):
    total = got[0].astype(F32)
    for k in range(1, 8):
        total += got[k].astype(F32)
    at = pl.multiple_of(at_ref[0], CHUNK)
    rows = pl.ds(at, CHUNK)
    step = adam(total, first[rows, :], second[rows, :])
    step = step.astype(BF)
    for k in range(OWNERS):
        out[k] = step


def spread_step(at, got, first, second):
    return pl.pallas_call(
        step_kernel,
        out_shape=jax.ShapeDtypeStruct((OWNERS, CHUNK, C), BF),
        in_specs=[SMEM] + [VMEM] * 3,
        out_specs=VMEM,
        compiler_params=SMALL,
        cost_estimate=cost(1 << 18, 1 << 20),
        name="spread_step",
    )(at, got, first, second)


def adam(grad, first, second):
    m_new = beta_one * first + (1.0 - beta_one) * grad
    v_new = beta_two * second + (1.0 - beta_two) * grad * grad
    return (
        m_new
        / (1.0 - beta_one**ADAM_STEP)
        / (jnp.sqrt(v_new / (1.0 - beta_two**ADAM_STEP)) + eps_adam)
    )


def from_neighbours(near, far):
    size = lax.axis_size(SPACE)
    pairs = [(i, i + 1) for i in range(1, size - 1, 2)]
    far_halo = lax.ppermute(far, SPACE, pairs + [(j, i) for i, j in pairs])
    near_halo = lax.ppermute(near, "core", [(0, 1), (1, 0)])
    return near_halo, far_halo


def body(volume, upstream, weight, first_moment, second_moment):
    vol = volume.reshape(2, CELLS, C)
    up = upstream.reshape(2, CELLS, C)
    core = lax.axis_index("core")
    at_core = core.reshape(1)
    near_halo, far_halo = from_neighbours(*both_planes(at_core, vol))
    inner, vol_t = inner_conv(vol, weight)
    near, part = near_side(at_core, near_halo, weight, inner, up, vol_t)
    far, kept, sent = far_side(at_core, far_halo, weight, inner, up, vol_t, part)

    rows = first_moment.shape[0]
    other = lax.ppermute(sent, "core", [(0, 1), (1, 0)])
    half = (kept + other.astype(F32)).astype(BF).reshape(16, 4, CHUNK, C)
    got = lax.all_to_all(half, ("x", "y"), 0, 0)
    grad_near, grad_far = from_neighbours(near, far)
    local = inner_back(at_core, near, far, weight, half)
    part = mixed_rows(got, local)
    got = lax.all_to_all(part, ("zl", "sample"), 0, 0)
    owner = core * 16 + lax.axis_index("x") * 4 + lax.axis_index("y")
    at = jnp.minimum(owner * CHUNK, rows - CHUNK).reshape(1)
    step = spread_step(at, got, first_moment, second_moment)
    whole = lax.all_to_all(step, ("core", "x", "y"), 0, 0)
    grad_volume = outer_back(at_core, grad_near, grad_far, weight, up, local)
    direction = first_rows(whole.reshape(OWNERS * CHUNK, C), rows)
    return (grad_volume.reshape(volume.shape), direction)


def solution(mesh):
    fine = Mesh(
        mesh.devices.reshape(4, 4, 2, 2, 4), ("x", "y", "zl", "core", "sample")
    )
    field = P("sample", SPACE, None, None, None)
    return jax.shard_map(
        body,
        mesh=fine,
        in_specs=(field, field, P(), P("sample", None), P("sample", None)),
        out_specs=(field, P("sample", None)),
        check_vma=False,
    )
```

```python
import functools
import jax
import jax.numpy as jnp
from jax import lax
from jax.experimental import pallas as pl
from jax.experimental.pallas import tpu as pltpu
from jax.sharding import Mesh, PartitionSpec as P

ADAM_STEP = 10


beta_one = 0.9
beta_two = 0.999
eps_adam = 1e-08

SPACE = ("x", "y", "zl", "core")
CHUNK = 32
OWNERS = 32
C = 128
COLS = 64
ROWS = 32
CELLS = ROWS * COLS
PADDED = CELLS + 2 * COLS
STRIP = 256
TILE = 512
BF = jnp.bfloat16
F32 = jnp.float32
VMEM = pl.BlockSpec(memory_space=pltpu.VMEM)
ANY = pl.BlockSpec(memory_space=pl.ANY)
HBM = pl.BlockSpec(memory_space=pltpu.HBM)
SMEM = pl.BlockSpec(memory_space=pltpu.SMEM)
WHOLE = pltpu.CompilerParams(vmem_limit_bytes=60 * 1024 * 1024)
LARGE = pltpu.CompilerParams(vmem_limit_bytes=62 * 1024 * 1024 + 512 * 1024)
SMALL = pltpu.CompilerParams(vmem_limit_bytes=4 * 1024 * 1024)
PARAMS = pltpu.CompilerParams(vmem_limit_bytes=32 * 1024 * 1024)


def cost(flops, moved, special=0):
    return pl.CostEstimate(flops=flops, bytes_accessed=moved, transcendentals=special)


def shifted_columns(planes, out, first, flip):
    width = 128 * len(planes)
    blank = jnp.zeros((COLS, width), BF)
    cols = slice(first, first + width)
    for c in range(3):
        out[c, 0:COLS, cols] = blank
        out[c, PADDED - COLS : PADDED, cols] = blank
    before, after = (2, 0) if flip else (0, 2)

    def strip(i, carry):
        at = pl.multiple_of(i * STRIP, STRIP)
        to = pl.ds(pl.multiple_of(at + COLS, COLS), STRIP)
        col = lax.broadcasted_iota(jnp.int32, (STRIP, C), 0) & (COLS - 1)
        for k, plane in enumerate(planes):
            cols = slice(first + k * C, first + (k + 1) * C)
            here = plane(pl.ds(at, STRIP))
            wide = here.astype(F32)
            out[1, to, cols] = here
            out[before, to, cols] = jnp.where(
                col == 0, 0.0, pltpu.roll(wide, 1, 0)
            ).astype(BF)
            out[after, to, cols] = jnp.where(
                col == COLS - 1, 0.0, pltpu.roll(wide, STRIP - 1, 0)
            ).astype(BF)
        return carry

    lax.fori_loop(0, CELLS // STRIP, strip, 0)


def transposed(plane, out, first):
    for at in range(0, CELLS, TILE):
        out[first : first + C, at : at + TILE] = jnp.transpose(
            plane(pl.ds(at, TILE))
        )


def rows_of(plane):
    return lambda rows: plane[rows, :]


def ordered(core, near, far):
    def pick(first, second):
        return lambda rows: jnp.where(core == 0, first[rows, :], second[rows, :])

    return pick(far, near), pick(near, far)


def fetched(source, held, sem):
    copy = pltpu.make_async_copy(source, held, sem)
    copy.start()
    return copy


def tap(a, b, c):
    return (a * 3 + b) * 3 + c


def taps_of(field, at, rows):
    return jnp.concatenate(
        [
            field[c, pl.ds(pl.multiple_of(at + b * COLS, COLS), rows), :]
            for b in range(3)
            for c in range(3)
        ],
        axis=1,
    )


def inner_kernel(vol, weight, out, vol_t, field, mixed, held, sem):
    copy = fetched(weight, held, sem)
    planes = [rows_of(vol.at[0]), rows_of(vol.at[1])]
    shifted_columns(planes, field, 0, False)
    copy.wait()
    for b in range(3):
        for c in range(3):
            base = (b * 3 + c) * 256
            for p in range(2):
                for z in range(2):
                    t = tap(1 + p - z, b, c)
                    mixed[base + p * C : base + (p + 1) * C, z * C : (z + 1) * C] = (
                        held[t * C : (t + 1) * C, :]
                    )

    def tile(i, carry):
        at = pl.multiple_of(i * TILE, TILE)
        got = jnp.dot(taps_of(field, at, TILE), mixed[...], preferred_element_type=F32)
        out[0, pl.ds(at, TILE), :] = got[:, 0:C]
        out[1, pl.ds(at, TILE), :] = got[:, C : 2 * C]
        return carry

    lax.fori_loop(0, CELLS // TILE, tile, 0)
    for p in range(2):
        transposed(planes[p], vol_t, p * C)


def inner_conv(vol, weight):
    return pl.pallas_call(
        inner_kernel,
        out_shape=[
            jax.ShapeDtypeStruct((2, CELLS, C), F32),
            jax.ShapeDtypeStruct((2 * C, CELLS), BF),
        ],
        in_specs=[VMEM, HBM],
        out_specs=[VMEM] * 2,
        scratch_shapes=[
            pltpu.VMEM((3, PADDED, 2 * C), BF),
            pltpu.VMEM((9 * 256, 2 * C), BF),
            pltpu.VMEM((27 * C, C), BF),
            pltpu.SemaphoreType.DMA,
        ],
        compiler_params=PARAMS,
        cost_estimate=cost(2 * CELLS * 2304 * 256, 5 << 20),
        name="inner_conv",
    )(vol, weight)


def side(z, halo, weight, inner, upstream, vol_t, grad, part, field, held, shifts, turned, sem):
    first = pl.multiple_of(z * 18 * C, 18 * C)
    copy = fetched(weight.at[pl.ds(first, 9 * C), :], held, sem)
    shifted_columns([rows_of(halo)], field, 0, False)
    transposed(rows_of(halo), turned, 0)
    blank = jnp.zeros((COLS, C), BF)
    for c in range(3):
        shifts[c, 0:COLS, :] = blank
        shifts[c, PADDED - COLS : PADDED, :] = blank
    copy.wait()

    def tile(i, carry):
        at = pl.multiple_of(i * TILE, TILE)
        rows = pl.ds(at, TILE)
        to = pl.ds(pl.multiple_of(at + COLS, COLS), TILE)
        preact = inner[z, rows, :] + jnp.dot(
            taps_of(field, at, TILE), held[...], preferred_element_type=F32
        )
        s = jax.nn.sigmoid(preact)
        slopes = s * (1.0 + preact * (1.0 - s))
        here = (upstream[z, rows, :].astype(F32) * slopes).astype(BF)
        grad[rows, :] = here
        wide = here.astype(F32)
        col = lax.broadcasted_iota(jnp.int32, (TILE, C), 0) & (COLS - 1)
        shifts[1, to, :] = here
        shifts[0, to, :] = jnp.where(col == 0, 0.0, pltpu.roll(wide, 1, 0)).astype(BF)
        shifts[2, to, :] = jnp.where(
            col == COLS - 1, 0.0, pltpu.roll(wide, TILE - 1, 0)
        ).astype(BF)
        return carry

    lax.fori_loop(0, CELLS // TILE, tile, 0)

    lhs = jnp.concatenate([vol_t[...], turned[...]], axis=0)
    offset_of = (1 - z, 2 - z, 2 * z)
    couples = [((b, 0), (b, 1)) for b in range(3)] + [((0, 2), (1, 2)), ((2, 2),)]
    for couple in couples:
        rhs = jnp.concatenate(
            [
                shifts[2 - c, (2 - b) * COLS : (2 - b) * COLS + CELLS, :]
                for b, c in couple
            ],
            axis=1,
        )
        got = jnp.dot(lhs, rhs, preferred_element_type=F32)
        for k, (b, c) in enumerate(couple):
            for p in range(3):
                for i in range(4):
                    chunk = 4 * tap(offset_of[p], b, c) + i
                    at = p * C + i * CHUNK
                    part[chunk + 5 * (chunk // 27)] = got[
                        at : at + CHUNK, k * C : (k + 1) * C
                    ]


def near_kernel(
    core_ref, halo, weight, inner, upstream, vol_t, grad, part, *scratch
):
    side(
        1 - core_ref[0], halo, weight, inner, upstream, vol_t, grad, part, *scratch
    )
    for owner in range(27, 32):
        for group in range(4):
            part[group * 32 + owner] = jnp.zeros((CHUNK, C), F32)


def far_kernel(
    core_ref, halo, weight, inner, upstream, vol_t, near, grad, kept, sent, part, *scratch
):
    core = core_ref[0]
    side(core, halo, weight, inner, upstream, vol_t, grad, part, *scratch)
    for owner in range(27, 32):
        for group in range(4):
            part[group * 32 + owner] = jnp.zeros((CHUNK, C), F32)

    def share(owner, carry):
        for group in range(4):
            mine = group * 32 + core * 16 + owner
            other = group * 32 + (1 - core) * 16 + owner
            kept[owner * 4 + group] = part[mine] + near[mine]
            sent[owner * 4 + group] = (part[other] + near[other]).astype(BF)
        return carry

    lax.fori_loop(0, 16, share, 0)


PLANE = jax.ShapeDtypeStruct((CELLS, C), BF)
PART = (4 * 32, CHUNK, C)
SIDE = [
    pltpu.VMEM((3, PADDED, C), BF),
    pltpu.VMEM((9 * C, C), BF),
    pltpu.VMEM((3, PADDED, C), BF),
    pltpu.VMEM((C, CELLS), BF),
    pltpu.SemaphoreType.DMA,
]


def near_side(core, halo, weight, inner, upstream, vol_t):
    return pl.pallas_call(
        near_kernel,
        out_shape=[PLANE, jax.ShapeDtypeStruct(PART, F32)],
        in_specs=[SMEM, VMEM, HBM, VMEM, VMEM, VMEM],
        out_specs=[VMEM, VMEM],
        scratch_shapes=SIDE,
        compiler_params=PARAMS,
        cost_estimate=cost(2 * CELLS * 3456 * 256, 5 << 20, CELLS * 128),
        name="near_side",
    )(core, halo, weight, inner, upstream, vol_t)


def far_side(core, halo, weight, inner, upstream, vol_t, near):
    return pl.pallas_call(
        far_kernel,
        out_shape=[
            PLANE,
            jax.ShapeDtypeStruct((64, CHUNK, C), F32),
            jax.ShapeDtypeStruct((64, CHUNK, C), BF),
        ],
        in_specs=[SMEM, VMEM, HBM, VMEM, VMEM, VMEM, VMEM],
        out_specs=[VMEM] * 3,
        scratch_shapes=[pltpu.VMEM(PART, F32)] + SIDE,
        compiler_params=PARAMS,
        cost_estimate=cost(2 * CELLS * 3456 * 256, 5 << 20, CELLS * 128),
        name="far_side",
    )(core, halo, weight, inner, upstream, vol_t, near)


def inner_back_kernel(
    core_ref, near, far, weight, later, out, field, mixed, held, made, sem, sems
):
    copy = fetched(weight, held, sem)
    shifted_columns(ordered(core_ref[0], near, far), field, 0, False)
    copy.wait()
    for b in range(3):
        for c in range(3):
            base = (b * 3 + c) * 256
            for p in range(2):
                for z in range(2):
                    t = tap(1 + z - p, 2 - b, 2 - c)
                    mixed[z * C : (z + 1) * C, base + p * C : base + (p + 1) * C] = (
                        held[t * C : (t + 1) * C, :]
                    )
    tiles = CELLS // TILE

    def leave(i, z):
        rows = pl.ds(pl.multiple_of(i * TILE, TILE), TILE)
        return pltpu.make_async_copy(
            made.at[z, rows, :], out.at[z, rows, :], sems.at[i, z]
        )

    def tile(i, carry):
        at = pl.multiple_of(i * TILE, TILE)
        got = lax.dot_general(
            taps_of(field, at, TILE),
            mixed[...],
            (((1,), (1,)), ((), ())),
            preferred_element_type=F32,
        )
        for z in range(2):
            made[z, pl.ds(at, TILE), :] = got[:, z * C : (z + 1) * C]
            leave(i, z).start()
        return carry

    lax.fori_loop(0, tiles, tile, 0)
    for i in range(tiles):
        for z in range(2):
            leave(i, z).wait()


def inner_back(core, near, far, weight, later):
    return pl.pallas_call(
        inner_back_kernel,
        out_shape=jax.ShapeDtypeStruct((2, CELLS, C), F32),
        in_specs=[SMEM, VMEM, VMEM, HBM, ANY],
        out_specs=HBM,
        scratch_shapes=[
            pltpu.VMEM((3, PADDED, 2 * C), BF),
            pltpu.VMEM((2 * C, 9 * 256), BF),
            pltpu.VMEM((27 * C, C), BF),
            pltpu.VMEM((2, CELLS, C), F32),
            pltpu.SemaphoreType.DMA,
            pltpu.SemaphoreType.DMA((CELLS // TILE, 2)),
        ],
        compiler_params=WHOLE,
        cost_estimate=cost(2 * CELLS * 2304 * 256, 5 << 20),
        name="inner_back",
    )(core, near, far, weight, later)


def outer_back_kernel(at_ref, halo, weight, given, kept, *rest):
    out, field, mixed, held, upstream, inner, made, sems, leave_sems = rest[-9:]
    z = at_ref[0]
    first = pl.multiple_of((2 - 2 * z) * 9 * C, 9 * C)
    copy = fetched(weight.at[pl.ds(first, 9 * C), :], held, sems.at[0])
    kept_copy = fetched(kept.at[z], inner, sems.at[1])
    given_copy = fetched(given.at[z], upstream, sems.at[2])
    shifted_columns([rows_of(halo)], field, 0, False)
    copy.wait()
    for b in range(3):
        for c in range(3):
            base = (b * 3 + c) * C
            t = tap(0, 2 - b, 2 - c)
            mixed[:, base : base + C] = held[t * C : (t + 1) * C, :]
    kept_copy.wait()
    given_copy.wait()
    tiles = CELLS // TILE

    def leave(i):
        rows = pl.ds(pl.multiple_of(i * TILE, TILE), TILE)
        return pltpu.make_async_copy(
            made.at[rows, :], out.at[z, rows, :], leave_sems.at[i]
        )

    def tile(i, carry):
        at = pl.multiple_of(i * TILE, TILE)
        rows = pl.ds(at, TILE)
        got = lax.dot_general(
            taps_of(field, at, TILE),
            mixed[...],
            (((1,), (1,)), ((), ())),
            preferred_element_type=F32,
        )
        made[rows, :] = (
            upstream[rows, :].astype(F32) + (inner[rows, :] + got)
        ).astype(BF)
        leave(i).start()
        return carry

    lax.fori_loop(0, tiles, tile, 0)
    for i in range(tiles):
        leave(i).wait()


def outer_back(name, z, halo, weight, given, inner, *begun):
    return pl.pallas_call(
        outer_back_kernel,
        out_shape=jax.ShapeDtypeStruct((2, CELLS, C), BF),
        in_specs=[SMEM, VMEM] + [HBM] * (3 + len(begun)),
        out_specs=HBM,
        scratch_shapes=[
            pltpu.VMEM((3, PADDED, C), BF),
            pltpu.VMEM((C, 9 * C), BF),
            pltpu.VMEM((9 * C, C), BF),
            pltpu.VMEM((CELLS, C), BF),
            pltpu.VMEM((CELLS, C), F32),
            pltpu.VMEM((CELLS, C), BF),
            pltpu.SemaphoreType.DMA((3,)),
            pltpu.SemaphoreType.DMA((CELLS // TILE,)),
        ],
        input_output_aliases={5: 0} if begun else {},
        compiler_params=LARGE,
        cost_estimate=cost(CELLS * 2304 * 256, 3 << 20),
        name=name,
    )(z, halo, weight, given, inner, *begun)


def planes_kernel(core_ref, vol, near, far):
    core = core_ref[0]
    far[...] = vol[core]
    near[...] = vol[1 - core]


def both_planes(core, vol):
    plane = jax.ShapeDtypeStruct((CELLS, C), BF)
    return pl.pallas_call(
        planes_kernel,
        out_shape=[plane, plane],
        in_specs=[SMEM, VMEM],
        out_specs=[VMEM, VMEM],
        compiler_params=SMALL,
        cost_estimate=cost(0, 2 << 20),
        name="both_planes",
    )(core, vol)


def first_rows_kernel(whole, out, wide, sems):
    rows = out.shape[0]
    step = rows // 4
    copies = []
    for k in range(4):
        part = slice(k * step, (k + 1) * step)
        wide[part, :] = whole[part, :].astype(F32)
        copy = pltpu.make_async_copy(wide.at[part, :], out.at[part, :], sems.at[k])
        copy.start()
        copies.append(copy)
    for copy in copies:
        copy.wait()


def first_rows(whole, rows):
    return pl.pallas_call(
        first_rows_kernel,
        out_shape=jax.ShapeDtypeStruct((rows, C), F32),
        in_specs=[VMEM],
        out_specs=ANY,
        scratch_shapes=[pltpu.VMEM((rows, C), F32), pltpu.SemaphoreType.DMA((4,))],
        compiler_params=SMALL,
        cost_estimate=cost(0, 1 << 20),
        name="first_rows",
    )(whole)


def mix_kernel(got, out):
    for group in range(4):
        total = got[0, group].astype(F32)
        for k in range(1, 16):
            total += got[k, group].astype(F32)
        out[group] = total.astype(BF)
        out[4 + group] = total.astype(BF)


def mixed_rows(got):
    return pl.pallas_call(
        mix_kernel,
        out_shape=jax.ShapeDtypeStruct((8, CHUNK, C), BF),
        in_specs=[VMEM],
        out_specs=VMEM,
        compiler_params=SMALL,
        cost_estimate=cost(1 << 18, 1 << 20),
        name="mixed_rows",
    )(got)


def step_kernel(at_ref, got, first, second, out):
    total = got[0].astype(F32)
    for k in range(1, 8):
        total += got[k].astype(F32)
    at = pl.multiple_of(at_ref[0], CHUNK)
    rows = pl.ds(at, CHUNK)
    step = adam(total, first[rows, :], second[rows, :])
    step = step.astype(BF)
    for k in range(OWNERS):
        out[k] = step


def spread_step(at, got, first, second):
    return pl.pallas_call(
        step_kernel,
        out_shape=jax.ShapeDtypeStruct((OWNERS, CHUNK, C), BF),
        in_specs=[SMEM] + [VMEM] * 3,
        out_specs=VMEM,
        compiler_params=SMALL,
        cost_estimate=cost(1 << 18, 1 << 20),
        name="spread_step",
    )(at, got, first, second)


def adam(grad, first, second):
    m_new = beta_one * first + (1.0 - beta_one) * grad
    v_new = beta_two * second + (1.0 - beta_two) * grad * grad
    return (
        m_new
        / (1.0 - beta_one**ADAM_STEP)
        / (jnp.sqrt(v_new / (1.0 - beta_two**ADAM_STEP)) + eps_adam)
    )


def from_neighbours(near, far):
    size = lax.axis_size(SPACE)
    pairs = [(i, i + 1) for i in range(1, size - 1, 2)]
    far_halo = lax.ppermute(far, SPACE, pairs + [(j, i) for i, j in pairs])
    near_halo = lax.ppermute(near, "core", [(0, 1), (1, 0)])
    return near_halo, far_halo


def body(volume, upstream, weight, first_moment, second_moment):
    vol = volume.reshape(2, CELLS, C)
    up = upstream.reshape(2, CELLS, C)
    core = lax.axis_index("core")
    at_core = core.reshape(1)
    near_halo, far_halo = from_neighbours(*both_planes(at_core, vol))
    inner, vol_t = inner_conv(vol, weight)
    near, part = near_side(at_core, near_halo, weight, inner, up, vol_t)
    far, kept, sent = far_side(at_core, far_halo, weight, inner, up, vol_t, part)

    rows = first_moment.shape[0]
    other = lax.ppermute(sent, "core", [(0, 1), (1, 0)])
    half = (kept + other.astype(F32)).astype(BF).reshape(16, 4, CHUNK, C)
    near_sent, half = lax.optimization_barrier((near, half))
    got = lax.all_to_all(half, ("x", "y"), 0, 0)
    grad_near, grad_far = from_neighbours(near_sent, far)
    local = inner_back(at_core, near, far, weight, half)
    got, local = lax.optimization_barrier((got, local))
    part = mixed_rows(got)
    grad_near, part = lax.optimization_barrier((grad_near, part))
    got = lax.all_to_all(part, ("zl", "sample"), 0, 0)
    half_done = outer_back("near_back", 1 - at_core, grad_near, weight, up, local)
    got, half_done = lax.optimization_barrier((got, half_done))
    owner = core * 16 + lax.axis_index("x") * 4 + lax.axis_index("y")
    at = jnp.minimum(owner * CHUNK, rows - CHUNK).reshape(1)
    step = spread_step(at, got, first_moment, second_moment)
    whole = lax.all_to_all(step, ("core", "x", "y"), 0, 0)
    grad_volume = outer_back(
        "far_back", at_core, grad_far, weight, up, local, half_done
    )
    direction = first_rows(whole.reshape(OWNERS * CHUNK, C), rows)
    return (grad_volume.reshape(volume.shape), direction)


def solution(mesh):
    fine = Mesh(
        mesh.devices.reshape(4, 4, 2, 2, 4), ("x", "y", "zl", "core", "sample")
    )
    field = P("sample", SPACE, None, None, None)
    return jax.shard_map(
        body,
        mesh=fine,
        in_specs=(field, field, P(), P("sample", None), P("sample", None)),
        out_specs=(field, P("sample", None)),
        check_vma=False,
    )
```

```python
import functools
import jax
import jax.numpy as jnp
from jax import lax
from jax.experimental import pallas as pl
from jax.experimental.pallas import tpu as pltpu
from jax.sharding import Mesh, PartitionSpec as P

ADAM_STEP = 10


beta_one = 0.9
beta_two = 0.999
eps_adam = 1e-08

SPACE = ("x", "y", "zl", "core")
CHUNK = 32
OWNERS = 32
C = 128
COLS = 64
ROWS = 32
CELLS = ROWS * COLS
PADDED = CELLS + 2 * COLS
STRIP = 256
TILE = 512
BF = jnp.bfloat16
F32 = jnp.float32
VMEM = pl.BlockSpec(memory_space=pltpu.VMEM)
ANY = pl.BlockSpec(memory_space=pl.ANY)
HBM = pl.BlockSpec(memory_space=pltpu.HBM)
SMEM = pl.BlockSpec(memory_space=pltpu.SMEM)
WHOLE = pltpu.CompilerParams(vmem_limit_bytes=60 * 1024 * 1024)
LARGE = pltpu.CompilerParams(vmem_limit_bytes=62 * 1024 * 1024 + 512 * 1024)
INNER = pltpu.CompilerParams(vmem_limit_bytes=44 * 1024 * 1024)
SMALL = pltpu.CompilerParams(vmem_limit_bytes=4 * 1024 * 1024)
PARAMS = pltpu.CompilerParams(vmem_limit_bytes=32 * 1024 * 1024)


def cost(flops, moved, special=0):
    return pl.CostEstimate(flops=flops, bytes_accessed=moved, transcendentals=special)


def shifted_columns(planes, out, first, flip):
    width = 128 * len(planes)
    blank = jnp.zeros((COLS, width), BF)
    cols = slice(first, first + width)
    for c in range(3):
        out[c, 0:COLS, cols] = blank
        out[c, PADDED - COLS : PADDED, cols] = blank
    before, after = (2, 0) if flip else (0, 2)

    def strip(i, carry):
        at = pl.multiple_of(i * STRIP, STRIP)
        to = pl.ds(pl.multiple_of(at + COLS, COLS), STRIP)
        col = lax.broadcasted_iota(jnp.int32, (STRIP, C), 0) & (COLS - 1)
        for k, plane in enumerate(planes):
            cols = slice(first + k * C, first + (k + 1) * C)
            here = plane(pl.ds(at, STRIP))
            wide = here.astype(F32)
            out[1, to, cols] = here
            out[before, to, cols] = jnp.where(
                col == 0, 0.0, pltpu.roll(wide, 1, 0)
            ).astype(BF)
            out[after, to, cols] = jnp.where(
                col == COLS - 1, 0.0, pltpu.roll(wide, STRIP - 1, 0)
            ).astype(BF)
        return carry

    lax.fori_loop(0, CELLS // STRIP, strip, 0)


def transposed(plane, out, first):
    for at in range(0, CELLS, TILE):
        out[first : first + C, at : at + TILE] = jnp.transpose(
            plane(pl.ds(at, TILE))
        )


def rows_of(plane):
    return lambda rows: plane[rows, :]


def ordered(core, near, far):
    def pick(first, second):
        return lambda rows: jnp.where(core == 0, first[rows, :], second[rows, :])

    return pick(far, near), pick(near, far)


def fetched(source, held, sem):
    copy = pltpu.make_async_copy(source, held, sem)
    copy.start()
    return copy


def tap(a, b, c):
    return (a * 3 + b) * 3 + c


def taps_of(field, at, rows):
    return jnp.concatenate(
        [
            field[c, pl.ds(pl.multiple_of(at + b * COLS, COLS), rows), :]
            for b in range(3)
            for c in range(3)
        ],
        axis=1,
    )


def inner_kernel(core_ref, near, far, weight, out, vol_t, field, mixed, held, sem):
    copy = fetched(weight, held, sem)
    planes = ordered(core_ref[0], near, far)
    shifted_columns(planes, field, 0, False)
    copy.wait()
    for b in range(3):
        for c in range(3):
            base = (b * 3 + c) * 256
            for p in range(2):
                for z in range(2):
                    t = tap(1 + p - z, b, c)
                    mixed[base + p * C : base + (p + 1) * C, z * C : (z + 1) * C] = (
                        held[t * C : (t + 1) * C, :]
                    )

    def tile(i, carry):
        at = pl.multiple_of(i * TILE, TILE)
        got = jnp.dot(taps_of(field, at, TILE), mixed[...], preferred_element_type=F32)
        out[0, pl.ds(at, TILE), :] = got[:, 0:C]
        out[1, pl.ds(at, TILE), :] = got[:, C : 2 * C]
        return carry

    lax.fori_loop(0, CELLS // TILE, tile, 0)
    for p in range(2):
        transposed(planes[p], vol_t, p * C)


def inner_conv(core, near, far, weight):
    return pl.pallas_call(
        inner_kernel,
        out_shape=[
            jax.ShapeDtypeStruct((2, CELLS, C), F32),
            jax.ShapeDtypeStruct((2 * C, CELLS), BF),
        ],
        in_specs=[SMEM, VMEM, VMEM, HBM],
        out_specs=[VMEM] * 2,
        scratch_shapes=[
            pltpu.VMEM((3, PADDED, 2 * C), BF),
            pltpu.VMEM((9 * 256, 2 * C), BF),
            pltpu.VMEM((27 * C, C), BF),
            pltpu.SemaphoreType.DMA,
        ],
        compiler_params=INNER,
        cost_estimate=cost(2 * CELLS * 2304 * 256, 5 << 20),
        name="inner_conv",
    )(core, near, far, weight)


def place(core, group, owner):
    half = jnp.where(owner // 16 == core, 0, 64)
    return half + (owner % 16) * 4 + group


def side(
    core,
    z,
    begun,
    halo,
    weight,
    inner,
    upstream,
    vol_t,
    grad,
    part,
    field,
    held,
    shifts,
    turned,
    sem,
    leave_sems,
):
    first = pl.multiple_of(z * 18 * C, 18 * C)
    copy = fetched(weight.at[pl.ds(first, 9 * C), :], held, sem)
    shifted_columns([rows_of(halo)], field, 0, False)
    transposed(rows_of(halo), turned, 0)
    blank = jnp.zeros((COLS, C), BF)
    for c in range(3):
        shifts[c, 0:COLS, :] = blank
        shifts[c, PADDED - COLS : PADDED, :] = blank
    copy.wait()
    for owner in range(27, 32):
        for group in range(4):
            part[place(core, group, owner)] = jnp.zeros((CHUNK, C), F32)

    def leave(i):
        at = pl.multiple_of(i * TILE, TILE)
        held_at = pl.ds(pl.multiple_of(at + COLS, COLS), TILE)
        return pltpu.make_async_copy(
            shifts.at[1, held_at, :], grad.at[pl.ds(at, TILE), :], leave_sems.at[i]
        )

    def tile(i, carry):
        at = pl.multiple_of(i * TILE, TILE)
        rows = pl.ds(at, TILE)
        to = pl.ds(pl.multiple_of(at + COLS, COLS), TILE)
        preact = inner[z, rows, :] + jnp.dot(
            taps_of(field, at, TILE), held[...], preferred_element_type=F32
        )
        s = jax.nn.sigmoid(preact)
        slopes = s * (1.0 + preact * (1.0 - s))
        here = (upstream[z, rows, :].astype(F32) * slopes).astype(BF)
        wide = here.astype(F32)
        col = lax.broadcasted_iota(jnp.int32, (TILE, C), 0) & (COLS - 1)
        shifts[1, to, :] = here
        leave(i).start()
        shifts[0, to, :] = jnp.where(col == 0, 0.0, pltpu.roll(wide, 1, 0)).astype(BF)
        shifts[2, to, :] = jnp.where(
            col == COLS - 1, 0.0, pltpu.roll(wide, TILE - 1, 0)
        ).astype(BF)
        return carry

    lax.fori_loop(0, CELLS // TILE, tile, 0)

    lhs = jnp.concatenate([vol_t[...], turned[...]], axis=0)
    offset_of = (1 - z, 2 - z, 2 * z)
    couples = [((b, 0), (b, 1)) for b in range(3)] + [((0, 2), (1, 2)), ((2, 2),)]
    for couple in couples:
        rhs = jnp.concatenate(
            [
                shifts[2 - c, (2 - b) * COLS : (2 - b) * COLS + CELLS, :]
                for b, c in couple
            ],
            axis=1,
        )
        got = jnp.dot(lhs, rhs, preferred_element_type=F32)
        for k, (b, c) in enumerate(couple):
            for p in range(3):
                for i in range(4):
                    chunk = 4 * tap(offset_of[p], b, c) + i
                    group = chunk // 27
                    at = place(core, group, chunk - 27 * group)
                    first = p * C + i * CHUNK
                    block = got[first : first + CHUNK, k * C : (k + 1) * C]
                    part[at] = block if begun is None else begun[at] + block
    for i in range(CELLS // TILE):
        leave(i).wait()


def near_kernel(core_ref, *refs):
    core = core_ref[0]
    side(core, 1 - core, None, *refs)


def far_kernel(
    core_ref, begun, halo, weight, inner, upstream, vol_t, grad, part, sent, *scratch
):
    core = core_ref[0]
    side(
        core, core, begun, halo, weight, inner, upstream, vol_t, grad, part, *scratch
    )
    sent[...] = part[64:128].astype(BF)


PLANE = jax.ShapeDtypeStruct((CELLS, C), BF)
PART = (4 * 32, CHUNK, C)
SIDE = [
    pltpu.VMEM((3, PADDED, C), BF),
    pltpu.VMEM((9 * C, C), BF),
    pltpu.VMEM((3, PADDED, C), BF),
    pltpu.VMEM((C, CELLS), BF),
    pltpu.SemaphoreType.DMA,
    pltpu.SemaphoreType.DMA((CELLS // TILE,)),
]


def near_side(core, halo, weight, inner, upstream, vol_t):
    return pl.pallas_call(
        near_kernel,
        out_shape=[PLANE, jax.ShapeDtypeStruct(PART, F32)],
        in_specs=[SMEM, VMEM, HBM, VMEM, VMEM, VMEM],
        out_specs=[HBM, VMEM],
        scratch_shapes=SIDE,
        compiler_params=PARAMS,
        cost_estimate=cost(2 * CELLS * 3456 * 256, 5 << 20, CELLS * 128),
        name="near_side",
    )(core, halo, weight, inner, upstream, vol_t)


def far_side(core, begun, halo, weight, inner, upstream, vol_t):
    return pl.pallas_call(
        far_kernel,
        out_shape=[
            PLANE,
            jax.ShapeDtypeStruct(PART, F32),
            jax.ShapeDtypeStruct((64, CHUNK, C), BF),
        ],
        in_specs=[SMEM, VMEM, VMEM, HBM, VMEM, VMEM, VMEM],
        out_specs=[HBM, VMEM, VMEM],
        scratch_shapes=SIDE,
        compiler_params=PARAMS,
        cost_estimate=cost(2 * CELLS * 3456 * 256, 5 << 20, CELLS * 128),
        name="far_side",
    )(core, begun, halo, weight, inner, upstream, vol_t)


def halves_kernel(part, other, half):
    half[...] = (part[0:64] + other[...].astype(F32)).astype(BF)


def both_halves(part, other):
    return pl.pallas_call(
        halves_kernel,
        out_shape=jax.ShapeDtypeStruct((64, CHUNK, C), BF),
        in_specs=[VMEM, VMEM],
        out_specs=VMEM,
        compiler_params=SMALL,
        cost_estimate=cost(1 << 18, 2 << 20),
        name="both_halves",
    )(part, other)


def inner_back_kernel(
    core_ref, near, far, weight, later, out, field, mixed, held, made, sem, sems
):
    copy = fetched(weight, held, sem)
    shifted_columns(ordered(core_ref[0], near, far), field, 0, False)
    copy.wait()
    for b in range(3):
        for c in range(3):
            base = (b * 3 + c) * 256
            for p in range(2):
                for z in range(2):
                    t = tap(1 + z - p, 2 - b, 2 - c)
                    mixed[z * C : (z + 1) * C, base + p * C : base + (p + 1) * C] = (
                        held[t * C : (t + 1) * C, :]
                    )
    tiles = CELLS // TILE

    def leave(i, z):
        rows = pl.ds(pl.multiple_of(i * TILE, TILE), TILE)
        return pltpu.make_async_copy(
            made.at[z, rows, :], out.at[z, rows, :], sems.at[i, z]
        )

    def tile(i, carry):
        at = pl.multiple_of(i * TILE, TILE)
        got = lax.dot_general(
            taps_of(field, at, TILE),
            mixed[...],
            (((1,), (1,)), ((), ())),
            preferred_element_type=F32,
        )
        for z in range(2):
            made[z, pl.ds(at, TILE), :] = got[:, z * C : (z + 1) * C]
            leave(i, z).start()
        return carry

    lax.fori_loop(0, tiles, tile, 0)
    for i in range(tiles):
        for z in range(2):
            leave(i, z).wait()


def inner_back(core, near, far, weight, later):
    return pl.pallas_call(
        inner_back_kernel,
        out_shape=jax.ShapeDtypeStruct((2, CELLS, C), F32),
        in_specs=[SMEM, VMEM, VMEM, HBM, ANY],
        out_specs=HBM,
        scratch_shapes=[
            pltpu.VMEM((3, PADDED, 2 * C), BF),
            pltpu.VMEM((2 * C, 9 * 256), BF),
            pltpu.VMEM((27 * C, C), BF),
            pltpu.VMEM((2, CELLS, C), F32),
            pltpu.SemaphoreType.DMA,
            pltpu.SemaphoreType.DMA((CELLS // TILE, 2)),
        ],
        compiler_params=WHOLE,
        cost_estimate=cost(2 * CELLS * 2304 * 256, 5 << 20),
        name="inner_back",
    )(core, near, far, weight, later)


def outer_back_kernel(at_ref, halo, weight, given, kept, *rest):
    out, field, mixed, held, upstream, inner, made, sems, leave_sems = rest[-9:]
    z = at_ref[0]
    first = pl.multiple_of((2 - 2 * z) * 9 * C, 9 * C)
    copy = fetched(weight.at[pl.ds(first, 9 * C), :], held, sems.at[0])
    kept_copy = fetched(kept.at[z], inner, sems.at[1])
    given_copy = fetched(given.at[z], upstream, sems.at[2])
    shifted_columns([rows_of(halo)], field, 0, False)
    copy.wait()
    for b in range(3):
        for c in range(3):
            base = (b * 3 + c) * C
            t = tap(0, 2 - b, 2 - c)
            mixed[:, base : base + C] = held[t * C : (t + 1) * C, :]
    kept_copy.wait()
    given_copy.wait()
    tiles = CELLS // TILE

    def leave(i):
        rows = pl.ds(pl.multiple_of(i * TILE, TILE), TILE)
        return pltpu.make_async_copy(
            made.at[rows, :], out.at[z, rows, :], leave_sems.at[i]
        )

    def tile(i, carry):
        at = pl.multiple_of(i * TILE, TILE)
        rows = pl.ds(at, TILE)
        got = lax.dot_general(
            taps_of(field, at, TILE),
            mixed[...],
            (((1,), (1,)), ((), ())),
            preferred_element_type=F32,
        )
        made[rows, :] = (
            upstream[rows, :].astype(F32) + (inner[rows, :] + got)
        ).astype(BF)
        leave(i).start()
        return carry

    lax.fori_loop(0, tiles, tile, 0)
    for i in range(tiles):
        leave(i).wait()


def outer_back(name, z, halo, weight, given, inner, *begun):
    return pl.pallas_call(
        outer_back_kernel,
        out_shape=jax.ShapeDtypeStruct((2, CELLS, C), BF),
        in_specs=[SMEM, VMEM] + [HBM] * (3 + len(begun)),
        out_specs=HBM,
        scratch_shapes=[
            pltpu.VMEM((3, PADDED, C), BF),
            pltpu.VMEM((C, 9 * C), BF),
            pltpu.VMEM((9 * C, C), BF),
            pltpu.VMEM((CELLS, C), BF),
            pltpu.VMEM((CELLS, C), F32),
            pltpu.VMEM((CELLS, C), BF),
            pltpu.SemaphoreType.DMA((3,)),
            pltpu.SemaphoreType.DMA((CELLS // TILE,)),
        ],
        input_output_aliases={5: 0} if begun else {},
        compiler_params=LARGE,
        cost_estimate=cost(CELLS * 2304 * 256, 3 << 20),
        name=name,
    )(z, halo, weight, given, inner, *begun)


def planes_kernel(core_ref, vol, near, far):
    core = core_ref[0]
    far[...] = vol[core]
    near[...] = vol[1 - core]


def both_planes(core, vol):
    plane = jax.ShapeDtypeStruct((CELLS, C), BF)
    return pl.pallas_call(
        planes_kernel,
        out_shape=[plane, plane],
        in_specs=[SMEM, VMEM],
        out_specs=[VMEM, VMEM],
        compiler_params=SMALL,
        cost_estimate=cost(0, 2 << 20),
        name="both_planes",
    )(core, vol)


def first_rows_kernel(whole, out, wide, sems):
    rows = out.shape[0]
    step = rows // 4
    copies = []
    for k in range(4):
        part = slice(k * step, (k + 1) * step)
        wide[part, :] = whole[part, :].astype(F32)
        copy = pltpu.make_async_copy(wide.at[part, :], out.at[part, :], sems.at[k])
        copy.start()
        copies.append(copy)
    for copy in copies:
        copy.wait()


def first_rows(whole, rows):
    return pl.pallas_call(
        first_rows_kernel,
        out_shape=jax.ShapeDtypeStruct((rows, C), F32),
        in_specs=[VMEM],
        out_specs=ANY,
        scratch_shapes=[pltpu.VMEM((rows, C), F32), pltpu.SemaphoreType.DMA((4,))],
        compiler_params=SMALL,
        cost_estimate=cost(0, 1 << 20),
        name="first_rows",
    )(whole)


def mix_kernel(got, out):
    for group in range(4):
        total = got[0, group].astype(F32)
        for k in range(1, 16):
            total += got[k, group].astype(F32)
        out[group] = total.astype(BF)
        out[4 + group] = total.astype(BF)


def mixed_rows(got):
    return pl.pallas_call(
        mix_kernel,
        out_shape=jax.ShapeDtypeStruct((8, CHUNK, C), BF),
        in_specs=[VMEM],
        out_specs=VMEM,
        compiler_params=SMALL,
        cost_estimate=cost(1 << 18, 1 << 20),
        name="mixed_rows",
    )(got)


def step_kernel(at_ref, got, first, second, out):
    total = got[0].astype(F32)
    for k in range(1, 8):
        total += got[k].astype(F32)
    at = pl.multiple_of(at_ref[0], CHUNK)
    rows = pl.ds(at, CHUNK)
    step = adam(total, first[rows, :], second[rows, :])
    step = step.astype(BF)
    for k in range(OWNERS):
        out[k] = step


def spread_step(at, got, first, second):
    return pl.pallas_call(
        step_kernel,
        out_shape=jax.ShapeDtypeStruct((OWNERS, CHUNK, C), BF),
        in_specs=[SMEM] + [VMEM] * 3,
        out_specs=VMEM,
        compiler_params=SMALL,
        cost_estimate=cost(1 << 18, 1 << 20),
        name="spread_step",
    )(at, got, first, second)


def adam(grad, first, second):
    m_new = beta_one * first + (1.0 - beta_one) * grad
    v_new = beta_two * second + (1.0 - beta_two) * grad * grad
    return (
        m_new
        / (1.0 - beta_one**ADAM_STEP)
        / (jnp.sqrt(v_new / (1.0 - beta_two**ADAM_STEP)) + eps_adam)
    )


def from_neighbours(near, far):
    size = lax.axis_size(SPACE)
    pairs = [(i, i + 1) for i in range(1, size - 1, 2)]
    far_halo = lax.ppermute(far, SPACE, pairs + [(j, i) for i, j in pairs])
    near_halo = lax.ppermute(near, "core", [(0, 1), (1, 0)])
    return near_halo, far_halo


def body(volume, upstream, weight, first_moment, second_moment):
    vol = volume.reshape(2, CELLS, C)
    up = upstream.reshape(2, CELLS, C)
    core = lax.axis_index("core")
    at_core = core.reshape(1)
    near, far = both_planes(at_core, vol)
    near_halo, far_halo = from_neighbours(near, far)
    inner, vol_t = inner_conv(at_core, near, far, weight)
    near, part = near_side(at_core, near_halo, weight, inner, up, vol_t)
    far, part, sent = far_side(at_core, part, far_halo, weight, inner, up, vol_t)

    rows = first_moment.shape[0]
    other = lax.ppermute(sent, "core", [(0, 1), (1, 0)])
    half = both_halves(part, other).reshape(16, 4, CHUNK, C)
    got = lax.all_to_all(half, ("x", "y"), 0, 0)
    grad_near, grad_far = from_neighbours(near, far)
    local = inner_back(at_core, near, far, weight, half)
    got, local = lax.optimization_barrier((got, local))
    part = mixed_rows(got)
    grad_near, part = lax.optimization_barrier((grad_near, part))
    got = lax.all_to_all(part, ("zl", "sample"), 0, 0)
    half_done = outer_back("near_back", 1 - at_core, grad_near, weight, up, local)
    got, half_done = lax.optimization_barrier((got, half_done))
    owner = core * 16 + lax.axis_index("x") * 4 + lax.axis_index("y")
    at = jnp.minimum(owner * CHUNK, rows - CHUNK).reshape(1)
    step = spread_step(at, got, first_moment, second_moment)
    whole = lax.all_to_all(step, ("core", "x", "y"), 0, 0)
    grad_volume = outer_back(
        "far_back", at_core, grad_far, weight, up, local, half_done
    )
    direction = first_rows(whole.reshape(OWNERS * CHUNK, C), rows)
    return (grad_volume.reshape(volume.shape), direction)


def solution(mesh):
    fine = Mesh(
        mesh.devices.reshape(4, 4, 2, 2, 4), ("x", "y", "zl", "core", "sample")
    )
    field = P("sample", SPACE, None, None, None)
    return jax.shard_map(
        body,
        mesh=fine,
        in_specs=(field, field, P(), P("sample", None), P("sample", None)),
        out_specs=(field, P("sample", None)),
        check_vma=False,
    )
```

```python
import functools
import jax
import jax.numpy as jnp
from jax import lax
from jax.experimental import pallas as pl
from jax.experimental.pallas import tpu as pltpu
from jax.sharding import Mesh, PartitionSpec as P

ADAM_STEP = 10


beta_one = 0.9
beta_two = 0.999
eps_adam = 1e-08

SPACE = ("x", "y", "zl", "core")
CHUNK = 32
OWNERS = 32
C = 128
COLS = 64
ROWS = 32
CELLS = ROWS * COLS
PADDED = CELLS + 2 * COLS
STRIP = 256
TILE = 512
BF = jnp.bfloat16
F32 = jnp.float32
VMEM = pl.BlockSpec(memory_space=pltpu.VMEM)
ANY = pl.BlockSpec(memory_space=pl.ANY)
HBM = pl.BlockSpec(memory_space=pltpu.HBM)
SMEM = pl.BlockSpec(memory_space=pltpu.SMEM)
WHOLE = pltpu.CompilerParams(vmem_limit_bytes=60 * 1024 * 1024)
LARGE = pltpu.CompilerParams(vmem_limit_bytes=62 * 1024 * 1024 + 512 * 1024)
INNER = pltpu.CompilerParams(vmem_limit_bytes=44 * 1024 * 1024)
SMALL = pltpu.CompilerParams(vmem_limit_bytes=4 * 1024 * 1024)
PARAMS = pltpu.CompilerParams(vmem_limit_bytes=32 * 1024 * 1024)


def cost(flops, moved, special=0):
    return pl.CostEstimate(flops=flops, bytes_accessed=moved, transcendentals=special)


def shifted_columns(planes, out, first, flip):
    width = 128 * len(planes)
    blank = jnp.zeros((COLS, width), BF)
    cols = slice(first, first + width)
    for c in range(3):
        out[c, 0:COLS, cols] = blank
        out[c, PADDED - COLS : PADDED, cols] = blank
    before, after = (2, 0) if flip else (0, 2)

    def strip(i, carry):
        at = pl.multiple_of(i * STRIP, STRIP)
        to = pl.ds(pl.multiple_of(at + COLS, COLS), STRIP)
        col = lax.broadcasted_iota(jnp.int32, (STRIP, C), 0) & (COLS - 1)
        for k, plane in enumerate(planes):
            cols = slice(first + k * C, first + (k + 1) * C)
            here = plane(pl.ds(at, STRIP))
            wide = here.astype(F32)
            out[1, to, cols] = here
            out[before, to, cols] = jnp.where(
                col == 0, 0.0, pltpu.roll(wide, 1, 0)
            ).astype(BF)
            out[after, to, cols] = jnp.where(
                col == COLS - 1, 0.0, pltpu.roll(wide, STRIP - 1, 0)
            ).astype(BF)
        return carry

    lax.fori_loop(0, CELLS // STRIP, strip, 0)


def transposed(plane, out, first):
    for at in range(0, CELLS, TILE):
        out[first : first + C, at : at + TILE] = jnp.transpose(
            plane(pl.ds(at, TILE))
        )


def rows_of(plane):
    return lambda rows: plane[rows, :]


def ordered(core, near, far):
    def pick(first, second):
        return lambda rows: jnp.where(core == 0, first[rows, :], second[rows, :])

    return pick(far, near), pick(near, far)


def fetched(source, held, sem):
    copy = pltpu.make_async_copy(source, held, sem)
    copy.start()
    return copy


def tap(a, b, c):
    return (a * 3 + b) * 3 + c


def taps_of(field, at, rows):
    return jnp.concatenate(
        [
            field[c, pl.ds(pl.multiple_of(at + b * COLS, COLS), rows), :]
            for b in range(3)
            for c in range(3)
        ],
        axis=1,
    )


def inner_kernel(core_ref, near, far, weight, out, vol_t, field, mixed, held, sem):
    copy = fetched(weight, held, sem)
    planes = ordered(core_ref[0], near, far)
    shifted_columns(planes, field, 0, False)
    copy.wait()
    for b in range(3):
        for c in range(3):
            base = (b * 3 + c) * 256
            for p in range(2):
                for z in range(2):
                    t = tap(1 + p - z, b, c)
                    mixed[base + p * C : base + (p + 1) * C, z * C : (z + 1) * C] = (
                        held[t * C : (t + 1) * C, :]
                    )

    def tile(i, carry):
        at = pl.multiple_of(i * TILE, TILE)
        got = jnp.dot(taps_of(field, at, TILE), mixed[...], preferred_element_type=F32)
        out[0, pl.ds(at, TILE), :] = got[:, 0:C]
        out[1, pl.ds(at, TILE), :] = got[:, C : 2 * C]
        return carry

    lax.fori_loop(0, CELLS // TILE, tile, 0, unroll=True)
    for p in range(2):
        transposed(planes[p], vol_t, p * C)


def inner_conv(core, near, far, weight):
    return pl.pallas_call(
        inner_kernel,
        out_shape=[
            jax.ShapeDtypeStruct((2, CELLS, C), F32),
            jax.ShapeDtypeStruct((2 * C, CELLS), BF),
        ],
        in_specs=[SMEM, VMEM, VMEM, HBM],
        out_specs=[VMEM] * 2,
        scratch_shapes=[
            pltpu.VMEM((3, PADDED, 2 * C), BF),
            pltpu.VMEM((9 * 256, 2 * C), BF),
            pltpu.VMEM((27 * C, C), BF),
            pltpu.SemaphoreType.DMA,
        ],
        compiler_params=INNER,
        cost_estimate=cost(2 * CELLS * 2304 * 256, 5 << 20),
        name="inner_conv",
    )(core, near, far, weight)


def place(core, group, owner):
    half = 0 if owner // 16 == core else 64
    return half + (owner % 16) * 4 + group


def side(
    core,
    z,
    begun,
    halo,
    weight,
    inner,
    upstream,
    vol_t,
    grad,
    part,
    field,
    held,
    shifts,
    turned,
    sem,
    leave_sems,
):
    first = z * 18 * C
    copy = fetched(weight.at[first : first + 9 * C, :], held, sem)
    shifted_columns([rows_of(halo)], field, 0, False)
    transposed(rows_of(halo), turned, 0)
    blank = jnp.zeros((COLS, C), BF)
    for c in range(3):
        shifts[c, 0:COLS, :] = blank
        shifts[c, PADDED - COLS : PADDED, :] = blank
    copy.wait()
    for owner in range(27, 32):
        for group in range(4):
            part[place(core, group, owner)] = jnp.zeros((CHUNK, C), F32)

    def leave(i):
        at = pl.multiple_of(i * TILE, TILE)
        held_at = pl.ds(pl.multiple_of(at + COLS, COLS), TILE)
        return pltpu.make_async_copy(
            shifts.at[1, held_at, :], grad.at[pl.ds(at, TILE), :], leave_sems.at[i]
        )

    def tile(i, carry):
        at = pl.multiple_of(i * TILE, TILE)
        rows = pl.ds(at, TILE)
        to = pl.ds(pl.multiple_of(at + COLS, COLS), TILE)
        preact = inner[z, rows, :] + jnp.dot(
            taps_of(field, at, TILE), held[...], preferred_element_type=F32
        )
        s = jax.nn.sigmoid(preact)
        slopes = s * (1.0 + preact * (1.0 - s))
        here = (upstream[z, rows, :].astype(F32) * slopes).astype(BF)
        wide = here.astype(F32)
        col = lax.broadcasted_iota(jnp.int32, (TILE, C), 0) & (COLS - 1)
        shifts[1, to, :] = here
        leave(i).start()
        shifts[0, to, :] = jnp.where(col == 0, 0.0, pltpu.roll(wide, 1, 0)).astype(BF)
        shifts[2, to, :] = jnp.where(
            col == COLS - 1, 0.0, pltpu.roll(wide, TILE - 1, 0)
        ).astype(BF)
        return carry

    lax.fori_loop(0, CELLS // TILE, tile, 0)

    lhs = jnp.concatenate([vol_t[...], turned[...]], axis=0)
    offset_of = (1 - z, 2 - z, 2 * z)
    couples = [((b, 0), (b, 1)) for b in range(3)] + [((0, 2), (1, 2)), ((2, 2),)]
    for couple in couples:
        rhs = jnp.concatenate(
            [
                shifts[2 - c, (2 - b) * COLS : (2 - b) * COLS + CELLS, :]
                for b, c in couple
            ],
            axis=1,
        )
        got = jnp.dot(lhs, rhs, preferred_element_type=F32)
        for k, (b, c) in enumerate(couple):
            for p in range(3):
                for i in range(4):
                    chunk = 4 * tap(offset_of[p], b, c) + i
                    group = chunk // 27
                    at = place(core, group, chunk - 27 * group)
                    first = p * C + i * CHUNK
                    block = got[first : first + CHUNK, k * C : (k + 1) * C]
                    part[at] = block if begun is None else begun[at] + block
    for i in range(CELLS // TILE):
        leave(i).wait()


def near_kernel(core_ref, *refs):
    for core in range(2):

        @pl.when(core_ref[0] == core)
        def _():
            side(core, 1 - core, None, *refs)


def far_kernel(
    core_ref, begun, halo, weight, inner, upstream, vol_t, grad, part, sent, *scratch
):
    for core in range(2):

        @pl.when(core_ref[0] == core)
        def _():
            side(
                core,
                core,
                begun,
                halo,
                weight,
                inner,
                upstream,
                vol_t,
                grad,
                part,
                *scratch,
            )

    sent[...] = part[64:128].astype(BF)


PLANE = jax.ShapeDtypeStruct((CELLS, C), BF)
PART = (4 * 32, CHUNK, C)
SIDE = [
    pltpu.VMEM((3, PADDED, C), BF),
    pltpu.VMEM((9 * C, C), BF),
    pltpu.VMEM((3, PADDED, C), BF),
    pltpu.VMEM((C, CELLS), BF),
    pltpu.SemaphoreType.DMA,
    pltpu.SemaphoreType.DMA((CELLS // TILE,)),
]


def near_side(core, halo, weight, inner, upstream, vol_t):
    return pl.pallas_call(
        near_kernel,
        out_shape=[PLANE, jax.ShapeDtypeStruct(PART, F32)],
        in_specs=[SMEM, VMEM, HBM, VMEM, VMEM, VMEM],
        out_specs=[HBM, VMEM],
        scratch_shapes=SIDE,
        compiler_params=PARAMS,
        cost_estimate=cost(2 * CELLS * 3456 * 256, 5 << 20, CELLS * 128),
        name="near_side",
    )(core, halo, weight, inner, upstream, vol_t)


def far_side(core, begun, halo, weight, inner, upstream, vol_t):
    return pl.pallas_call(
        far_kernel,
        out_shape=[
            PLANE,
            jax.ShapeDtypeStruct(PART, F32),
            jax.ShapeDtypeStruct((64, CHUNK, C), BF),
        ],
        in_specs=[SMEM, VMEM, VMEM, HBM, VMEM, VMEM, VMEM],
        out_specs=[HBM, VMEM, VMEM],
        scratch_shapes=SIDE,
        compiler_params=PARAMS,
        cost_estimate=cost(2 * CELLS * 3456 * 256, 5 << 20, CELLS * 128),
        name="far_side",
    )(core, begun, halo, weight, inner, upstream, vol_t)


def halves_kernel(part, other, half):
    half[...] = (part[0:64] + other[...].astype(F32)).astype(BF)


def both_halves(part, other):
    return pl.pallas_call(
        halves_kernel,
        out_shape=jax.ShapeDtypeStruct((64, CHUNK, C), BF),
        in_specs=[VMEM, VMEM],
        out_specs=VMEM,
        compiler_params=SMALL,
        cost_estimate=cost(1 << 18, 2 << 20),
        name="both_halves",
    )(part, other)


def inner_back_kernel(
    core_ref, near, far, weight, later, out, field, mixed, held, made, sem, sems
):
    copy = fetched(weight, held, sem)
    shifted_columns(ordered(core_ref[0], near, far), field, 0, False)
    copy.wait()
    for b in range(3):
        for c in range(3):
            base = (b * 3 + c) * 256
            for p in range(2):
                for z in range(2):
                    t = tap(1 + z - p, 2 - b, 2 - c)
                    mixed[z * C : (z + 1) * C, base + p * C : base + (p + 1) * C] = (
                        held[t * C : (t + 1) * C, :]
                    )
    tiles = CELLS // TILE

    def leave(i, z):
        rows = pl.ds(pl.multiple_of(i * TILE, TILE), TILE)
        return pltpu.make_async_copy(
            made.at[z, rows, :], out.at[z, rows, :], sems.at[i, z]
        )

    def tile(i, carry):
        at = pl.multiple_of(i * TILE, TILE)
        got = lax.dot_general(
            taps_of(field, at, TILE),
            mixed[...],
            (((1,), (1,)), ((), ())),
            preferred_element_type=F32,
        )
        for z in range(2):
            made[z, pl.ds(at, TILE), :] = got[:, z * C : (z + 1) * C]
            leave(i, z).start()
        return carry

    lax.fori_loop(0, tiles, tile, 0, unroll=True)
    for i in range(tiles):
        for z in range(2):
            leave(i, z).wait()


def inner_back(core, near, far, weight, later):
    return pl.pallas_call(
        inner_back_kernel,
        out_shape=jax.ShapeDtypeStruct((2, CELLS, C), F32),
        in_specs=[SMEM, VMEM, VMEM, HBM, ANY],
        out_specs=HBM,
        scratch_shapes=[
            pltpu.VMEM((3, PADDED, 2 * C), BF),
            pltpu.VMEM((2 * C, 9 * 256), BF),
            pltpu.VMEM((27 * C, C), BF),
            pltpu.VMEM((2, CELLS, C), F32),
            pltpu.SemaphoreType.DMA,
            pltpu.SemaphoreType.DMA((CELLS // TILE, 2)),
        ],
        compiler_params=WHOLE,
        cost_estimate=cost(2 * CELLS * 2304 * 256, 5 << 20),
        name="inner_back",
    )(core, near, far, weight, later)


def outer_back_kernel(at_ref, halo, weight, given, kept, *rest):
    out, field, mixed, held, upstream, inner, made, sems, leave_sems = rest[-9:]
    z = at_ref[0]
    first = pl.multiple_of((2 - 2 * z) * 9 * C, 9 * C)
    copy = fetched(weight.at[pl.ds(first, 9 * C), :], held, sems.at[0])
    kept_copy = fetched(kept.at[z], inner, sems.at[1])
    given_copy = fetched(given.at[z], upstream, sems.at[2])
    shifted_columns([rows_of(halo)], field, 0, False)
    copy.wait()
    for b in range(3):
        for c in range(3):
            base = (b * 3 + c) * C
            t = tap(0, 2 - b, 2 - c)
            mixed[:, base : base + C] = held[t * C : (t + 1) * C, :]
    kept_copy.wait()
    given_copy.wait()
    tiles = CELLS // TILE

    def leave(i):
        rows = pl.ds(pl.multiple_of(i * TILE, TILE), TILE)
        return pltpu.make_async_copy(
            made.at[rows, :], out.at[z, rows, :], leave_sems.at[i]
        )

    def tile(i, carry):
        at = pl.multiple_of(i * TILE, TILE)
        rows = pl.ds(at, TILE)
        got = lax.dot_general(
            taps_of(field, at, TILE),
            mixed[...],
            (((1,), (1,)), ((), ())),
            preferred_element_type=F32,
        )
        made[rows, :] = (
            upstream[rows, :].astype(F32) + (inner[rows, :] + got)
        ).astype(BF)
        leave(i).start()
        return carry

    lax.fori_loop(0, tiles, tile, 0, unroll=True)
    for i in range(tiles):
        leave(i).wait()


def outer_back(name, z, halo, weight, given, inner, *begun):
    return pl.pallas_call(
        outer_back_kernel,
        out_shape=jax.ShapeDtypeStruct((2, CELLS, C), BF),
        in_specs=[SMEM, VMEM] + [HBM] * (3 + len(begun)),
        out_specs=HBM,
        scratch_shapes=[
            pltpu.VMEM((3, PADDED, C), BF),
            pltpu.VMEM((C, 9 * C), BF),
            pltpu.VMEM((9 * C, C), BF),
            pltpu.VMEM((CELLS, C), BF),
            pltpu.VMEM((CELLS, C), F32),
            pltpu.VMEM((CELLS, C), BF),
            pltpu.SemaphoreType.DMA((3,)),
            pltpu.SemaphoreType.DMA((CELLS // TILE,)),
        ],
        input_output_aliases={5: 0} if begun else {},
        compiler_params=LARGE,
        cost_estimate=cost(CELLS * 2304 * 256, 3 << 20),
        name=name,
    )(z, halo, weight, given, inner, *begun)


def planes_kernel(core_ref, vol, near, far):
    core = core_ref[0]
    far[...] = vol[core]
    near[...] = vol[1 - core]


def both_planes(core, vol):
    plane = jax.ShapeDtypeStruct((CELLS, C), BF)
    return pl.pallas_call(
        planes_kernel,
        out_shape=[plane, plane],
        in_specs=[SMEM, VMEM],
        out_specs=[VMEM, VMEM],
        compiler_params=SMALL,
        cost_estimate=cost(0, 2 << 20),
        name="both_planes",
    )(core, vol)


def first_rows_kernel(whole, out, wide, sems):
    rows = out.shape[0]
    step = rows // 4
    copies = []
    for k in range(4):
        part = slice(k * step, (k + 1) * step)
        wide[part, :] = whole[part, :].astype(F32)
        copy = pltpu.make_async_copy(wide.at[part, :], out.at[part, :], sems.at[k])
        copy.start()
        copies.append(copy)
    for copy in copies:
        copy.wait()


def first_rows(whole, rows):
    return pl.pallas_call(
        first_rows_kernel,
        out_shape=jax.ShapeDtypeStruct((rows, C), F32),
        in_specs=[VMEM],
        out_specs=ANY,
        scratch_shapes=[pltpu.VMEM((rows, C), F32), pltpu.SemaphoreType.DMA((4,))],
        compiler_params=SMALL,
        cost_estimate=cost(0, 1 << 20),
        name="first_rows",
    )(whole)


def mix_kernel(got, out):
    for group in range(4):
        total = got[0, group].astype(F32)
        for k in range(1, 16):
            total += got[k, group].astype(F32)
        out[group] = total.astype(BF)
        out[4 + group] = total.astype(BF)


def mixed_rows(got):
    return pl.pallas_call(
        mix_kernel,
        out_shape=jax.ShapeDtypeStruct((8, CHUNK, C), BF),
        in_specs=[VMEM],
        out_specs=VMEM,
        compiler_params=SMALL,
        cost_estimate=cost(1 << 18, 1 << 20),
        name="mixed_rows",
    )(got)


def step_kernel(at_ref, got, first, second, out):
    total = got[0].astype(F32)
    for k in range(1, 8):
        total += got[k].astype(F32)
    at = pl.multiple_of(at_ref[0], CHUNK)
    rows = pl.ds(at, CHUNK)
    step = adam(total, first[rows, :], second[rows, :])
    step = step.astype(BF)
    for k in range(OWNERS):
        out[k] = step


def spread_step(at, got, first, second):
    return pl.pallas_call(
        step_kernel,
        out_shape=jax.ShapeDtypeStruct((OWNERS, CHUNK, C), BF),
        in_specs=[SMEM] + [VMEM] * 3,
        out_specs=VMEM,
        compiler_params=SMALL,
        cost_estimate=cost(1 << 18, 1 << 20),
        name="spread_step",
    )(at, got, first, second)


def adam(grad, first, second):
    m_new = beta_one * first + (1.0 - beta_one) * grad
    v_new = beta_two * second + (1.0 - beta_two) * grad * grad
    return (
        m_new
        / (1.0 - beta_one**ADAM_STEP)
        / (jnp.sqrt(v_new / (1.0 - beta_two**ADAM_STEP)) + eps_adam)
    )


def from_neighbours(near, far):
    size = lax.axis_size(SPACE)
    pairs = [(i, i + 1) for i in range(1, size - 1, 2)]
    far_halo = lax.ppermute(far, SPACE, pairs + [(j, i) for i, j in pairs])
    near_halo = lax.ppermute(near, "core", [(0, 1), (1, 0)])
    return near_halo, far_halo


def body(volume, upstream, weight, first_moment, second_moment):
    vol = volume.reshape(2, CELLS, C)
    up = upstream.reshape(2, CELLS, C)
    core = lax.axis_index("core")
    at_core = core.reshape(1)
    near, far = both_planes(at_core, vol)
    near_halo, far_halo = from_neighbours(near, far)
    inner, vol_t = inner_conv(at_core, near, far, weight)
    near, part = near_side(at_core, near_halo, weight, inner, up, vol_t)
    far, part, sent = far_side(at_core, part, far_halo, weight, inner, up, vol_t)

    rows = first_moment.shape[0]
    other = lax.ppermute(sent, "core", [(0, 1), (1, 0)])
    half = both_halves(part, other).reshape(16, 4, CHUNK, C)
    got = lax.all_to_all(half, ("x", "y"), 0, 0)
    grad_near, grad_far = from_neighbours(near, far)
    local = inner_back(at_core, near, far, weight, half)
    got, local = lax.optimization_barrier((got, local))
    part = mixed_rows(got)
    grad_near, part = lax.optimization_barrier((grad_near, part))
    got = lax.all_to_all(part, ("zl", "sample"), 0, 0)
    half_done = outer_back("near_back", 1 - at_core, grad_near, weight, up, local)
    got, half_done = lax.optimization_barrier((got, half_done))
    owner = core * 16 + lax.axis_index("x") * 4 + lax.axis_index("y")
    at = jnp.minimum(owner * CHUNK, rows - CHUNK).reshape(1)
    step = spread_step(at, got, first_moment, second_moment)
    whole = lax.all_to_all(step, ("core", "x", "y"), 0, 0)
    grad_volume = outer_back(
        "far_back", at_core, grad_far, weight, up, local, half_done
    )
    direction = first_rows(whole.reshape(OWNERS * CHUNK, C), rows)
    return (grad_volume.reshape(volume.shape), direction)


def solution(mesh):
    fine = Mesh(
        mesh.devices.reshape(4, 4, 2, 2, 4), ("x", "y", "zl", "core", "sample")
    )
    field = P("sample", SPACE, None, None, None)
    return jax.shard_map(
        body,
        mesh=fine,
        in_specs=(field, field, P(), P("sample", None), P("sample", None)),
        out_specs=(field, P("sample", None)),
        check_vma=False,
    )
```

```python
import functools
import jax
import jax.numpy as jnp
from jax import lax
from jax.experimental import pallas as pl
from jax.experimental.pallas import tpu as pltpu
from jax.sharding import Mesh, PartitionSpec as P

ADAM_STEP = 10


beta_one = 0.9
beta_two = 0.999
eps_adam = 1e-08

SPACE = ("x", "y", "zl", "core")
CHUNK = 32
OWNERS = 32
C = 128
COLS = 64
ROWS = 32
CELLS = ROWS * COLS
PADDED = CELLS + 2 * COLS
STRIP = 256
TILE = 512
BF = jnp.bfloat16
F32 = jnp.float32
VMEM = pl.BlockSpec(memory_space=pltpu.VMEM)
ANY = pl.BlockSpec(memory_space=pl.ANY)
HBM = pl.BlockSpec(memory_space=pltpu.HBM)
SMEM = pl.BlockSpec(memory_space=pltpu.SMEM)
WHOLE = pltpu.CompilerParams(vmem_limit_bytes=60 * 1024 * 1024)
LARGE = pltpu.CompilerParams(vmem_limit_bytes=62 * 1024 * 1024 + 512 * 1024)
INNER = pltpu.CompilerParams(vmem_limit_bytes=44 * 1024 * 1024)
SMALL = pltpu.CompilerParams(vmem_limit_bytes=4 * 1024 * 1024)
PARAMS = pltpu.CompilerParams(vmem_limit_bytes=32 * 1024 * 1024)


def cost(flops, moved, special=0):
    return pl.CostEstimate(flops=flops, bytes_accessed=moved, transcendentals=special)


def shifted_columns(planes, out, first, flip):
    width = 128 * len(planes)
    blank = jnp.zeros((COLS, width), BF)
    cols = slice(first, first + width)
    for c in range(3):
        out[c, 0:COLS, cols] = blank
        out[c, PADDED - COLS : PADDED, cols] = blank
    before, after = (2, 0) if flip else (0, 2)

    def strip(i, carry):
        at = pl.multiple_of(i * STRIP, STRIP)
        to = pl.ds(pl.multiple_of(at + COLS, COLS), STRIP)
        col = lax.broadcasted_iota(jnp.int32, (STRIP, C), 0) & (COLS - 1)
        for k, plane in enumerate(planes):
            cols = slice(first + k * C, first + (k + 1) * C)
            here = plane(pl.ds(at, STRIP))
            wide = here.astype(F32)
            out[1, to, cols] = here
            out[before, to, cols] = jnp.where(
                col == 0, 0.0, pltpu.roll(wide, 1, 0)
            ).astype(BF)
            out[after, to, cols] = jnp.where(
                col == COLS - 1, 0.0, pltpu.roll(wide, STRIP - 1, 0)
            ).astype(BF)
        return carry

    lax.fori_loop(0, CELLS // STRIP, strip, 0)


def transposed(plane, out, first):
    for at in range(0, CELLS, TILE):
        out[first : first + C, at : at + TILE] = jnp.transpose(
            plane(pl.ds(at, TILE))
        )


def rows_of(plane):
    return lambda rows: plane[rows, :]


def ordered(core, near, far):
    def pick(first, second):
        return lambda rows: jnp.where(core == 0, first[rows, :], second[rows, :])

    return pick(far, near), pick(near, far)


def fetched(source, held, sem):
    copy = pltpu.make_async_copy(source, held, sem)
    copy.start()
    return copy


def tap(a, b, c):
    return (a * 3 + b) * 3 + c


def taps_of(field, at, rows):
    return jnp.concatenate(
        [
            field[c, pl.ds(pl.multiple_of(at + b * COLS, COLS), rows), :]
            for b in range(3)
            for c in range(3)
        ],
        axis=1,
    )


def inner_kernel(core_ref, near, far, weight, out, vol_t, field, mixed, held, sem):
    copy = fetched(weight, held, sem)
    planes = ordered(core_ref[0], near, far)
    shifted_columns(planes, field, 0, False)
    copy.wait()
    for b in range(3):
        for c in range(3):
            base = (b * 3 + c) * 256
            for p in range(2):
                for z in range(2):
                    t = tap(1 + p - z, b, c)
                    mixed[base + p * C : base + (p + 1) * C, z * C : (z + 1) * C] = (
                        held[t * C : (t + 1) * C, :]
                    )

    def tile(i, carry):
        at = pl.multiple_of(i * TILE, TILE)
        got = jnp.dot(taps_of(field, at, TILE), mixed[...], preferred_element_type=F32)
        out[0, pl.ds(at, TILE), :] = got[:, 0:C]
        out[1, pl.ds(at, TILE), :] = got[:, C : 2 * C]
        return carry

    lax.fori_loop(0, CELLS // TILE, tile, 0, unroll=True)
    for p in range(2):
        transposed(planes[p], vol_t, p * C)


def inner_conv(core, near, far, weight):
    return pl.pallas_call(
        inner_kernel,
        out_shape=[
            jax.ShapeDtypeStruct((2, CELLS, C), F32),
            jax.ShapeDtypeStruct((2 * C, CELLS), BF),
        ],
        in_specs=[SMEM, VMEM, VMEM, HBM],
        out_specs=[VMEM] * 2,
        scratch_shapes=[
            pltpu.VMEM((3, PADDED, 2 * C), BF),
            pltpu.VMEM((9 * 256, 2 * C), BF),
            pltpu.VMEM((27 * C, C), BF),
            pltpu.SemaphoreType.DMA,
        ],
        compiler_params=INNER,
        cost_estimate=cost(2 * CELLS * 2304 * 256, 5 << 20),
        name="inner_conv",
    )(core, near, far, weight)


def place(core, group, owner):
    half = 0 if owner // 16 == core else 64
    return half + (owner % 16) * 4 + group


def side(
    core,
    z,
    begun,
    halo,
    weight,
    inner,
    upstream,
    vol_t,
    grad,
    part,
    field,
    held,
    shifts,
    turned,
    sem,
    leave_sems,
):
    first = z * 18 * C
    copy = fetched(weight.at[first : first + 9 * C, :], held, sem)
    shifted_columns([rows_of(halo)], field, 0, False)
    transposed(rows_of(halo), turned, 0)
    blank = jnp.zeros((COLS, C), BF)
    for c in range(3):
        shifts[c, 0:COLS, :] = blank
        shifts[c, PADDED - COLS : PADDED, :] = blank
    copy.wait()
    for owner in range(27, 32):
        for group in range(4):
            part[place(core, group, owner)] = jnp.zeros((CHUNK, C), F32)

    def leave(i):
        at = pl.multiple_of(i * TILE, TILE)
        held_at = pl.ds(pl.multiple_of(at + COLS, COLS), TILE)
        return pltpu.make_async_copy(
            shifts.at[1, held_at, :], grad.at[pl.ds(at, TILE), :], leave_sems.at[i]
        )

    def tile(i, carry):
        at = pl.multiple_of(i * TILE, TILE)
        rows = pl.ds(at, TILE)
        to = pl.ds(pl.multiple_of(at + COLS, COLS), TILE)
        preact = inner[z, rows, :] + jnp.dot(
            taps_of(field, at, TILE), held[...], preferred_element_type=F32
        )
        s = jax.nn.sigmoid(preact)
        slopes = s * (1.0 + preact * (1.0 - s))
        here = (upstream[z, rows, :].astype(F32) * slopes).astype(BF)
        wide = here.astype(F32)
        col = lax.broadcasted_iota(jnp.int32, (TILE, C), 0) & (COLS - 1)
        shifts[1, to, :] = here
        leave(i).start()
        shifts[0, to, :] = jnp.where(col == 0, 0.0, pltpu.roll(wide, 1, 0)).astype(BF)
        shifts[2, to, :] = jnp.where(
            col == COLS - 1, 0.0, pltpu.roll(wide, TILE - 1, 0)
        ).astype(BF)
        return carry

    lax.fori_loop(0, CELLS // TILE, tile, 0)

    lhs = jnp.concatenate([vol_t[...], turned[...]], axis=0)
    offset_of = (1 - z, 2 - z, 2 * z)
    couples = [((b, 0), (b, 1)) for b in range(3)] + [((0, 2), (1, 2)), ((2, 2),)]
    for couple in couples:
        rhs = jnp.concatenate(
            [
                shifts[2 - c, (2 - b) * COLS : (2 - b) * COLS + CELLS, :]
                for b, c in couple
            ],
            axis=1,
        )
        got = jnp.dot(lhs, rhs, preferred_element_type=F32)
        for k, (b, c) in enumerate(couple):
            for p in range(3):
                for i in range(4):
                    chunk = 4 * tap(offset_of[p], b, c) + i
                    group = chunk // 27
                    at = place(core, group, chunk - 27 * group)
                    first = p * C + i * CHUNK
                    block = got[first : first + CHUNK, k * C : (k + 1) * C]
                    part[at] = block if begun is None else begun[at] + block
    for i in range(CELLS // TILE):
        leave(i).wait()


def near_kernel(core_ref, *refs):
    for core in range(2):

        @pl.when(core_ref[0] == core)
        def _():
            side(core, 1 - core, None, *refs)


def far_kernel(
    core_ref, begun, halo, weight, inner, upstream, vol_t, grad, part, sent, *scratch
):
    for core in range(2):

        @pl.when(core_ref[0] == core)
        def _():
            side(
                core,
                core,
                begun,
                halo,
                weight,
                inner,
                upstream,
                vol_t,
                grad,
                part,
                *scratch,
            )

    sent[...] = part[64:128].astype(BF)


PLANE = jax.ShapeDtypeStruct((CELLS, C), BF)
PART = (4 * 32, CHUNK, C)
SIDE = [
    pltpu.VMEM((3, PADDED, C), BF),
    pltpu.VMEM((9 * C, C), BF),
    pltpu.VMEM((3, PADDED, C), BF),
    pltpu.VMEM((C, CELLS), BF),
    pltpu.SemaphoreType.DMA,
    pltpu.SemaphoreType.DMA((CELLS // TILE,)),
]


def near_side(core, halo, weight, inner, upstream, vol_t):
    return pl.pallas_call(
        near_kernel,
        out_shape=[PLANE, jax.ShapeDtypeStruct(PART, F32)],
        in_specs=[SMEM, VMEM, HBM, VMEM, VMEM, VMEM],
        out_specs=[HBM, VMEM],
        scratch_shapes=SIDE,
        compiler_params=PARAMS,
        cost_estimate=cost(2 * CELLS * 3456 * 256, 5 << 20, CELLS * 128),
        name="near_side",
    )(core, halo, weight, inner, upstream, vol_t)


def far_side(core, begun, halo, weight, inner, upstream, vol_t):
    return pl.pallas_call(
        far_kernel,
        out_shape=[
            PLANE,
            jax.ShapeDtypeStruct(PART, F32),
            jax.ShapeDtypeStruct((64, CHUNK, C), BF),
        ],
        in_specs=[SMEM, VMEM, VMEM, HBM, VMEM, VMEM, VMEM],
        out_specs=[HBM, VMEM, VMEM],
        scratch_shapes=SIDE,
        compiler_params=PARAMS,
        cost_estimate=cost(2 * CELLS * 3456 * 256, 5 << 20, CELLS * 128),
        name="far_side",
    )(core, begun, halo, weight, inner, upstream, vol_t)


def halves_kernel(part, other, half, held, sems):
    copies = []
    for k in range(4):
        rows = slice(k * 16, (k + 1) * 16)
        held[rows] = (part[rows] + other[rows].astype(F32)).astype(BF)
        copy = pltpu.make_async_copy(held.at[rows], half.at[rows], sems.at[k])
        copy.start()
        copies.append(copy)
    for copy in copies:
        copy.wait()


def both_halves(part, other):
    return pl.pallas_call(
        halves_kernel,
        out_shape=jax.ShapeDtypeStruct((64, CHUNK, C), BF),
        in_specs=[VMEM, VMEM],
        out_specs=HBM,
        scratch_shapes=[
            pltpu.VMEM((64, CHUNK, C), BF),
            pltpu.SemaphoreType.DMA((4,)),
        ],
        compiler_params=SMALL,
        cost_estimate=cost(1 << 18, 2 << 20),
        name="both_halves",
    )(part, other)


def inner_back_kernel(
    core_ref, near, far, weight, later, out, field, mixed, held, made, sem, sems
):
    copy = fetched(weight, held, sem)
    shifted_columns(ordered(core_ref[0], near, far), field, 0, False)
    copy.wait()
    for b in range(3):
        for c in range(3):
            base = (b * 3 + c) * 256
            for p in range(2):
                for z in range(2):
                    t = tap(1 + z - p, 2 - b, 2 - c)
                    mixed[z * C : (z + 1) * C, base + p * C : base + (p + 1) * C] = (
                        held[t * C : (t + 1) * C, :]
                    )
    tiles = CELLS // TILE

    def leave(i, z):
        rows = pl.ds(pl.multiple_of(i * TILE, TILE), TILE)
        return pltpu.make_async_copy(
            made.at[z, rows, :], out.at[z, rows, :], sems.at[i, z]
        )

    def tile(i, carry):
        at = pl.multiple_of(i * TILE, TILE)
        got = lax.dot_general(
            taps_of(field, at, TILE),
            mixed[...],
            (((1,), (1,)), ((), ())),
            preferred_element_type=F32,
        )
        for z in range(2):
            made[z, pl.ds(at, TILE), :] = got[:, z * C : (z + 1) * C]
            leave(i, z).start()
        return carry

    lax.fori_loop(0, tiles, tile, 0, unroll=True)
    for i in range(tiles):
        for z in range(2):
            leave(i, z).wait()


def inner_back(core, near, far, weight, later):
    return pl.pallas_call(
        inner_back_kernel,
        out_shape=jax.ShapeDtypeStruct((2, CELLS, C), F32),
        in_specs=[SMEM, VMEM, VMEM, HBM, ANY],
        out_specs=HBM,
        scratch_shapes=[
            pltpu.VMEM((3, PADDED, 2 * C), BF),
            pltpu.VMEM((2 * C, 9 * 256), BF),
            pltpu.VMEM((27 * C, C), BF),
            pltpu.VMEM((2, CELLS, C), F32),
            pltpu.SemaphoreType.DMA,
            pltpu.SemaphoreType.DMA((CELLS // TILE, 2)),
        ],
        compiler_params=WHOLE,
        cost_estimate=cost(2 * CELLS * 2304 * 256, 5 << 20),
        name="inner_back",
    )(core, near, far, weight, later)


def outer_back_kernel(at_ref, halo, weight, given, kept, *rest):
    out, field, mixed, held, upstream, inner, made, sems, leave_sems = rest[-9:]
    z = at_ref[0]
    first = pl.multiple_of((2 - 2 * z) * 9 * C, 9 * C)
    copy = fetched(weight.at[pl.ds(first, 9 * C), :], held, sems.at[0])
    kept_copy = fetched(kept.at[z], inner, sems.at[1])
    given_copy = fetched(given.at[z], upstream, sems.at[2])
    shifted_columns([rows_of(halo)], field, 0, False)
    copy.wait()
    for b in range(3):
        for c in range(3):
            base = (b * 3 + c) * C
            t = tap(0, 2 - b, 2 - c)
            mixed[:, base : base + C] = held[t * C : (t + 1) * C, :]
    kept_copy.wait()
    given_copy.wait()
    tiles = CELLS // TILE

    def leave(i):
        rows = pl.ds(pl.multiple_of(i * TILE, TILE), TILE)
        return pltpu.make_async_copy(
            made.at[rows, :], out.at[z, rows, :], leave_sems.at[i]
        )

    def tile(i, carry):
        at = pl.multiple_of(i * TILE, TILE)
        rows = pl.ds(at, TILE)
        got = lax.dot_general(
            taps_of(field, at, TILE),
            mixed[...],
            (((1,), (1,)), ((), ())),
            preferred_element_type=F32,
        )
        made[rows, :] = (
            upstream[rows, :].astype(F32) + (inner[rows, :] + got)
        ).astype(BF)
        leave(i).start()
        return carry

    lax.fori_loop(0, tiles, tile, 0, unroll=True)
    for i in range(tiles):
        leave(i).wait()


def outer_back(name, z, halo, weight, given, inner, *begun):
    return pl.pallas_call(
        outer_back_kernel,
        out_shape=jax.ShapeDtypeStruct((2, CELLS, C), BF),
        in_specs=[SMEM, VMEM] + [HBM] * (3 + len(begun)),
        out_specs=HBM,
        scratch_shapes=[
            pltpu.VMEM((3, PADDED, C), BF),
            pltpu.VMEM((C, 9 * C), BF),
            pltpu.VMEM((9 * C, C), BF),
            pltpu.VMEM((CELLS, C), BF),
            pltpu.VMEM((CELLS, C), F32),
            pltpu.VMEM((CELLS, C), BF),
            pltpu.SemaphoreType.DMA((3,)),
            pltpu.SemaphoreType.DMA((CELLS // TILE,)),
        ],
        input_output_aliases={5: 0} if begun else {},
        compiler_params=LARGE,
        cost_estimate=cost(CELLS * 2304 * 256, 3 << 20),
        name=name,
    )(z, halo, weight, given, inner, *begun)


def planes_kernel(core_ref, vol, near, far):
    core = core_ref[0]
    far[...] = vol[core]
    near[...] = vol[1 - core]


def both_planes(core, vol):
    plane = jax.ShapeDtypeStruct((CELLS, C), BF)
    return pl.pallas_call(
        planes_kernel,
        out_shape=[plane, plane],
        in_specs=[SMEM, VMEM],
        out_specs=[VMEM, VMEM],
        compiler_params=SMALL,
        cost_estimate=cost(0, 2 << 20),
        name="both_planes",
    )(core, vol)


def first_rows_kernel(whole, out, wide, sems):
    rows = out.shape[0]
    step = rows // 4
    copies = []
    for k in range(4):
        part = slice(k * step, (k + 1) * step)
        wide[part, :] = whole[part, :].astype(F32)
        copy = pltpu.make_async_copy(wide.at[part, :], out.at[part, :], sems.at[k])
        copy.start()
        copies.append(copy)
    for copy in copies:
        copy.wait()


def first_rows(whole, rows):
    return pl.pallas_call(
        first_rows_kernel,
        out_shape=jax.ShapeDtypeStruct((rows, C), F32),
        in_specs=[VMEM],
        out_specs=ANY,
        scratch_shapes=[pltpu.VMEM((rows, C), F32), pltpu.SemaphoreType.DMA((4,))],
        compiler_params=SMALL,
        cost_estimate=cost(0, 1 << 20),
        name="first_rows",
    )(whole)


def mix_kernel(got, out):
    for group in range(4):
        total = got[0, group].astype(F32)
        for k in range(1, 16):
            total += got[k, group].astype(F32)
        out[group] = total.astype(BF)
        out[4 + group] = total.astype(BF)


def mixed_rows(got):
    return pl.pallas_call(
        mix_kernel,
        out_shape=jax.ShapeDtypeStruct((8, CHUNK, C), BF),
        in_specs=[VMEM],
        out_specs=VMEM,
        compiler_params=SMALL,
        cost_estimate=cost(1 << 18, 1 << 20),
        name="mixed_rows",
    )(got)


def step_kernel(at_ref, got, first, second, out):
    total = got[0].astype(F32)
    for k in range(1, 8):
        total += got[k].astype(F32)
    at = pl.multiple_of(at_ref[0], CHUNK)
    rows = pl.ds(at, CHUNK)
    step = adam(total, first[rows, :], second[rows, :])
    step = step.astype(BF)
    for k in range(OWNERS):
        out[k] = step


def spread_step(at, got, first, second):
    return pl.pallas_call(
        step_kernel,
        out_shape=jax.ShapeDtypeStruct((OWNERS, CHUNK, C), BF),
        in_specs=[SMEM] + [VMEM] * 3,
        out_specs=VMEM,
        compiler_params=SMALL,
        cost_estimate=cost(1 << 18, 1 << 20),
        name="spread_step",
    )(at, got, first, second)


def adam(grad, first, second):
    m_new = beta_one * first + (1.0 - beta_one) * grad
    v_new = beta_two * second + (1.0 - beta_two) * grad * grad
    return (
        m_new
        / (1.0 - beta_one**ADAM_STEP)
        / (jnp.sqrt(v_new / (1.0 - beta_two**ADAM_STEP)) + eps_adam)
    )


def from_neighbours(near, far):
    size = lax.axis_size(SPACE)
    pairs = [(i, i + 1) for i in range(1, size - 1, 2)]
    far_halo = lax.ppermute(far, SPACE, pairs + [(j, i) for i, j in pairs])
    near_halo = lax.ppermute(near, "core", [(0, 1), (1, 0)])
    return near_halo, far_halo


def body(volume, upstream, weight, first_moment, second_moment):
    vol = volume.reshape(2, CELLS, C)
    up = upstream.reshape(2, CELLS, C)
    core = lax.axis_index("core")
    at_core = core.reshape(1)
    near, far = both_planes(at_core, vol)
    near_halo, far_halo = from_neighbours(near, far)
    inner, vol_t = inner_conv(at_core, near, far, weight)
    near, part = near_side(at_core, near_halo, weight, inner, up, vol_t)
    far, part, sent = far_side(at_core, part, far_halo, weight, inner, up, vol_t)

    rows = first_moment.shape[0]
    other = lax.ppermute(sent, "core", [(0, 1), (1, 0)])
    half = both_halves(part, other).reshape(16, 4, CHUNK, C)
    got = lax.all_to_all(half, ("x", "y"), 0, 0)
    local = inner_back(at_core, near, far, weight, half)
    far_sent, local = lax.optimization_barrier((far, local))
    grad_near, grad_far = from_neighbours(near, far_sent)
    got, local = lax.optimization_barrier((got, local))
    part = mixed_rows(got)
    grad_near, part = lax.optimization_barrier((grad_near, part))
    got = lax.all_to_all(part, ("zl", "sample"), 0, 0)
    half_done = outer_back("near_back", 1 - at_core, grad_near, weight, up, local)
    got, half_done = lax.optimization_barrier((got, half_done))
    owner = core * 16 + lax.axis_index("x") * 4 + lax.axis_index("y")
    at = jnp.minimum(owner * CHUNK, rows - CHUNK).reshape(1)
    step = spread_step(at, got, first_moment, second_moment)
    whole = lax.all_to_all(step, ("core", "x", "y"), 0, 0)
    grad_volume = outer_back(
        "far_back", at_core, grad_far, weight, up, local, half_done
    )
    direction = first_rows(whole.reshape(OWNERS * CHUNK, C), rows)
    return (grad_volume.reshape(volume.shape), direction)


def solution(mesh):
    fine = Mesh(
        mesh.devices.reshape(4, 4, 2, 2, 4), ("x", "y", "zl", "core", "sample")
    )
    field = P("sample", SPACE, None, None, None)
    return jax.shard_map(
        body,
        mesh=fine,
        in_specs=(field, field, P(), P("sample", None), P("sample", None)),
        out_specs=(field, P("sample", None)),
        check_vma=False,
    )
```

```python
import functools
import jax
import jax.numpy as jnp
from jax import lax
from jax.experimental import pallas as pl
from jax.experimental.pallas import tpu as pltpu
from jax.sharding import Mesh, PartitionSpec as P

ADAM_STEP = 10


beta_one = 0.9
beta_two = 0.999
eps_adam = 1e-08

SPACE = ("x", "y", "zl", "core")
CHUNK = 32
OWNERS = 32
C = 128
COLS = 64
ROWS = 32
CELLS = ROWS * COLS
PADDED = CELLS + 2 * COLS
STRIP = 256
TILE = 512
SIDE_TILE = 1024
BF = jnp.bfloat16
F32 = jnp.float32
VMEM = pl.BlockSpec(memory_space=pltpu.VMEM)
ANY = pl.BlockSpec(memory_space=pl.ANY)
HBM = pl.BlockSpec(memory_space=pltpu.HBM)
SMEM = pl.BlockSpec(memory_space=pltpu.SMEM)
WHOLE = pltpu.CompilerParams(vmem_limit_bytes=60 * 1024 * 1024)
LARGE = pltpu.CompilerParams(vmem_limit_bytes=62 * 1024 * 1024 + 512 * 1024)
INNER = pltpu.CompilerParams(vmem_limit_bytes=44 * 1024 * 1024)
SMALL = pltpu.CompilerParams(vmem_limit_bytes=4 * 1024 * 1024)
PARAMS = pltpu.CompilerParams(vmem_limit_bytes=32 * 1024 * 1024)


def cost(flops, moved, special=0):
    return pl.CostEstimate(flops=flops, bytes_accessed=moved, transcendentals=special)


def shifted_columns(planes, out, first, flip):
    width = 128 * len(planes)
    blank = jnp.zeros((COLS, width), BF)
    cols = slice(first, first + width)
    for c in range(3):
        out[c, 0:COLS, cols] = blank
        out[c, PADDED - COLS : PADDED, cols] = blank
    before, after = (2, 0) if flip else (0, 2)

    def strip(i, carry):
        at = pl.multiple_of(i * STRIP, STRIP)
        to = pl.ds(pl.multiple_of(at + COLS, COLS), STRIP)
        col = lax.broadcasted_iota(jnp.int32, (STRIP, C), 0) & (COLS - 1)
        for k, plane in enumerate(planes):
            cols = slice(first + k * C, first + (k + 1) * C)
            here = plane(pl.ds(at, STRIP))
            wide = here.astype(F32)
            out[1, to, cols] = here
            out[before, to, cols] = jnp.where(
                col == 0, 0.0, pltpu.roll(wide, 1, 0)
            ).astype(BF)
            out[after, to, cols] = jnp.where(
                col == COLS - 1, 0.0, pltpu.roll(wide, STRIP - 1, 0)
            ).astype(BF)
        return carry

    lax.fori_loop(0, CELLS // STRIP, strip, 0)


def transposed(plane, out, first):
    for at in range(0, CELLS, TILE):
        out[first : first + C, at : at + TILE] = jnp.transpose(
            plane(pl.ds(at, TILE))
        )


def rows_of(plane):
    return lambda rows: plane[rows, :]


def ordered(core, near, far):
    def pick(first, second):
        return lambda rows: jnp.where(core == 0, first[rows, :], second[rows, :])

    return pick(far, near), pick(near, far)


def fetched(source, held, sem):
    copy = pltpu.make_async_copy(source, held, sem)
    copy.start()
    return copy


def tap(a, b, c):
    return (a * 3 + b) * 3 + c


def taps_of(field, at, rows):
    return jnp.concatenate(
        [
            field[c, pl.ds(pl.multiple_of(at + b * COLS, COLS), rows), :]
            for b in range(3)
            for c in range(3)
        ],
        axis=1,
    )


def inner_kernel(core_ref, near, far, weight, out, vol_t, field, mixed, held, sem):
    copy = fetched(weight, held, sem)
    planes = ordered(core_ref[0], near, far)
    shifted_columns(planes, field, 0, False)
    copy.wait()
    for b in range(3):
        for c in range(3):
            base = (b * 3 + c) * 256
            for p in range(2):
                for z in range(2):
                    t = tap(1 + p - z, b, c)
                    mixed[base + p * C : base + (p + 1) * C, z * C : (z + 1) * C] = (
                        held[t * C : (t + 1) * C, :]
                    )

    def tile(i, carry):
        at = pl.multiple_of(i * TILE, TILE)
        got = jnp.dot(taps_of(field, at, TILE), mixed[...], preferred_element_type=F32)
        out[0, pl.ds(at, TILE), :] = got[:, 0:C]
        out[1, pl.ds(at, TILE), :] = got[:, C : 2 * C]
        return carry

    lax.fori_loop(0, CELLS // TILE, tile, 0, unroll=True)
    for p in range(2):
        transposed(planes[p], vol_t, p * C)


def inner_conv(core, near, far, weight):
    return pl.pallas_call(
        inner_kernel,
        out_shape=[
            jax.ShapeDtypeStruct((2, CELLS, C), F32),
            jax.ShapeDtypeStruct((2 * C, CELLS), BF),
        ],
        in_specs=[SMEM, VMEM, VMEM, HBM],
        out_specs=[VMEM] * 2,
        scratch_shapes=[
            pltpu.VMEM((3, PADDED, 2 * C), BF),
            pltpu.VMEM((9 * 256, 2 * C), BF),
            pltpu.VMEM((27 * C, C), BF),
            pltpu.SemaphoreType.DMA,
        ],
        compiler_params=INNER,
        cost_estimate=cost(2 * CELLS * 2304 * 256, 5 << 20),
        name="inner_conv",
    )(core, near, far, weight)


def place(core, group, owner):
    half = 0 if owner // 16 == core else 64
    return half + (owner % 16) * 4 + group


def side(
    core,
    z,
    begun,
    halo,
    weight,
    inner,
    upstream,
    vol_t,
    grad,
    part,
    field,
    held,
    shifts,
    turned,
    sem,
    leave_sems,
):
    first = z * 18 * C
    copy = fetched(weight.at[first : first + 9 * C, :], held, sem)
    shifted_columns([rows_of(halo)], field, 0, False)
    transposed(rows_of(halo), turned, 0)
    blank = jnp.zeros((COLS, C), BF)
    for c in range(3):
        shifts[c, 0:COLS, :] = blank
        shifts[c, PADDED - COLS : PADDED, :] = blank
    copy.wait()
    for owner in range(27, 32):
        for group in range(4):
            part[place(core, group, owner)] = jnp.zeros((CHUNK, C), F32)

    def leave(i):
        at = pl.multiple_of(i * SIDE_TILE, SIDE_TILE)
        held_at = pl.ds(pl.multiple_of(at + COLS, COLS), SIDE_TILE)
        return pltpu.make_async_copy(
            shifts.at[1, held_at, :], grad.at[pl.ds(at, SIDE_TILE), :], leave_sems.at[i]
        )

    def tile(i, carry):
        at = pl.multiple_of(i * SIDE_TILE, SIDE_TILE)
        rows = pl.ds(at, SIDE_TILE)
        to = pl.ds(pl.multiple_of(at + COLS, COLS), SIDE_TILE)
        preact = inner[z, rows, :] + jnp.dot(
            taps_of(field, at, SIDE_TILE), held[...], preferred_element_type=F32
        )
        s = jax.nn.sigmoid(preact)
        slopes = s * (1.0 + preact * (1.0 - s))
        here = (upstream[z, rows, :].astype(F32) * slopes).astype(BF)
        wide = here.astype(F32)
        col = lax.broadcasted_iota(jnp.int32, (SIDE_TILE, C), 0) & (COLS - 1)
        shifts[1, to, :] = here
        leave(i).start()
        shifts[0, to, :] = jnp.where(col == 0, 0.0, pltpu.roll(wide, 1, 0)).astype(BF)
        shifts[2, to, :] = jnp.where(
            col == COLS - 1, 0.0, pltpu.roll(wide, SIDE_TILE - 1, 0)
        ).astype(BF)
        return carry

    lax.fori_loop(0, CELLS // SIDE_TILE, tile, 0)

    lhs = jnp.concatenate([vol_t[...], turned[...]], axis=0)
    offset_of = (1 - z, 2 - z, 2 * z)
    couples = [((b, 0), (b, 1)) for b in range(3)] + [((0, 2), (1, 2)), ((2, 2),)]
    for couple in couples:
        rhs = jnp.concatenate(
            [
                shifts[2 - c, (2 - b) * COLS : (2 - b) * COLS + CELLS, :]
                for b, c in couple
            ],
            axis=1,
        )
        got = jnp.dot(lhs, rhs, preferred_element_type=F32)
        for k, (b, c) in enumerate(couple):
            for p in range(3):
                for i in range(4):
                    chunk = 4 * tap(offset_of[p], b, c) + i
                    group = chunk // 27
                    at = place(core, group, chunk - 27 * group)
                    first = p * C + i * CHUNK
                    block = got[first : first + CHUNK, k * C : (k + 1) * C]
                    part[at] = block if begun is None else begun[at] + block
    for i in range(CELLS // SIDE_TILE):
        leave(i).wait()


def near_kernel(core_ref, *refs):
    for core in range(2):

        @pl.when(core_ref[0] == core)
        def _():
            side(core, 1 - core, None, *refs)


def far_kernel(
    core_ref, begun, halo, weight, inner, upstream, vol_t, grad, part, sent, *scratch
):
    for core in range(2):

        @pl.when(core_ref[0] == core)
        def _():
            side(
                core,
                core,
                begun,
                halo,
                weight,
                inner,
                upstream,
                vol_t,
                grad,
                part,
                *scratch,
            )

    sent[...] = part[64:128].astype(BF)


PLANE = jax.ShapeDtypeStruct((CELLS, C), BF)
PART = (4 * 32, CHUNK, C)
SIDE = [
    pltpu.VMEM((3, PADDED, C), BF),
    pltpu.VMEM((9 * C, C), BF),
    pltpu.VMEM((3, PADDED, C), BF),
    pltpu.VMEM((C, CELLS), BF),
    pltpu.SemaphoreType.DMA,
    pltpu.SemaphoreType.DMA((CELLS // SIDE_TILE,)),
]


def near_side(core, halo, weight, inner, upstream, vol_t):
    return pl.pallas_call(
        near_kernel,
        out_shape=[PLANE, jax.ShapeDtypeStruct(PART, F32)],
        in_specs=[SMEM, VMEM, HBM, VMEM, VMEM, VMEM],
        out_specs=[HBM, VMEM],
        scratch_shapes=SIDE,
        compiler_params=PARAMS,
        cost_estimate=cost(2 * CELLS * 3456 * 256, 5 << 20, CELLS * 128),
        name="near_side",
    )(core, halo, weight, inner, upstream, vol_t)


def far_side(core, begun, halo, weight, inner, upstream, vol_t):
    return pl.pallas_call(
        far_kernel,
        out_shape=[
            PLANE,
            jax.ShapeDtypeStruct(PART, F32),
            jax.ShapeDtypeStruct((64, CHUNK, C), BF),
        ],
        in_specs=[SMEM, VMEM, VMEM, HBM, VMEM, VMEM, VMEM],
        out_specs=[HBM, VMEM, VMEM],
        scratch_shapes=SIDE,
        compiler_params=PARAMS,
        cost_estimate=cost(2 * CELLS * 3456 * 256, 5 << 20, CELLS * 128),
        name="far_side",
    )(core, begun, halo, weight, inner, upstream, vol_t)


def halves_kernel(part, other, half):
    half[...] = (part[0:64] + other[...].astype(F32)).astype(BF)


def both_halves(part, other):
    return pl.pallas_call(
        halves_kernel,
        out_shape=jax.ShapeDtypeStruct((64, CHUNK, C), BF),
        in_specs=[VMEM, VMEM],
        out_specs=VMEM,
        compiler_params=SMALL,
        cost_estimate=cost(1 << 18, 2 << 20),
        name="both_halves",
    )(part, other)


def inner_back_kernel(
    core_ref, near, far, weight, later, out, field, mixed, held, made, sem, sems
):
    copy = fetched(weight, held, sem)
    shifted_columns(ordered(core_ref[0], near, far), field, 0, False)
    copy.wait()
    for b in range(3):
        for c in range(3):
            base = (b * 3 + c) * 256
            for p in range(2):
                for z in range(2):
                    t = tap(1 + z - p, 2 - b, 2 - c)
                    mixed[z * C : (z + 1) * C, base + p * C : base + (p + 1) * C] = (
                        held[t * C : (t + 1) * C, :]
                    )
    tiles = CELLS // TILE

    def leave(i, z):
        rows = pl.ds(pl.multiple_of(i * TILE, TILE), TILE)
        return pltpu.make_async_copy(
            made.at[z, rows, :], out.at[z, rows, :], sems.at[i, z]
        )

    def tile(i, carry):
        at = pl.multiple_of(i * TILE, TILE)
        got = lax.dot_general(
            taps_of(field, at, TILE),
            mixed[...],
            (((1,), (1,)), ((), ())),
            preferred_element_type=F32,
        )
        for z in range(2):
            made[z, pl.ds(at, TILE), :] = got[:, z * C : (z + 1) * C]
            leave(i, z).start()
        return carry

    lax.fori_loop(0, tiles, tile, 0, unroll=True)
    for i in range(tiles):
        for z in range(2):
            leave(i, z).wait()


def inner_back(core, near, far, weight, later):
    return pl.pallas_call(
        inner_back_kernel,
        out_shape=jax.ShapeDtypeStruct((2, CELLS, C), F32),
        in_specs=[SMEM, VMEM, VMEM, HBM, ANY],
        out_specs=HBM,
        scratch_shapes=[
            pltpu.VMEM((3, PADDED, 2 * C), BF),
            pltpu.VMEM((2 * C, 9 * 256), BF),
            pltpu.VMEM((27 * C, C), BF),
            pltpu.VMEM((2, CELLS, C), F32),
            pltpu.SemaphoreType.DMA,
            pltpu.SemaphoreType.DMA((CELLS // TILE, 2)),
        ],
        compiler_params=WHOLE,
        cost_estimate=cost(2 * CELLS * 2304 * 256, 5 << 20),
        name="inner_back",
    )(core, near, far, weight, later)


def outer_back_kernel(at_ref, halo, weight, given, kept, *rest):
    out, field, mixed, held, upstream, inner, made, sems, leave_sems = rest[-9:]
    z = at_ref[0]
    first = pl.multiple_of((2 - 2 * z) * 9 * C, 9 * C)
    copy = fetched(weight.at[pl.ds(first, 9 * C), :], held, sems.at[0])
    kept_copy = fetched(kept.at[z], inner, sems.at[1])
    given_copy = fetched(given.at[z], upstream, sems.at[2])
    shifted_columns([rows_of(halo)], field, 0, False)
    copy.wait()
    for b in range(3):
        for c in range(3):
            base = (b * 3 + c) * C
            t = tap(0, 2 - b, 2 - c)
            mixed[:, base : base + C] = held[t * C : (t + 1) * C, :]
    kept_copy.wait()
    given_copy.wait()
    tiles = CELLS // TILE

    def leave(i):
        rows = pl.ds(pl.multiple_of(i * TILE, TILE), TILE)
        return pltpu.make_async_copy(
            made.at[rows, :], out.at[z, rows, :], leave_sems.at[i]
        )

    def tile(i, carry):
        at = pl.multiple_of(i * TILE, TILE)
        rows = pl.ds(at, TILE)
        got = lax.dot_general(
            taps_of(field, at, TILE),
            mixed[...],
            (((1,), (1,)), ((), ())),
            preferred_element_type=F32,
        )
        made[rows, :] = (
            upstream[rows, :].astype(F32) + (inner[rows, :] + got)
        ).astype(BF)
        leave(i).start()
        return carry

    lax.fori_loop(0, tiles, tile, 0, unroll=True)
    for i in range(tiles):
        leave(i).wait()


def outer_back(name, z, halo, weight, given, inner, *begun):
    return pl.pallas_call(
        outer_back_kernel,
        out_shape=jax.ShapeDtypeStruct((2, CELLS, C), BF),
        in_specs=[SMEM, VMEM] + [HBM] * (3 + len(begun)),
        out_specs=HBM,
        scratch_shapes=[
            pltpu.VMEM((3, PADDED, C), BF),
            pltpu.VMEM((C, 9 * C), BF),
            pltpu.VMEM((9 * C, C), BF),
            pltpu.VMEM((CELLS, C), BF),
            pltpu.VMEM((CELLS, C), F32),
            pltpu.VMEM((CELLS, C), BF),
            pltpu.SemaphoreType.DMA((3,)),
            pltpu.SemaphoreType.DMA((CELLS // TILE,)),
        ],
        input_output_aliases={5: 0} if begun else {},
        compiler_params=LARGE,
        cost_estimate=cost(CELLS * 2304 * 256, 3 << 20),
        name=name,
    )(z, halo, weight, given, inner, *begun)


def planes_kernel(core_ref, vol, near, far):
    core = core_ref[0]
    far[...] = vol[core]
    near[...] = vol[1 - core]


def both_planes(core, vol):
    plane = jax.ShapeDtypeStruct((CELLS, C), BF)
    return pl.pallas_call(
        planes_kernel,
        out_shape=[plane, plane],
        in_specs=[SMEM, VMEM],
        out_specs=[VMEM, VMEM],
        compiler_params=SMALL,
        cost_estimate=cost(0, 2 << 20),
        name="both_planes",
    )(core, vol)


def first_rows_kernel(whole, out, wide, sems):
    rows = out.shape[0]
    step = rows // 4
    copies = []
    for k in range(4):
        part = slice(k * step, (k + 1) * step)
        wide[part, :] = whole[part, :].astype(F32)
        copy = pltpu.make_async_copy(wide.at[part, :], out.at[part, :], sems.at[k])
        copy.start()
        copies.append(copy)
    for copy in copies:
        copy.wait()


def first_rows(whole, rows):
    return pl.pallas_call(
        first_rows_kernel,
        out_shape=jax.ShapeDtypeStruct((rows, C), F32),
        in_specs=[VMEM],
        out_specs=ANY,
        scratch_shapes=[pltpu.VMEM((rows, C), F32), pltpu.SemaphoreType.DMA((4,))],
        compiler_params=SMALL,
        cost_estimate=cost(0, 1 << 20),
        name="first_rows",
    )(whole)


def mix_kernel(got, out):
    for group in range(4):
        total = got[0, group].astype(F32)
        for k in range(1, 16):
            total += got[k, group].astype(F32)
        out[group] = total.astype(BF)
        out[4 + group] = total.astype(BF)


def mixed_rows(got):
    return pl.pallas_call(
        mix_kernel,
        out_shape=jax.ShapeDtypeStruct((8, CHUNK, C), BF),
        in_specs=[VMEM],
        out_specs=VMEM,
        compiler_params=SMALL,
        cost_estimate=cost(1 << 18, 1 << 20),
        name="mixed_rows",
    )(got)


def step_kernel(at_ref, got, first, second, out):
    total = got[0].astype(F32)
    for k in range(1, 8):
        total += got[k].astype(F32)
    at = pl.multiple_of(at_ref[0], CHUNK)
    rows = pl.ds(at, CHUNK)
    step = adam(total, first[rows, :], second[rows, :])
    step = step.astype(BF)
    for k in range(OWNERS):
        out[k] = step


def spread_step(at, got, first, second):
    return pl.pallas_call(
        step_kernel,
        out_shape=jax.ShapeDtypeStruct((OWNERS, CHUNK, C), BF),
        in_specs=[SMEM] + [VMEM] * 3,
        out_specs=VMEM,
        compiler_params=SMALL,
        cost_estimate=cost(1 << 18, 1 << 20),
        name="spread_step",
    )(at, got, first, second)


def adam(grad, first, second):
    m_new = beta_one * first + (1.0 - beta_one) * grad
    v_new = beta_two * second + (1.0 - beta_two) * grad * grad
    return (
        m_new
        / (1.0 - beta_one**ADAM_STEP)
        / (jnp.sqrt(v_new / (1.0 - beta_two**ADAM_STEP)) + eps_adam)
    )


def from_neighbours(near, far):
    size = lax.axis_size(SPACE)
    pairs = [(i, i + 1) for i in range(1, size - 1, 2)]
    far_halo = lax.ppermute(far, SPACE, pairs + [(j, i) for i, j in pairs])
    near_halo = lax.ppermute(near, "core", [(0, 1), (1, 0)])
    return near_halo, far_halo


def body(volume, upstream, weight, first_moment, second_moment):
    vol = volume.reshape(2, CELLS, C)
    up = upstream.reshape(2, CELLS, C)
    core = lax.axis_index("core")
    at_core = core.reshape(1)
    near, far = both_planes(at_core, vol)
    near_halo, far_halo = from_neighbours(near, far)
    inner, vol_t = inner_conv(at_core, near, far, weight)
    near, part = near_side(at_core, near_halo, weight, inner, up, vol_t)
    far, part, sent = far_side(at_core, part, far_halo, weight, inner, up, vol_t)

    rows = first_moment.shape[0]
    other = lax.ppermute(sent, "core", [(0, 1), (1, 0)])
    half = both_halves(part, other).reshape(16, 4, CHUNK, C)
    got = lax.all_to_all(half, ("x", "y"), 0, 0)
    grad_near, grad_far = from_neighbours(near, far)
    local = inner_back(at_core, near, far, weight, half)
    got, local = lax.optimization_barrier((got, local))
    part = mixed_rows(got)
    grad_near, part = lax.optimization_barrier((grad_near, part))
    got = lax.all_to_all(part, ("zl", "sample"), 0, 0)
    half_done = outer_back("near_back", 1 - at_core, grad_near, weight, up, local)
    got, half_done = lax.optimization_barrier((got, half_done))
    owner = core * 16 + lax.axis_index("x") * 4 + lax.axis_index("y")
    at = jnp.minimum(owner * CHUNK, rows - CHUNK).reshape(1)
    step = spread_step(at, got, first_moment, second_moment)
    whole = lax.all_to_all(step, ("core", "x", "y"), 0, 0)
    grad_volume = outer_back(
        "far_back", at_core, grad_far, weight, up, local, half_done
    )
    direction = first_rows(whole.reshape(OWNERS * CHUNK, C), rows)
    return (grad_volume.reshape(volume.shape), direction)


def solution(mesh):
    fine = Mesh(
        mesh.devices.reshape(4, 4, 2, 2, 4), ("x", "y", "zl", "core", "sample")
    )
    field = P("sample", SPACE, None, None, None)
    return jax.shard_map(
        body,
        mesh=fine,
        in_specs=(field, field, P(), P("sample", None), P("sample", None)),
        out_specs=(field, P("sample", None)),
        check_vma=False,
    )
```

```python
import functools
import jax
import jax.numpy as jnp
from jax import lax
from jax.experimental import pallas as pl
from jax.experimental.pallas import tpu as pltpu
from jax.sharding import Mesh, PartitionSpec as P

ADAM_STEP = 10


beta_one = 0.9
beta_two = 0.999
eps_adam = 1e-08

SPACE = ("x", "y", "zl", "core")
CHUNK = 32
OWNERS = 32
C = 128
COLS = 64
ROWS = 32
CELLS = ROWS * COLS
PADDED = CELLS + 2 * COLS
STRIP = 256
TILE = 512
SIDE_TILE = 1024
BF = jnp.bfloat16
F32 = jnp.float32
VMEM = pl.BlockSpec(memory_space=pltpu.VMEM)
ANY = pl.BlockSpec(memory_space=pl.ANY)
HBM = pl.BlockSpec(memory_space=pltpu.HBM)
SMEM = pl.BlockSpec(memory_space=pltpu.SMEM)
WHOLE = pltpu.CompilerParams(vmem_limit_bytes=60 * 1024 * 1024)
LARGE = pltpu.CompilerParams(vmem_limit_bytes=62 * 1024 * 1024 + 512 * 1024)
INNER = pltpu.CompilerParams(vmem_limit_bytes=44 * 1024 * 1024)
SMALL = pltpu.CompilerParams(vmem_limit_bytes=4 * 1024 * 1024)
PARAMS = pltpu.CompilerParams(vmem_limit_bytes=32 * 1024 * 1024)


def cost(flops, moved, special=0):
    return pl.CostEstimate(flops=flops, bytes_accessed=moved, transcendentals=special)


def shifted_columns(planes, out, first, flip):
    width = 128 * len(planes)
    blank = jnp.zeros((COLS, width), BF)
    cols = slice(first, first + width)
    for c in range(3):
        out[c, 0:COLS, cols] = blank
        out[c, PADDED - COLS : PADDED, cols] = blank
    before, after = (2, 0) if flip else (0, 2)

    def strip(i, carry):
        at = pl.multiple_of(i * STRIP, STRIP)
        to = pl.ds(pl.multiple_of(at + COLS, COLS), STRIP)
        col = lax.broadcasted_iota(jnp.int32, (STRIP, C), 0) & (COLS - 1)
        for k, plane in enumerate(planes):
            cols = slice(first + k * C, first + (k + 1) * C)
            here = plane(pl.ds(at, STRIP))
            wide = here.astype(F32)
            out[1, to, cols] = here
            out[before, to, cols] = jnp.where(
                col == 0, 0.0, pltpu.roll(wide, 1, 0)
            ).astype(BF)
            out[after, to, cols] = jnp.where(
                col == COLS - 1, 0.0, pltpu.roll(wide, STRIP - 1, 0)
            ).astype(BF)
        return carry

    lax.fori_loop(0, CELLS // STRIP, strip, 0)


def transposed(plane, out, first):
    for at in range(0, CELLS, TILE):
        out[first : first + C, at : at + TILE] = jnp.transpose(
            plane(pl.ds(at, TILE))
        )


def rows_of(plane):
    return lambda rows: plane[rows, :]


def ordered(core, near, far):
    def pick(first, second):
        return lambda rows: jnp.where(core == 0, first[rows, :], second[rows, :])

    return pick(far, near), pick(near, far)


def fetched(source, held, sem):
    copy = pltpu.make_async_copy(source, held, sem)
    copy.start()
    return copy


def tap(a, b, c):
    return (a * 3 + b) * 3 + c


def taps_of(field, at, rows):
    return jnp.concatenate(
        [
            field[c, pl.ds(pl.multiple_of(at + b * COLS, COLS), rows), :]
            for b in range(3)
            for c in range(3)
        ],
        axis=1,
    )


def inner_kernel(core_ref, near, far, weight, out, vol_t, field, mixed, held, sem):
    copy = fetched(weight, held, sem)
    planes = ordered(core_ref[0], near, far)
    shifted_columns(planes, field, 0, False)
    copy.wait()
    for b in range(3):
        for c in range(3):
            base = (b * 3 + c) * 256
            for p in range(2):
                for z in range(2):
                    t = tap(1 + p - z, b, c)
                    mixed[base + p * C : base + (p + 1) * C, z * C : (z + 1) * C] = (
                        held[t * C : (t + 1) * C, :]
                    )

    def tile(i, carry):
        at = pl.multiple_of(i * TILE, TILE)
        got = jnp.dot(taps_of(field, at, TILE), mixed[...], preferred_element_type=F32)
        out[0, pl.ds(at, TILE), :] = got[:, 0:C]
        out[1, pl.ds(at, TILE), :] = got[:, C : 2 * C]
        return carry

    lax.fori_loop(0, CELLS // TILE, tile, 0, unroll=True)
    for p in range(2):
        transposed(planes[p], vol_t, p * C)


def inner_conv(core, near, far, weight):
    return pl.pallas_call(
        inner_kernel,
        out_shape=[
            jax.ShapeDtypeStruct((2, CELLS, C), F32),
            jax.ShapeDtypeStruct((2 * C, CELLS), BF),
        ],
        in_specs=[SMEM, VMEM, VMEM, HBM],
        out_specs=[VMEM] * 2,
        scratch_shapes=[
            pltpu.VMEM((3, PADDED, 2 * C), BF),
            pltpu.VMEM((9 * 256, 2 * C), BF),
            pltpu.VMEM((27 * C, C), BF),
            pltpu.SemaphoreType.DMA,
        ],
        compiler_params=INNER,
        cost_estimate=cost(2 * CELLS * 2304 * 256, 5 << 20),
        name="inner_conv",
    )(core, near, far, weight)


def place(core, group, owner):
    half = 0 if owner // 16 == core else 64
    return half + (owner % 16) * 4 + group


def side(
    core,
    z,
    begun,
    halo,
    weight,
    inner,
    upstream,
    vol_t,
    grad,
    part,
    field,
    held,
    shifts,
    turned,
    sem,
    leave_sems,
):
    first = z * 18 * C
    copy = fetched(weight.at[first : first + 9 * C, :], held, sem)
    shifted_columns([rows_of(halo)], field, 0, False)
    transposed(rows_of(halo), turned, 0)
    blank = jnp.zeros((COLS, C), BF)
    for c in range(3):
        shifts[c, 0:COLS, :] = blank
        shifts[c, PADDED - COLS : PADDED, :] = blank
    copy.wait()
    for owner in range(27, 32):
        for group in range(4):
            part[place(core, group, owner)] = jnp.zeros((CHUNK, C), F32)

    def leave(i):
        at = pl.multiple_of(i * SIDE_TILE, SIDE_TILE)
        held_at = pl.ds(pl.multiple_of(at + COLS, COLS), SIDE_TILE)
        return pltpu.make_async_copy(
            shifts.at[1, held_at, :], grad.at[pl.ds(at, SIDE_TILE), :], leave_sems.at[i]
        )

    def tile(i, carry):
        at = pl.multiple_of(i * SIDE_TILE, SIDE_TILE)
        rows = pl.ds(at, SIDE_TILE)
        to = pl.ds(pl.multiple_of(at + COLS, COLS), SIDE_TILE)
        preact = inner[z, rows, :] + jnp.dot(
            taps_of(field, at, SIDE_TILE), held[...], preferred_element_type=F32
        )
        s = jax.nn.sigmoid(preact)
        slopes = s * (1.0 + preact * (1.0 - s))
        here = (upstream[z, rows, :].astype(F32) * slopes).astype(BF)
        wide = here.astype(F32)
        col = lax.broadcasted_iota(jnp.int32, (SIDE_TILE, C), 0) & (COLS - 1)
        shifts[1, to, :] = here
        leave(i).start()
        shifts[0, to, :] = jnp.where(col == 0, 0.0, pltpu.roll(wide, 1, 0)).astype(BF)
        shifts[2, to, :] = jnp.where(
            col == COLS - 1, 0.0, pltpu.roll(wide, SIDE_TILE - 1, 0)
        ).astype(BF)
        return carry

    lax.fori_loop(0, CELLS // SIDE_TILE, tile, 0)

    lhs = jnp.concatenate([vol_t[...], turned[...]], axis=0)
    offset_of = (1 - z, 2 - z, 2 * z)
    couples = [((b, 0), (b, 1)) for b in range(3)] + [((0, 2), (1, 2)), ((2, 2),)]
    for couple in couples:
        rhs = jnp.concatenate(
            [
                shifts[2 - c, (2 - b) * COLS : (2 - b) * COLS + CELLS, :]
                for b, c in couple
            ],
            axis=1,
        )
        got = jnp.dot(lhs, rhs, preferred_element_type=F32)
        for k, (b, c) in enumerate(couple):
            for p in range(3):
                for i in range(4):
                    chunk = 4 * tap(offset_of[p], b, c) + i
                    group = chunk // 27
                    at = place(core, group, chunk - 27 * group)
                    first = p * C + i * CHUNK
                    block = got[first : first + CHUNK, k * C : (k + 1) * C]
                    part[at] = block if begun is None else begun[at] + block
    for i in range(CELLS // SIDE_TILE):
        leave(i).wait()


def near_kernel(core_ref, *refs):
    for core in range(2):

        @pl.when(core_ref[0] == core)
        def _():
            side(core, 1 - core, None, *refs)


def far_kernel(
    core_ref, begun, halo, weight, inner, upstream, vol_t, grad, part, sent, *scratch
):
    for core in range(2):

        @pl.when(core_ref[0] == core)
        def _():
            side(
                core,
                core,
                begun,
                halo,
                weight,
                inner,
                upstream,
                vol_t,
                grad,
                part,
                *scratch,
            )

    sent[...] = part[64:128].astype(BF)


PLANE = jax.ShapeDtypeStruct((CELLS, C), BF)
PART = (4 * 32, CHUNK, C)
SIDE = [
    pltpu.VMEM((3, PADDED, C), BF),
    pltpu.VMEM((9 * C, C), BF),
    pltpu.VMEM((3, PADDED, C), BF),
    pltpu.VMEM((C, CELLS), BF),
    pltpu.SemaphoreType.DMA,
    pltpu.SemaphoreType.DMA((CELLS // SIDE_TILE,)),
]


def near_side(core, halo, weight, inner, upstream, vol_t):
    return pl.pallas_call(
        near_kernel,
        out_shape=[PLANE, jax.ShapeDtypeStruct(PART, F32)],
        in_specs=[SMEM, VMEM, HBM, VMEM, VMEM, VMEM],
        out_specs=[HBM, VMEM],
        scratch_shapes=SIDE,
        compiler_params=PARAMS,
        cost_estimate=cost(2 * CELLS * 3456 * 256, 5 << 20, CELLS * 128),
        name="near_side",
    )(core, halo, weight, inner, upstream, vol_t)


def far_side(core, begun, halo, weight, inner, upstream, vol_t):
    return pl.pallas_call(
        far_kernel,
        out_shape=[
            PLANE,
            jax.ShapeDtypeStruct(PART, F32),
            jax.ShapeDtypeStruct((64, CHUNK, C), BF),
        ],
        in_specs=[SMEM, VMEM, VMEM, HBM, VMEM, VMEM, VMEM],
        out_specs=[HBM, VMEM, VMEM],
        scratch_shapes=SIDE,
        compiler_params=PARAMS,
        cost_estimate=cost(2 * CELLS * 3456 * 256, 5 << 20, CELLS * 128),
        name="far_side",
    )(core, begun, halo, weight, inner, upstream, vol_t)


def halves_kernel(part, other, half, held, sems):
    copies = []
    for k in range(4):
        rows = slice(k * 16, (k + 1) * 16)
        held[rows] = (part[rows] + other[rows].astype(F32)).astype(BF)
        copy = pltpu.make_async_copy(held.at[rows], half.at[rows], sems.at[k])
        copy.start()
        copies.append(copy)
    for copy in copies:
        copy.wait()


def both_halves(part, other):
    return pl.pallas_call(
        halves_kernel,
        out_shape=jax.ShapeDtypeStruct((64, CHUNK, C), BF),
        in_specs=[VMEM, VMEM],
        out_specs=HBM,
        scratch_shapes=[
            pltpu.VMEM((64, CHUNK, C), BF),
            pltpu.SemaphoreType.DMA((4,)),
        ],
        compiler_params=SMALL,
        cost_estimate=cost(1 << 18, 2 << 20),
        name="both_halves",
    )(part, other)


def inner_back_kernel(
    core_ref, near, far, weight, later, out, field, mixed, held, made, sem, sems
):
    copy = fetched(weight, held, sem)
    shifted_columns(ordered(core_ref[0], near, far), field, 0, False)
    copy.wait()
    for b in range(3):
        for c in range(3):
            base = (b * 3 + c) * 256
            for p in range(2):
                for z in range(2):
                    t = tap(1 + z - p, 2 - b, 2 - c)
                    mixed[z * C : (z + 1) * C, base + p * C : base + (p + 1) * C] = (
                        held[t * C : (t + 1) * C, :]
                    )
    tiles = CELLS // TILE

    def leave(i, z):
        rows = pl.ds(pl.multiple_of(i * TILE, TILE), TILE)
        return pltpu.make_async_copy(
            made.at[z, rows, :], out.at[z, rows, :], sems.at[i, z]
        )

    def tile(i, carry):
        at = pl.multiple_of(i * TILE, TILE)
        got = lax.dot_general(
            taps_of(field, at, TILE),
            mixed[...],
            (((1,), (1,)), ((), ())),
            preferred_element_type=F32,
        )
        for z in range(2):
            made[z, pl.ds(at, TILE), :] = got[:, z * C : (z + 1) * C]
            leave(i, z).start()
        return carry

    lax.fori_loop(0, tiles, tile, 0, unroll=True)
    for i in range(tiles):
        for z in range(2):
            leave(i, z).wait()


def inner_back(core, near, far, weight, later):
    return pl.pallas_call(
        inner_back_kernel,
        out_shape=jax.ShapeDtypeStruct((2, CELLS, C), F32),
        in_specs=[SMEM, VMEM, VMEM, HBM, ANY],
        out_specs=HBM,
        scratch_shapes=[
            pltpu.VMEM((3, PADDED, 2 * C), BF),
            pltpu.VMEM((2 * C, 9 * 256), BF),
            pltpu.VMEM((27 * C, C), BF),
            pltpu.VMEM((2, CELLS, C), F32),
            pltpu.SemaphoreType.DMA,
            pltpu.SemaphoreType.DMA((CELLS // TILE, 2)),
        ],
        compiler_params=WHOLE,
        cost_estimate=cost(2 * CELLS * 2304 * 256, 5 << 20),
        name="inner_back",
    )(core, near, far, weight, later)


def outer_back_kernel(at_ref, halo, weight, given, kept, *rest):
    out, field, mixed, held, upstream, inner, made, sems, leave_sems = rest[-9:]
    z = at_ref[0]
    first = pl.multiple_of((2 - 2 * z) * 9 * C, 9 * C)
    copy = fetched(weight.at[pl.ds(first, 9 * C), :], held, sems.at[0])
    kept_copy = fetched(kept.at[z], inner, sems.at[1])
    given_copy = fetched(given.at[z], upstream, sems.at[2])
    shifted_columns([rows_of(halo)], field, 0, False)
    copy.wait()
    for b in range(3):
        for c in range(3):
            base = (b * 3 + c) * C
            t = tap(0, 2 - b, 2 - c)
            mixed[:, base : base + C] = held[t * C : (t + 1) * C, :]
    kept_copy.wait()
    given_copy.wait()
    tiles = CELLS // TILE

    def leave(i):
        rows = pl.ds(pl.multiple_of(i * TILE, TILE), TILE)
        return pltpu.make_async_copy(
            made.at[rows, :], out.at[z, rows, :], leave_sems.at[i]
        )

    def tile(i, carry):
        at = pl.multiple_of(i * TILE, TILE)
        rows = pl.ds(at, TILE)
        got = lax.dot_general(
            taps_of(field, at, TILE),
            mixed[...],
            (((1,), (1,)), ((), ())),
            preferred_element_type=F32,
        )
        made[rows, :] = (
            upstream[rows, :].astype(F32) + (inner[rows, :] + got)
        ).astype(BF)
        leave(i).start()
        return carry

    lax.fori_loop(0, tiles, tile, 0, unroll=True)
    for i in range(tiles):
        leave(i).wait()


def outer_back(name, z, halo, weight, given, inner, *begun):
    return pl.pallas_call(
        outer_back_kernel,
        out_shape=jax.ShapeDtypeStruct((2, CELLS, C), BF),
        in_specs=[SMEM, VMEM] + [HBM] * (3 + len(begun)),
        out_specs=HBM,
        scratch_shapes=[
            pltpu.VMEM((3, PADDED, C), BF),
            pltpu.VMEM((C, 9 * C), BF),
            pltpu.VMEM((9 * C, C), BF),
            pltpu.VMEM((CELLS, C), BF),
            pltpu.VMEM((CELLS, C), F32),
            pltpu.VMEM((CELLS, C), BF),
            pltpu.SemaphoreType.DMA((3,)),
            pltpu.SemaphoreType.DMA((CELLS // TILE,)),
        ],
        input_output_aliases={5: 0} if begun else {},
        compiler_params=LARGE,
        cost_estimate=cost(CELLS * 2304 * 256, 3 << 20),
        name=name,
    )(z, halo, weight, given, inner, *begun)


def planes_kernel(core_ref, vol, near, far):
    core = core_ref[0]
    far[...] = vol[core]
    near[...] = vol[1 - core]


def both_planes(core, vol):
    plane = jax.ShapeDtypeStruct((CELLS, C), BF)
    return pl.pallas_call(
        planes_kernel,
        out_shape=[plane, plane],
        in_specs=[SMEM, VMEM],
        out_specs=[VMEM, VMEM],
        compiler_params=SMALL,
        cost_estimate=cost(0, 2 << 20),
        name="both_planes",
    )(core, vol)


def first_rows_kernel(whole, out, wide, sems):
    rows = out.shape[0]
    step = rows // 4
    copies = []
    for k in range(4):
        part = slice(k * step, (k + 1) * step)
        wide[part, :] = whole[part, :].astype(F32)
        copy = pltpu.make_async_copy(wide.at[part, :], out.at[part, :], sems.at[k])
        copy.start()
        copies.append(copy)
    for copy in copies:
        copy.wait()


def first_rows(whole, rows):
    return pl.pallas_call(
        first_rows_kernel,
        out_shape=jax.ShapeDtypeStruct((rows, C), F32),
        in_specs=[VMEM],
        out_specs=ANY,
        scratch_shapes=[pltpu.VMEM((rows, C), F32), pltpu.SemaphoreType.DMA((4,))],
        compiler_params=SMALL,
        cost_estimate=cost(0, 1 << 20),
        name="first_rows",
    )(whole)


def mix_kernel(got, out):
    for group in range(4):
        total = got[0, group].astype(F32)
        for k in range(1, 16):
            total += got[k, group].astype(F32)
        out[group] = total.astype(BF)
        out[4 + group] = total.astype(BF)


def mixed_rows(got):
    return pl.pallas_call(
        mix_kernel,
        out_shape=jax.ShapeDtypeStruct((8, CHUNK, C), BF),
        in_specs=[VMEM],
        out_specs=VMEM,
        compiler_params=SMALL,
        cost_estimate=cost(1 << 18, 1 << 20),
        name="mixed_rows",
    )(got)


def step_kernel(at_ref, got, first, second, out):
    total = got[0].astype(F32)
    for k in range(1, 8):
        total += got[k].astype(F32)
    at = pl.multiple_of(at_ref[0], CHUNK)
    rows = pl.ds(at, CHUNK)
    step = adam(total, first[rows, :], second[rows, :])
    step = step.astype(BF)
    for k in range(OWNERS):
        out[k] = step


def spread_step(at, got, first, second):
    return pl.pallas_call(
        step_kernel,
        out_shape=jax.ShapeDtypeStruct((OWNERS, CHUNK, C), BF),
        in_specs=[SMEM] + [VMEM] * 3,
        out_specs=VMEM,
        compiler_params=SMALL,
        cost_estimate=cost(1 << 18, 1 << 20),
        name="spread_step",
    )(at, got, first, second)


def adam(grad, first, second):
    m_new = beta_one * first + (1.0 - beta_one) * grad
    v_new = beta_two * second + (1.0 - beta_two) * grad * grad
    return (
        m_new
        / (1.0 - beta_one**ADAM_STEP)
        / (jnp.sqrt(v_new / (1.0 - beta_two**ADAM_STEP)) + eps_adam)
    )


def from_neighbours(near, far):
    size = lax.axis_size(SPACE)
    pairs = [(i, i + 1) for i in range(1, size - 1, 2)]
    far_halo = lax.ppermute(far, SPACE, pairs + [(j, i) for i, j in pairs])
    near_halo = lax.ppermute(near, "core", [(0, 1), (1, 0)])
    return near_halo, far_halo


def body(volume, upstream, weight, first_moment, second_moment):
    vol = volume.reshape(2, CELLS, C)
    up = upstream.reshape(2, CELLS, C)
    core = lax.axis_index("core")
    at_core = core.reshape(1)
    near, far = both_planes(at_core, vol)
    near_halo, far_halo = from_neighbours(near, far)
    inner, vol_t = inner_conv(at_core, near, far, weight)
    near, part = near_side(at_core, near_halo, weight, inner, up, vol_t)
    far, part, sent = far_side(at_core, part, far_halo, weight, inner, up, vol_t)

    rows = first_moment.shape[0]
    other = lax.ppermute(sent, "core", [(0, 1), (1, 0)])
    half = both_halves(part, other).reshape(16, 4, CHUNK, C)
    got = lax.all_to_all(half, ("x", "y"), 0, 0)
    grad_near, grad_far = from_neighbours(near, far)
    local = inner_back(at_core, near, far, weight, half)
    got, local = lax.optimization_barrier((got, local))
    part = mixed_rows(got)
    grad_near, part = lax.optimization_barrier((grad_near, part))
    got = lax.all_to_all(part, ("zl", "sample"), 0, 0)
    half_done = outer_back("near_back", 1 - at_core, grad_near, weight, up, local)
    got, half_done = lax.optimization_barrier((got, half_done))
    owner = core * 16 + lax.axis_index("x") * 4 + lax.axis_index("y")
    at = jnp.minimum(owner * CHUNK, rows - CHUNK).reshape(1)
    step = spread_step(at, got, first_moment, second_moment)
    whole = lax.all_to_all(step, ("core", "x", "y"), 0, 0)
    grad_volume = outer_back(
        "far_back", at_core, grad_far, weight, up, local, half_done
    )
    direction = first_rows(whole.reshape(OWNERS * CHUNK, C), rows)
    return (grad_volume.reshape(volume.shape), direction)


def solution(mesh):
    fine = Mesh(
        mesh.devices.reshape(4, 4, 2, 2, 4), ("x", "y", "zl", "core", "sample")
    )
    field = P("sample", SPACE, None, None, None)
    return jax.shard_map(
        body,
        mesh=fine,
        in_specs=(field, field, P(), P("sample", None), P("sample", None)),
        out_specs=(field, P("sample", None)),
        check_vma=False,
    )
```
